32 devices in a mesh: rows: 8 (over z, y), edges: 4 (over x, core).
Axes of the slice: x: 2, y: 2, z: 4, core: 2. Of those that a mesh axis runs over, the one named last changes fastest.
Arguments:
- features: bfloat16 [40960, 256], P(('rows', 'edges')), may hold values from -6 to 6
- edge_src: int32 [40960], P(('rows', 'edges')), may hold values from 0 to 1023, as said below
- edge_dst: int32 [40960], P(('rows', 'edges')), may hold values from 0 to 1023, as said below
- edge_cell: int32 [40960], P(('rows', 'edges')), may hold values from 0 to 2
- cell_bias: bfloat16 [3, 512], replicated, may hold values from -4 to 4
- w_in: bfloat16 [256, 512], replicated, may hold values from -0.375 to 0.375
- w_out: bfloat16 [256, 256], replicated, may hold values from -0.0068359375 to 0.0068359375
- vectors: float32 [128, 16384], P('edges', 'rows'), may hold values from -6 to 6
- cheb_coef: float32 [5], replicated, may hold values from 0.5 to 1.5
Outputs:
- filtered: float32 [128, 16384], P('edges', 'rows')
The draws below stay inside these ranges and needn't reach their ends.
Inputs may be any that keep to these rules, and one draw needn't show every extreme that they name: `edge_src`: number the devices d = 0 .. 1024 / 32 - 1 along rows and edges together (rows first) and let quarter q be atoms q * 32 to (q + 1) * 32 - 1. Device d holds 1280 edges in order of source atom (cyclically): first the edges of quarter d - 1 it holds, then edges of quarter d, then edges of quarter d + 1 (cyclically over devices). Between 160 and 320 belong to quarter d - 1 and between 160 and 320 to quarter d + 1; for each kind, some device has exactly 320. `edge_dst`: each source, target pair occurs once. The target's tile (atom // 8) lies within 3 tiles of the source's tile, cyclically over 1024 / 8 tiles.
All inputs are finite; a program needn't handle non-finite values.
Results may differ from the reference program's by a relative error of at most 0.0065.
Values may be sent and summed in bfloat16 or wider, within the bound.
No kernel may reach another device: no remote copies, remote signals or barrier semaphores. Data moves between devices by JAX's collectives and lax.ppermute only.
A program may use at most 64 MiB of HBM per device.

```python
import jax
import jax.numpy as jnp
from jax import lax

ORB = 16
TILE_ATOMS = 8
BAND = 3
NEIGH = 40
FEAT = 256
HID = 256
VEC = 128
STEPS = 4
ATOM_Q = 32
E_DEV = 1280
SPILL = 320
NATOM = 1024
EDGES = 40960
NROWS = 16384


def edge_lists(key):
    nquart = NATOM // ATOM_Q
    ntiles = NATOM // TILE_ATOMS
    ncand = (2 * BAND + 1) * TILE_ATOMS
    keys = jax.random.split(jax.random.fold_in(key, 11), 7)
    half = SPILL // 2
    low = half + jax.random.randint(keys[0], (nquart,), 0, half + 1)
    high = half + jax.random.randint(keys[1], (nquart,), 0, half + 1)
    low = low.at[jax.random.randint(keys[2], (), 0, nquart)].set(SPILL)
    high = high.at[jax.random.randint(keys[3], (), 0, nquart)].set(SPILL)
    own = E_DEV - low - high
    qsize = own + jnp.roll(high, 1) + jnp.roll(low, -1)
    base = qsize // ATOM_Q
    extra = qsize % ATOM_Q
    place = jnp.arange(ATOM_Q, dtype=jnp.int32)
    degree = base[:, None] + (place[None, :] < extra[:, None]).astype(jnp.int32)
    signs = jax.random.randint(keys[4], (nquart, ATOM_Q // 2), 0, 2) * 2 - 1
    amount = jax.random.randint(keys[5], (nquart, ATOM_Q // 2), 0, 3)
    change = jnp.stack([signs * amount, -signs * amount], axis=-1).reshape(nquart, ATOM_Q)
    degree = (degree + change).reshape(NATOM)
    scores = jax.random.randint(keys[6], (NATOM, ncand), 0, 1048576) * ncand + jnp.arange(ncand, dtype=jnp.int32)[None, :]
    order = jnp.argsort(scores, axis=1).astype(jnp.int32)
    qstart = jnp.cumsum(qsize) - qsize
    atom_start = jnp.cumsum(degree) - degree
    slot = jnp.arange(E_DEV, dtype=jnp.int32)[None, :]
    device = jnp.arange(nquart, dtype=jnp.int32)[:, None]
    before = (device - 1) % nquart
    after = (device + 1) % nquart
    low_d = low[:, None]
    own_d = own[:, None]
    from_before = qstart[before] + qsize[before] - low_d + slot
    from_mine = qstart[device] + high[before] + (slot - low_d)
    from_after = qstart[after] + (slot - low_d - own_d)
    position = jnp.where(slot < low_d, from_before, jnp.where(slot < low_d + own_d, from_mine, from_after)).reshape(-1)
    atom = (jnp.searchsorted(atom_start, position, side='right') - 1).astype(jnp.int32)
    rank = position - atom_start[atom]
    cand = order[atom, rank]
    tile = atom // TILE_ATOMS
    target = (tile - BAND + cand // TILE_ATOMS) % ntiles * TILE_ATOMS + cand % TILE_ATOMS
    return (atom.astype(jnp.int32), target.astype(jnp.int32))


def draw_edge_src(key, part):
    return edge_lists(key)[0]


def draw_edge_dst(key, part):
    return edge_lists(key)[1]


def set_ends(values, rng, low, high):
    longest = values.shape.index(max(values.shape))
    spots = []
    for shift in (0, 1):
        where = [jax.random.randint(jax.random.fold_in(rng, axis), (), 0, length) for axis, length in enumerate(values.shape)]
        where[longest] = (where[longest] + shift) % values.shape[longest]
        spots.append(tuple(where))
    return values.at[spots[0]].set(low).at[spots[1]].set(high)


def level_of(stream_key, extent, shards, smallest, high):
    gain = 1.0
    for dim, parts in shards:
        heights = jax.random.uniform(jax.random.fold_in(jax.random.fold_in(stream_key, 6), dim), (parts,), jnp.float32, smallest / len(shards), high / len(shards))
        gain = gain * jnp.repeat(jnp.exp(heights), extent[dim] // parts).reshape((-1,) + (1,) * (len(extent) - 1 - dim))
    return gain


def noise(stream_key, dims, spread, bound, cuts=(), held_as=jnp.bfloat16):
    loudness = level_of(stream_key, dims, cuts, -0.22, 0.18) if cuts else 1.0
    values = jax.random.normal(stream_key, dims, jnp.float32) * spread * loudness
    return jnp.minimum(jnp.maximum(values, -bound), bound).astype(held_as)


def setup_inputs(seed: int = 0) -> dict:
    seeds = jax.random.split(jax.random.key(seed), 10)
    return {
        "features": noise(seeds[0], (EDGES, FEAT), 1.0, 6.0, ((0, 32),)),
        "edge_src": draw_edge_src(jax.random.fold_in(seeds[9], 71), 0),
        "edge_dst": draw_edge_dst(jax.random.fold_in(seeds[9], 71), 0),
        "edge_cell": set_ends(jax.random.randint(seeds[3], (EDGES,), 0, 3), jax.random.fold_in(seeds[3], 1), 0, 2).astype(jnp.int32),
        "cell_bias": noise(seeds[4], (3, 2 * HID), 1.0, 4.0),
        "w_in": noise(seeds[5], (FEAT, 2 * HID), FEAT ** -0.5, 0.375),
        "w_out": noise(seeds[6], (HID, ORB * ORB), (HID * ORB * NEIGH * 5) ** -0.5, 0.0068359375),
        "vectors": noise(seeds[7], (VEC, NROWS), 1.0, 6.0, ((0, 4), (1, 8)), jnp.float32),
        "cheb_coef": jnp.clip(jax.random.uniform(seeds[8], (STEPS + 1,), jnp.float32, 0.5, 1.5), 0.5, 1.5),
    }


def pair_blocks(feat, cell, cell_bias, w_in, w_out):
    pre = jnp.dot(feat, w_in, preferred_element_type=jnp.float32) + cell_bias[cell].astype(jnp.float32)
    hidden = (jax.nn.silu(pre[:, :HID]) * pre[:, HID:]).astype(jnp.bfloat16)
    return jnp.dot(hidden, w_out, preferred_element_type=jnp.float32).astype(jnp.bfloat16)


def reference(features, edge_src, edge_dst, edge_cell, cell_bias, w_in, w_out, vectors, cheb_coef):
    groups = EDGES // E_DEV

    def one_group(pieces):
        return pair_blocks(pieces[0], pieces[1], cell_bias, w_in, w_out)

    blocks = lax.map(one_group, (features.reshape(groups, E_DEV, FEAT), edge_cell.reshape(groups, E_DEV)))
    blocks = blocks.reshape(EDGES, ORB, ORB)
    ntiles = NATOM // TILE_ATOMS
    nband = 2 * BAND + 1
    tile_size = TILE_ATOMS * ORB
    src_tile = edge_src // TILE_ATOMS
    shift_tile = (edge_dst // TILE_ATOMS - src_tile + BAND) % ntiles
    flat = ((src_tile * nband + shift_tile) * TILE_ATOMS + edge_src % TILE_ATOMS) * TILE_ATOMS + edge_dst % TILE_ATOMS
    band = jnp.zeros((ntiles * nband * TILE_ATOMS * TILE_ATOMS, ORB, ORB), jnp.bfloat16).at[flat.astype(jnp.int32)].add(blocks)
    band = band.reshape(ntiles, nband, TILE_ATOMS, TILE_ATOMS, ORB, ORB).transpose(0, 1, 2, 4, 3, 5)
    band = band.reshape(ntiles, nband, tile_size, tile_size)

    def apply(field):
        field3 = field.reshape(VEC, ntiles, tile_size)
        total = jnp.zeros((VEC, ntiles, tile_size), jnp.float32)
        for diag in range(nband):
            moved = jnp.roll(field3, -(diag - BAND), axis=1)
            total = total + jnp.einsum("vtc,trc->vtr", moved, band[:, diag].astype(jnp.float32), precision=lax.Precision.HIGHEST)
        return total.reshape(VEC, NROWS)

    previous = vectors
    current = apply(previous)
    result = cheb_coef[0] * previous + cheb_coef[1] * current
    for step in range(2, STEPS + 1):
        following = 2.0 * apply(current) - previous
        result = result + cheb_coef[step] * following
        previous, current = current, following
    return result
```

```python
import functools

import jax
import jax.numpy as jnp
from jax import lax
from jax.experimental import pallas as pl
from jax.experimental.pallas import tpu as pltpu
from jax.sharding import PartitionSpec as P

ORB = 16
TILE_ATOMS = 8
BAND = 3
HID = 256
VEC = 128
STEPS = 4
ATOM_Q = 32
SPILL = 320
ID_ROWS = 16
PAIR_ATOMS = 2 * TILE_ATOMS
WIN_ATOMS = (2 * BAND + 2) * TILE_ATOMS
HALO = BAND * TILE_ATOMS * ORB
BF = jnp.bfloat16
F32 = jnp.float32
NT = (((1,), (1,)), ((), ()))


def nt_dot(a, b):
    return lax.dot_general(a, b, NT, preferred_element_type=F32)


def iota(shape, dim):
    return lax.broadcasted_iota(jnp.int32, shape, dim)


def band_kernel(feat, ids, blue, red, cell_bias, w_in, w_out, band, blk, bias8):
    nfeat, width = w_in.shape
    nblk = w_out.shape[1]
    eye = (iota((width, width), 0) == iota((width, width), 1)).astype(BF)
    w_in_t = nt_dot(eye, w_in[...]).astype(BF)
    bias8[...] = jnp.zeros(bias8.shape, F32)
    bias8[0:3, :] = cell_bias[...].astype(F32)
    bias_t = nt_dot(eye, bias8[...].astype(BF)).astype(BF)
    row, col = iota((nblk, nblk), 0), iota((nblk, nblk), 1)
    swap = (col == (row % ORB) * ORB + row // ORB).astype(BF)
    w_out_t = nt_dot(swap, w_out[...]).astype(BF)

    def rows_of(msg, k):
        return msg[SPILL : SPILL + ID_ROWS, :].astype(F32)[2 * k : 2 * k + 2, :]

    parts = []
    own = feat.shape[0]
    for lo in range(0, own, 256):
        parts.append((feat[lo : lo + 256, :], [ids[k : k + 1, lo : lo + 256] for k in range(3)]))
    for msg in (blue, red):
        parts.append((msg[0:256, :], [rows_of(msg, k)[0:1] for k in range(3)]))
    tail = [(rows_of(blue, k)[1:2] + rows_of(red, k)[1:2])[:, :128] for k in range(3)]
    parts.append((jnp.concatenate([blue[256:SPILL, :], red[256:SPILL, :]], axis=0), tail))
    at = 0
    atoms, cols = [], []
    for x, (a, b, c) in parts:
        n = x.shape[0]
        cell1 = (iota((8, n), 0).astype(F32) == c).astype(BF)
        pre = nt_dot(w_in_t, x) + jnp.dot(bias_t, cell1, preferred_element_type=F32)
        gate, up = pre[:HID], pre[HID:]
        hidden = (gate * (0.5 + 0.5 * jnp.tanh(0.5 * gate)) * up).astype(BF)
        blk[:, at : at + n] = jnp.dot(w_out_t, hidden, preferred_element_type=F32).astype(BF)
        atoms.append(a)
        cols.append(b)
        at += n
    atom = jnp.concatenate(atoms, axis=1)
    odd_tile = jnp.floor(atom * (1.0 / TILE_ATOMS)) - 2.0 * jnp.floor(atom * (0.5 / TILE_ATOMS))
    target = jnp.concatenate(cols, axis=1) + TILE_ATOMS * odd_tile
    onehot_t = (iota((WIN_ATOMS, at), 0).astype(F32) == target).astype(BF)
    low = iota((ORB, 128), 1) < WIN_ATOMS
    for first in range(0, ATOM_Q, 4):
        onehot = jnp.concatenate(
            [
                jnp.broadcast_to((atom == float(s)).astype(F32), (WIN_ATOMS, at)).astype(BF) * onehot_t
                for s in range(first, first + 4)
            ],
            axis=0,
        )
        dense = nt_dot(blk[...], onehot)
        for sp in range(2):
            s = first + 2 * sp
            pair, at_row = s // PAIR_ATOMS, s % PAIR_ATOMS * ORB
            for j in range(ORB // 2):
                x = dense[2 * j * ORB : (2 * j + 1) * ORB, sp * 128 : sp * 128 + 128]
                y = dense[(2 * j + 1) * ORB : (2 * j + 2) * ORB, sp * 128 : sp * 128 + 128]
                lanes = slice(j * 128, j * 128 + 128)
                band[pair, at_row : at_row + ORB, lanes] = jnp.where(
                    low, x, pltpu.roll(y, WIN_ATOMS, 1)
                ).astype(BF)
                band[pair, at_row + ORB : at_row + 2 * ORB, lanes] = jnp.where(
                    low, pltpu.roll(x, WIN_ATOMS, 1), y
                ).astype(BF)


def apply_band(band, wide, pair):
    height = PAIR_ATOMS * ORB
    pieces = [
        wide[pl.ds(pair * height + q, WIN_ATOMS, stride=ORB), :] for q in range(ORB)
    ]
    rhs = jnp.concatenate(pieces, axis=0).astype(BF)
    return jnp.dot(band[pair], rhs, preferred_element_type=F32)


def fill_wide(side, own, blue, red, wide):
    rows = own.shape[0]
    end = HALO + rows
    off = pl.multiple_of(side * end, 128)
    wide[pl.ds(off, HALO), :] = blue
    wide[pl.ds(pl.multiple_of(end - off, 128), HALO), :] = red
    wide[HALO:end, :] = own


def put_sends(side, value_ref, to_blue, to_red):
    inner = value_ref.shape[0] - HALO
    off = pl.multiple_of(side * inner, 128)
    to_blue[...] = value_ref[pl.ds(off, HALO), :].astype(BF)
    to_red[...] = value_ref[pl.ds(pl.multiple_of(inner - off, 128), HALO), :].astype(BF)


def first_kernel(side, band, field, blue, red, t0, t1, to_blue, to_red, wide):
    t0[...] = field[...].astype(F32).T
    fill_wide(side[0], t0[...], blue[...].astype(F32).T, red[...].astype(F32).T, wide)
    height = PAIR_ATOMS * ORB
    for pair in range(band.shape[0]):
        t1[pair * height : (pair + 1) * height, :] = apply_band(band, wide, pair)
    put_sends(side[0], t1, to_blue, to_red)


def next_kernel(side, band, before, now, blue, red, after, to_blue, to_red, wide):
    fill_wide(side[0], now[...], blue[...].astype(F32), red[...].astype(F32), wide)
    height = PAIR_ATOMS * ORB
    for pair in range(band.shape[0]):
        span = slice(pair * height, (pair + 1) * height)
        after[span, :] = 2.0 * apply_band(band, wide, pair) - before[span, :]
    put_sends(side[0], after, to_blue, to_red)


def last_kernel(side, coef, band, t0, t1, t2, t3, blue, red, out, wide):
    fill_wide(side[0], t3[...], blue[...].astype(F32), red[...].astype(F32), wide)
    height = PAIR_ATOMS * ORB
    for pair in range(band.shape[0]):
        span = slice(pair * height, (pair + 1) * height)
        t4 = 2.0 * apply_band(band, wide, pair) - t2[span, :]
        total = coef[0] * t0[span, :] + coef[1] * t1[span, :] + coef[2] * t2[span, :]
        total = total + coef[3] * t3[span, :] + coef[4] * t4
        out[:, span] = total.T.astype(BF)


VMEM = pl.BlockSpec(memory_space=pltpu.VMEM)
SMEM = pl.BlockSpec(memory_space=pltpu.SMEM)
PARAMS = pltpu.CompilerParams(vmem_limit_bytes=40 * 1024 * 1024)


def shape(dims, dtype):
    return jax.ShapeDtypeStruct(dims, dtype)


def per_device(features, edge_src, edge_dst, edge_cell, cell_bias, w_in, w_out, vectors, cheb_coef):
    axes = ("rows", "edges")
    ndev = lax.axis_size("rows") * lax.axis_size("edges")
    quarter = lax.axis_index("rows") * lax.axis_size("edges") + lax.axis_index("edges")
    natom = ATOM_Q * ndev
    ntiles = natom // TILE_ATOMS
    side = quarter % 2
    red_pairs = [(i, i ^ 1) for i in range(ndev)]
    blue_pairs = [(i, (i + 1) % ndev if i % 2 else (i - 1) % ndev) for i in range(ndev)]
    nown = features.shape[0]

    rel = edge_src - quarter * ATOM_Q
    rel = jnp.where(rel > natom // 2, rel - natom, jnp.where(rel < -(natom // 2), rel + natom, rel))
    shift_tile = (edge_dst // TILE_ATOMS - edge_src // TILE_ATOMS + BAND + ntiles) % ntiles
    col = shift_tile * TILE_ATOMS + edge_dst % TILE_ATOMS
    ids = jnp.stack([rel, col, edge_cell]).astype(F32)

    def message(first, delta, gap):
        rows = lax.dynamic_slice_in_dim(features, first, SPILL, 0)
        part = lax.dynamic_slice_in_dim(ids, first, SPILL, 1)
        part = part + jnp.array([[1.0], [0.0], [0.0]], F32) * delta
        zeros = jnp.zeros((3, 64), F32)
        tail = [zeros, part[:, 256:]] if gap else [part[:, 256:], zeros]
        block = jnp.concatenate([part[:, :256], *tail, zeros, zeros], axis=1).reshape(6, 256)
        block = jnp.concatenate([block, jnp.zeros((ID_ROWS - 6, 256), F32)], axis=0).astype(BF)
        return jnp.concatenate([rows, block], axis=0)

    low_first, high_first = 0, nown - SPILL
    blue_first = jnp.where(side == 0, low_first, high_first)
    red_first = high_first - blue_first
    sign = (1 - 2 * side).astype(F32) * ATOM_Q
    blue_msg = lax.ppermute(message(blue_first, sign, False), axes, blue_pairs)
    red_msg = lax.ppermute(message(red_first, -sign, True), axes, red_pairs)

    def halo(first, last):
        return (
            lax.ppermute(first, axes, blue_pairs),
            lax.ppermute(last, axes, red_pairs),
        )

    field = lax.all_to_all(vectors.astype(BF), "edges", split_axis=1, concat_axis=0, tiled=True)
    nrow = field.shape[1]
    inner = nrow - HALO
    t0_blue, t0_red = halo(
        lax.dynamic_slice_in_dim(field, side * inner, HALO, 1),
        lax.dynamic_slice_in_dim(field, inner - side * inner, HALO, 1),
    )

    total_len = nown + 2 * SPILL
    band = pl.pallas_call(
        band_kernel,
        name="band",
        out_shape=shape((ATOM_Q // PAIR_ATOMS, PAIR_ATOMS * ORB, WIN_ATOMS * ORB), BF),
        in_specs=[VMEM] * 7,
        out_specs=VMEM,
        scratch_shapes=[
            pltpu.VMEM((ORB * ORB, total_len), BF),
            pltpu.VMEM((8, 2 * HID), F32),
        ],
        compiler_params=PARAMS,
    )(features, ids, blue_msg, red_msg, cell_bias, w_in, w_out)

    side1 = side.reshape(1)
    wide = [pltpu.VMEM((nrow + 2 * HALO, VEC), F32)]
    full, part = shape((nrow, VEC), F32), shape((HALO, VEC), BF)
    t0, t1, to_blue, to_red = pl.pallas_call(
        first_kernel,
        name="first",
        out_shape=(full, full, part, part),
        in_specs=[SMEM] + [VMEM] * 4,
        out_specs=(VMEM,) * 4,
        scratch_shapes=wide,
        compiler_params=PARAMS,
    )(side1, band, field, t0_blue, t0_red)

    fields = [t0, t1]
    for _ in range(2, STEPS):
        blue, red = halo(to_blue, to_red)
        following, to_blue, to_red = pl.pallas_call(
            next_kernel,
            name="next",
            out_shape=(full, part, part),
            in_specs=[SMEM] + [VMEM] * 5,
            out_specs=(VMEM,) * 3,
            scratch_shapes=wide,
            compiler_params=PARAMS,
        )(side1, band, fields[-2], fields[-1], blue, red)
        fields.append(following)
    blue, red = halo(to_blue, to_red)
    result = pl.pallas_call(
        last_kernel,
        name="last",
        out_shape=shape((VEC, nrow), BF),
        in_specs=[SMEM, SMEM] + [VMEM] * 7,
        out_specs=VMEM,
        scratch_shapes=wide,
        compiler_params=PARAMS,
    )(side1, cheb_coef, band, *fields, blue, red)
    result = lax.all_to_all(result, "edges", split_axis=0, concat_axis=1, tiled=True)
    return result.astype(F32)


def solution(mesh):
    placed = (
        P(("rows", "edges"), None),
        P(("rows", "edges")),
        P(("rows", "edges")),
        P(("rows", "edges")),
        P(),
        P(),
        P(),
        P("edges", "rows"),
        P(),
    )
    return jax.shard_map(
        per_device, mesh=mesh, in_specs=placed, out_specs=P("edges", "rows"), check_vma=False
    )
```

```python
import functools

import jax
import jax.numpy as jnp
from jax import lax
from jax.experimental import pallas as pl
from jax.experimental.pallas import tpu as pltpu
from jax.sharding import PartitionSpec as P

ORB = 16
TILE_ATOMS = 8
BAND = 3
HID = 256
VEC = 128
STEPS = 4
ATOM_Q = 32
SPILL = 320
ID_ROWS = 16
PAIR_ATOMS = 2 * TILE_ATOMS
WIN_ATOMS = (2 * BAND + 2) * TILE_ATOMS
HALO = BAND * TILE_ATOMS * ORB
BF = jnp.bfloat16
F32 = jnp.float32
NT = (((1,), (1,)), ((), ()))


def nt_dot(a, b):
    return lax.dot_general(a, b, NT, preferred_element_type=F32)


def iota(shape, dim):
    return lax.broadcasted_iota(jnp.int32, shape, dim)


def device_side():
    return (lax.axis_index("rows") * lax.axis_size("edges") + lax.axis_index("edges")) % 2


def prep_kernel(feat, src, dst, cell, vectors, blue, red, ids, p0, p1, p2, p3, sems):
    ndev = lax.axis_size("rows") * lax.axis_size("edges")
    member = lax.axis_index("edges")
    quarter = lax.axis_index("rows") * lax.axis_size("edges") + member
    side = quarter % 2
    high = feat.shape[0] - SPILL
    off = pl.multiple_of(side * high, 64)
    copies = [
        pltpu.make_async_copy(feat.at[pl.ds(off, SPILL)], blue.at[pl.ds(0, SPILL)], sems.at[0]),
        pltpu.make_async_copy(
            feat.at[pl.ds(pl.multiple_of(high - off, 64), SPILL)], red.at[pl.ds(0, SPILL)], sems.at[1]
        ),
    ]
    for copy in copies:
        copy.start()
    natom = ATOM_Q * ndev
    ntiles = natom // TILE_ATOMS
    rel = src[...] - quarter * ATOM_Q
    rel = jnp.where(rel > natom // 2, rel - natom, jnp.where(rel < -(natom // 2), rel + natom, rel))
    shift = (dst[...] >> 3) - (src[...] >> 3) + BAND
    shift = jnp.where(shift < 0, shift + ntiles, jnp.where(shift >= ntiles, shift - ntiles, shift))
    three = [x.astype(F32) for x in (rel, shift * TILE_ATOMS + (dst[...] & 7), cell[...])]
    for k in range(3):
        ids[k] = three[k]
    lane, line = iota((3, 128), 1), iota((3, 128), 0)
    nrow = src.shape[0]
    starts = [x[0:3] for x in three]
    ends = [x[nrow - 3 : nrow] for x in three]
    starts[0] = jnp.where((line == 2) & (lane >= 64), -64.0, starts[0] + ATOM_Q)
    ends[0] = jnp.where((line == 0) & (lane < 64), -64.0, ends[0] - ATOM_Q)
    pad = jnp.zeros((ID_ROWS - 9, 128), F32)
    low_ids = jnp.concatenate(starts + [pad], axis=0)
    high_ids = jnp.concatenate(ends + [pad], axis=0)
    none = jnp.zeros((ID_ROWS, 128), BF)
    for msg, ids_of in (
        (blue, jnp.where(side == 0, low_ids, high_ids)),
        (red, jnp.where(side == 0, high_ids, low_ids)),
    ):
        msg[SPILL : SPILL + ID_ROWS, 0:128] = ids_of.astype(BF)
        msg[SPILL : SPILL + ID_ROWS, 128:256] = none
    for k, piece in enumerate((p0, p1, p2, p3)):
        width = piece.shape[1]
        at = pl.multiple_of((member ^ k) * width, width)
        piece[...] = vectors[:, pl.ds(at, width)].astype(BF)
    for copy in copies:
        copy.wait()


def field_kernel(p0, p1, p2, p3, t0, to_blue, to_red, field):
    member = lax.axis_index("edges")
    for k, piece in enumerate((p0, p1, p2, p3)):
        high = piece.shape[0]
        field[pl.ds(pl.multiple_of((member ^ k) * high, high), high), :] = piece[...].astype(F32)
    t0[...] = field[...].T
    put_sends(t0, to_blue, to_red)


def band_kernel(feat, ids, blue, red, cell_bias, w_in, w_out, band, blk, bias8, spill):
    nfeat, width = w_in.shape
    nblk = w_out.shape[1]
    eye = (iota((width, width), 0) == iota((width, width), 1)).astype(BF)
    w_in_t = nt_dot(eye, w_in[...]).astype(BF)
    bias8[...] = jnp.zeros(bias8.shape, F32)
    bias8[0:3, :] = cell_bias[...].astype(F32)
    bias_t = nt_dot(eye, bias8[...].astype(BF)).astype(BF)
    row, col = iota((nblk, nblk), 0), iota((nblk, nblk), 1)
    swap = (col == (row % ORB) * ORB + row // ORB).astype(BF)
    w_out_t = nt_dot(swap, w_out[...]).astype(BF)

    side = device_side()
    parts = []
    for lo in range(0, feat.shape[0], 256):
        line = lo // 128
        parts.append(
            (
                lambda lo=lo: feat[lo : lo + 256, :],
                [jnp.concatenate([ids[k, line : line + 1], ids[k, line + 1 : line + 2]], axis=1) for k in range(3)],
            )
        )
    rows = spill.shape[0] // 2
    for m, (msg, gap) in enumerate(((blue, side == 0), (red, side == 1))):
        base = m * rows
        spill[base : base + 64, :] = jnp.zeros((64, nfeat), BF)
        spill[base + rows - 64 : base + rows, :] = jnp.zeros((64, nfeat), BF)
        at = pl.multiple_of(base + jnp.where(gap, 64, 0), 64)
        spill[pl.ds(at, SPILL), :] = msg[0:SPILL, :]
    lines = []
    for msg in (blue, red):
        block = msg[SPILL : SPILL + ID_ROWS, 0:128].astype(F32)
        lines.extend([[block[3 * k + n : 3 * k + n + 1] for k in range(3)] for n in range(3)])
    for lo in range(0, 2 * rows, 256):
        first, second = lines[lo // 128], lines[lo // 128 + 1]
        parts.append(
            (
                lambda lo=lo: spill[lo : lo + 256, :],
                [jnp.concatenate([first[k], second[k]], axis=1) for k in range(3)],
            )
        )
    at = 0
    atoms, cols = [], []
    for get, (a, b, c) in parts:
        x = get()
        n = x.shape[0]
        cell1 = (iota((8, n), 0).astype(F32) == c).astype(BF)
        pre = nt_dot(w_in_t, x) + jnp.dot(bias_t, cell1, preferred_element_type=F32)
        gate, up = pre[:HID], pre[HID:]
        hidden = (gate * (0.5 + 0.5 * jnp.tanh(0.5 * gate)) * up).astype(BF)
        blk[:, at : at + n] = jnp.dot(w_out_t, hidden, preferred_element_type=F32).astype(BF)
        atoms.append(a)
        cols.append(b)
        at += n
    atom = jnp.concatenate(atoms, axis=1)
    odd_tile = jnp.floor(atom * (1.0 / TILE_ATOMS)) - 2.0 * jnp.floor(atom * (0.5 / TILE_ATOMS))
    target = jnp.concatenate(cols, axis=1) + TILE_ATOMS * odd_tile
    onehot_t = (iota((WIN_ATOMS, at), 0).astype(F32) == target).astype(BF)
    low = iota((ORB, 128), 1) < WIN_ATOMS
    for first in range(0, ATOM_Q, 4):
        onehot = jnp.concatenate(
            [
                jnp.broadcast_to((atom == float(s)).astype(F32), (WIN_ATOMS, at)).astype(BF) * onehot_t
                for s in range(first, first + 4)
            ],
            axis=0,
        )
        dense = nt_dot(blk[...], onehot)
        for sp in range(2):
            s = first + 2 * sp
            pair, at_row = s // PAIR_ATOMS, s % PAIR_ATOMS * ORB
            for j in range(ORB // 2):
                x = dense[2 * j * ORB : (2 * j + 1) * ORB, sp * 128 : sp * 128 + 128]
                y = dense[(2 * j + 1) * ORB : (2 * j + 2) * ORB, sp * 128 : sp * 128 + 128]
                lanes = slice(j * 128, j * 128 + 128)
                band[pair, at_row : at_row + ORB, lanes] = jnp.where(
                    low, x, pltpu.roll(y, WIN_ATOMS, 1)
                ).astype(BF)
                band[pair, at_row + ORB : at_row + 2 * ORB, lanes] = jnp.where(
                    low, pltpu.roll(x, WIN_ATOMS, 1), y
                ).astype(BF)


def apply_band(band, wide, pair):
    height = PAIR_ATOMS * ORB
    pieces = [
        wide[pl.ds(pair * height + q, WIN_ATOMS, stride=ORB), :] for q in range(ORB)
    ]
    rhs = jnp.concatenate(pieces, axis=0).astype(BF)
    return jnp.dot(band[pair], rhs, preferred_element_type=F32)


def fill_wide(own, blue, red, wide):
    side = device_side()
    rows = own.shape[0]
    end = HALO + rows
    off = pl.multiple_of(side * end, 128)
    wide[pl.ds(off, HALO), :] = blue
    wide[pl.ds(pl.multiple_of(end - off, 128), HALO), :] = red
    wide[HALO:end, :] = own


def put_sends(value_ref, to_blue, to_red):
    side = device_side()
    inner = value_ref.shape[0] - HALO
    off = pl.multiple_of(side * inner, 128)
    to_blue[...] = value_ref[pl.ds(off, HALO), :].astype(BF)
    to_red[...] = value_ref[pl.ds(pl.multiple_of(inner - off, 128), HALO), :].astype(BF)


def first_kernel(band, t0, blue, red, t1, to_blue, to_red, wide):
    fill_wide(t0[...], blue[...].astype(F32), red[...].astype(F32), wide)
    height = PAIR_ATOMS * ORB
    for pair in range(band.shape[0]):
        t1[pair * height : (pair + 1) * height, :] = apply_band(band, wide, pair)
    put_sends(t1, to_blue, to_red)


def next_kernel(band, before, now, blue, red, after, to_blue, to_red, wide):
    fill_wide(now[...], blue[...].astype(F32), red[...].astype(F32), wide)
    height = PAIR_ATOMS * ORB
    for pair in range(band.shape[0]):
        span = slice(pair * height, (pair + 1) * height)
        after[span, :] = 2.0 * apply_band(band, wide, pair) - before[span, :]
    put_sends(after, to_blue, to_red)


def last_kernel(coef, band, t0, t1, t2, t3, blue, red, p0, p1, p2, p3, wide, out):
    member = lax.axis_index("edges")
    fill_wide(t3[...], blue[...].astype(F32), red[...].astype(F32), wide)
    height = PAIR_ATOMS * ORB
    for pair in range(band.shape[0]):
        span = slice(pair * height, (pair + 1) * height)
        t4 = 2.0 * apply_band(band, wide, pair) - t2[span, :]
        total = coef[0] * t0[span, :] + coef[1] * t1[span, :] + coef[2] * t2[span, :]
        total = total + coef[3] * t3[span, :] + coef[4] * t4
        out[:, span] = total.T
    for k, piece in enumerate((p0, p1, p2, p3)):
        high = piece.shape[0]
        piece[...] = out[pl.ds(pl.multiple_of((member ^ k) * high, high), high), :].astype(BF)


def join_kernel(p0, p1, p2, p3, out):
    member = lax.axis_index("edges")
    for k, piece in enumerate((p0, p1, p2, p3)):
        width = piece.shape[1]
        at = pl.multiple_of((member ^ k) * width, width)
        out[:, pl.ds(at, width)] = piece[...].astype(F32)


VMEM = pl.BlockSpec(memory_space=pltpu.VMEM)
SMEM = pl.BlockSpec(memory_space=pltpu.SMEM)
ANYWHERE = pl.BlockSpec(memory_space=pl.ANY)
PARAMS = pltpu.CompilerParams(vmem_limit_bytes=40 * 1024 * 1024)


def shape(dims, dtype):
    return jax.ShapeDtypeStruct(dims, dtype)


def call(kernel, name, outs, scratch, *args, smem=(), anywhere=()):
    spaces = [SMEM if k in smem else ANYWHERE if k in anywhere else VMEM for k in range(len(args))]
    return pl.pallas_call(
        kernel,
        name=name,
        out_shape=outs,
        in_specs=spaces,
        out_specs=(VMEM,) * len(outs),
        scratch_shapes=scratch,
        compiler_params=PARAMS,
    )(*args)


def per_device(features, edge_src, edge_dst, edge_cell, cell_bias, w_in, w_out, vectors, cheb_coef):
    axes = ("rows", "edges")
    nedge = lax.axis_size("edges")
    ndev = lax.axis_size("rows") * nedge
    red_pairs = [(i, i ^ 1) for i in range(ndev)]
    blue_pairs = [(i, (i + 1) % ndev if i % 2 else (i - 1) % ndev) for i in range(ndev)]
    nown, nfeat = features.shape
    high, ncol = vectors.shape
    nrow = ncol // nedge

    def swap(first, last):
        return (
            lax.ppermute(first, axes, blue_pairs),
            lax.ppermute(last, axes, red_pairs),
        )

    def exchange(pieces):
        return [pieces[0]] + [
            lax.ppermute(pieces[k], "edges", [(i, i ^ k) for i in range(nedge)]) for k in (1, 2, 3)
        ]

    msg = shape((SPILL + ID_ROWS, nfeat), BF)
    piece = shape((high, nrow), BF)
    lines = (nown // 128, 128)
    blue_msg, red_msg, ids, *pieces = call(
        prep_kernel,
        "prep",
        (msg, msg, shape((3,) + lines, F32)) + (piece,) * 4,
        [pltpu.SemaphoreType.DMA((2,))],
        features,
        edge_src.reshape(lines),
        edge_dst.reshape(lines),
        edge_cell.reshape(lines),
        vectors,
        anywhere=(0,),
    )
    blue_msg, red_msg = swap(blue_msg, red_msg)
    pieces = exchange(pieces)
    full, part = shape((nrow, VEC), F32), shape((HALO, VEC), BF)
    t0, to_blue, to_red = call(
        field_kernel, "field", (full, part, part), [pltpu.VMEM((VEC, nrow), F32)], *pieces
    )
    blue, red = swap(to_blue, to_red)

    spill_len = 2 * (SPILL + 64)
    (band,) = call(
        band_kernel,
        "band",
        (shape((ATOM_Q // PAIR_ATOMS, PAIR_ATOMS * ORB, WIN_ATOMS * ORB), BF),),
        [
            pltpu.VMEM((ORB * ORB, nown + spill_len), BF),
            pltpu.VMEM((8, 2 * HID), F32),
            pltpu.VMEM((spill_len, nfeat), BF),
        ],
        features,
        ids,
        blue_msg,
        red_msg,
        cell_bias,
        w_in,
        w_out,
    )

    wide = pltpu.VMEM((nrow + 2 * HALO, VEC), F32)
    t1, to_blue, to_red = call(first_kernel, "first", (full, part, part), [wide], band, t0, blue, red)
    fields = [t0, t1]
    for _ in range(2, STEPS):
        blue, red = swap(to_blue, to_red)
        following, to_blue, to_red = call(
            next_kernel, "next", (full, part, part), [wide], band, fields[-2], fields[-1], blue, red
        )
        fields.append(following)
    blue, red = swap(to_blue, to_red)
    pieces = call(
        last_kernel,
        "last",
        (piece,) * 4,
        [wide, pltpu.VMEM((VEC, nrow), F32)],
        cheb_coef,
        band,
        *fields,
        blue,
        red,
        smem=(0,),
    )
    (result,) = call(join_kernel, "join", (shape((high, ncol), F32),), [], *exchange(pieces))
    return result


def solution(mesh):
    placed = (
        P(("rows", "edges"), None),
        P(("rows", "edges")),
        P(("rows", "edges")),
        P(("rows", "edges")),
        P(),
        P(),
        P(),
        P("edges", "rows"),
        P(),
    )
    return jax.shard_map(
        per_device, mesh=mesh, in_specs=placed, out_specs=P("edges", "rows"), check_vma=False
    )
```

```python
import functools

import jax
import jax.numpy as jnp
from jax import lax
from jax.experimental import pallas as pl
from jax.experimental.pallas import tpu as pltpu
from jax.sharding import PartitionSpec as P

ORB = 16
TILE_ATOMS = 8
BAND = 3
HID = 256
VEC = 128
STEPS = 4
ATOM_Q = 32
SPILL = 320
ID_ROWS = 16
PAIR_ATOMS = 2 * TILE_ATOMS
WIN_ATOMS = (2 * BAND + 2) * TILE_ATOMS
HALO = BAND * TILE_ATOMS * ORB
GROUP = 4
GROUP_SPAN = 384
BF = jnp.bfloat16
F32 = jnp.float32
NT = (((1,), (1,)), ((), ()))


def nt_dot(a, b):
    return lax.dot_general(a, b, NT, preferred_element_type=F32)


def iota(shape, dim):
    return lax.broadcasted_iota(jnp.int32, shape, dim)


def device_side():
    return (lax.axis_index("rows") * lax.axis_size("edges") + lax.axis_index("edges")) % 2


def split_kernel(vec_hbm, p0, p1, p2, p3, vectors, sem):
    member = lax.axis_index("edges")
    load = pltpu.make_async_copy(vec_hbm, vectors, sem)
    load.start()
    load.wait()
    for k, piece in enumerate((p0, p1, p2, p3)):
        width = piece.shape[1]
        at = pl.multiple_of((member ^ k) * width, width)
        piece[...] = vectors[:, pl.ds(at, width)].astype(BF)


def message_kernel(feat, src_hbm, dst_hbm, cell_hbm, _, blue, red, ids, src, dst, cell, sems):
    ndev = lax.axis_size("rows") * lax.axis_size("edges")
    quarter = lax.axis_index("rows") * lax.axis_size("edges") + lax.axis_index("edges")
    side = quarter % 2
    high = feat.shape[0] - SPILL
    off = pl.multiple_of(side * high, 64)
    copies = [
        pltpu.make_async_copy(feat.at[pl.ds(off, SPILL)], blue.at[pl.ds(0, SPILL)], sems.at[0]),
        pltpu.make_async_copy(
            feat.at[pl.ds(pl.multiple_of(high - off, 64), SPILL)], red.at[pl.ds(0, SPILL)], sems.at[1]
        ),
    ]
    loads = [
        pltpu.make_async_copy(x, y, sems.at[2 + n])
        for n, (x, y) in enumerate(((src_hbm, src), (dst_hbm, dst), (cell_hbm, cell)))
    ]
    for copy in loads + copies:
        copy.start()
    for copy in loads:
        copy.wait()
    natom = ATOM_Q * ndev
    ntiles = natom // TILE_ATOMS
    rel = src[...] - quarter * ATOM_Q
    rel = jnp.where(rel > natom // 2, rel - natom, jnp.where(rel < -(natom // 2), rel + natom, rel))
    shift = (dst[...] >> 3) - (src[...] >> 3) + BAND
    shift = jnp.where(shift < 0, shift + ntiles, jnp.where(shift >= ntiles, shift - ntiles, shift))
    three = [x.astype(F32) for x in (rel, shift * TILE_ATOMS + (dst[...] & 7), cell[...])]
    for k in range(3):
        ids[k] = three[k]
    lane, line = iota((3, 128), 1), iota((3, 128), 0)
    nrow = src.shape[0]
    starts = [x[0:3] for x in three]
    ends = [x[nrow - 3 : nrow] for x in three]
    starts[0] = jnp.where((line == 2) & (lane >= 64), -64.0, starts[0] + ATOM_Q)
    ends[0] = jnp.where((line == 0) & (lane < 64), -64.0, ends[0] - ATOM_Q)
    pad = jnp.zeros((ID_ROWS - 9, 128), F32)
    low_ids = jnp.concatenate(starts + [pad], axis=0)
    high_ids = jnp.concatenate(ends + [pad], axis=0)
    none = jnp.zeros((ID_ROWS, 128), BF)
    for msg, ids_of in (
        (blue, jnp.where(side == 0, low_ids, high_ids)),
        (red, jnp.where(side == 0, high_ids, low_ids)),
    ):
        msg[SPILL : SPILL + ID_ROWS, 0:128] = ids_of.astype(BF)
        msg[SPILL : SPILL + ID_ROWS, 128:256] = none
    for copy in copies:
        copy.wait()


def field_kernel(p0, p1, p2, p3, t0, to_blue, to_red, field):
    member = lax.axis_index("edges")
    for k, piece in enumerate((p0, p1, p2, p3)):
        high = piece.shape[0]
        field[pl.ds(pl.multiple_of((member ^ k) * high, high), high), :] = piece[...].astype(F32)
    t0[...] = field[...].T
    put_sends(t0, to_blue, to_red)


def pair_blocks(x, cell, w_in_t, bias_t, w_out_t):
    cell1 = (iota((8, x.shape[0]), 0).astype(F32) == cell).astype(BF)
    pre = nt_dot(w_in_t, x) + jnp.dot(bias_t, cell1, preferred_element_type=F32)
    gate, up = pre[:HID], pre[HID:]
    hidden = (gate * (0.5 + 0.5 * jnp.tanh(0.5 * gate)) * up).astype(BF)
    return jnp.dot(w_out_t, hidden, preferred_element_type=F32).astype(BF)


def dense_of(blocks, atom, target, first):
    span = atom.shape[1]
    column = (iota((WIN_ATOMS, span), 0).astype(F32) == target).astype(BF)
    onehot = [
        jnp.broadcast_to((atom == float(s)).astype(F32), (WIN_ATOMS, span)).astype(BF) * column
        for s in range(first, first + GROUP)
    ]
    return nt_dot(blocks, jnp.concatenate(onehot, axis=0))


def put_dense(band, dense, first, add):
    low = iota((ORB, 128), 1) < WIN_ATOMS
    for sp in range(GROUP // 2):
        s = first + 2 * sp
        pair, at_row = s // PAIR_ATOMS, s % PAIR_ATOMS * ORB
        for j in range(ORB // 2):
            x = dense[2 * j * ORB : (2 * j + 1) * ORB, sp * 128 : sp * 128 + 128]
            y = dense[(2 * j + 1) * ORB : (2 * j + 2) * ORB, sp * 128 : sp * 128 + 128]
            lanes = slice(j * 128, j * 128 + 128)
            both = (
                jnp.where(low, x, pltpu.roll(y, WIN_ATOMS, 1)),
                jnp.where(low, pltpu.roll(x, WIN_ATOMS, 1), y),
            )
            for n, value in enumerate(both):
                rows = slice(at_row + n * ORB, at_row + (n + 1) * ORB)
                if add:
                    value = value + band[pair, rows, lanes].astype(F32)
                band[pair, rows, lanes] = value.astype(BF)


def odd_tile(atom):
    return jnp.floor(atom * (1.0 / TILE_ATOMS)) - 2.0 * jnp.floor(atom * (0.5 / TILE_ATOMS))


def own_kernel(feat, ids, cell_bias, w_in, w_out, band, w_in_t, bias_t, w_out_t, blk, bias8, rows):
    nfeat, width = w_in.shape
    nblk = w_out.shape[1]
    eye = (iota((width, width), 0) == iota((width, width), 1)).astype(BF)
    w_in_t[...] = nt_dot(eye, w_in[...]).astype(BF)
    bias8[...] = jnp.zeros(bias8.shape, F32)
    bias8[0:3, :] = cell_bias[...].astype(F32)
    bias_t[...] = nt_dot(eye, bias8[...].astype(BF)).astype(BF)
    row, col = iota((nblk, nblk), 0), iota((nblk, nblk), 1)
    swap = (col == (row % ORB) * ORB + row // ORB).astype(BF)
    w_out_t[...] = nt_dot(swap, w_out[...]).astype(BF)
    own = feat.shape[0]
    for lo in range(0, own, 256):
        span = slice(lo, lo + 256)
        line = lo // 128
        a, b, c = [
            jnp.concatenate([ids[k, line : line + 1], ids[k, line + 1 : line + 2]], axis=1) for k in range(3)
        ]
        blk[:, span] = pair_blocks(feat[span, :], c, w_in_t[...], bias_t[...], w_out_t[...])
        rows[0:1, span] = a
        rows[1:2, span] = b + TILE_ATOMS * odd_tile(a)
    for first in range(0, ATOM_Q, GROUP):
        start = jnp.sum((ids[0] < float(first)).astype(F32)).astype(jnp.int32)
        at = pl.multiple_of(jnp.minimum(start // 128 * 128, own - GROUP_SPAN), 128)
        span = pl.ds(at, GROUP_SPAN)
        put_dense(band, dense_of(blk[:, span], rows[0:1, span], rows[1:2, span], first), first, False)


def spill_kernel(own_band, blue, red, w_in_t, bias_t, w_out_t, band, blk, spill):
    side = device_side()
    nfeat = spill.shape[1]
    rows = spill.shape[0] // 2
    for m, (msg, gap) in enumerate(((blue, side == 0), (red, side == 1))):
        base = m * rows
        spill[base : base + 64, :] = jnp.zeros((64, nfeat), BF)
        spill[base + rows - 64 : base + rows, :] = jnp.zeros((64, nfeat), BF)
        at = pl.multiple_of(base + jnp.where(gap, 64, 0), 64)
        spill[pl.ds(at, SPILL), :] = msg[0:SPILL, :]
    lines, ends = [], []
    for msg in (blue, red):
        block = msg[SPILL : SPILL + ID_ROWS, 0:128].astype(F32)
        lines.extend([[block[3 * k + n : 3 * k + n + 1] for k in range(3)] for n in range(3)])
        a = block[0:3]
        mine = (a >= 0.0) & (a < float(ATOM_Q))
        ends.append(
            (
                jnp.min(jnp.where(mine, a, float(ATOM_Q))).astype(jnp.int32),
                jnp.max(jnp.where(mine, a, -1.0)).astype(jnp.int32),
            )
        )
    for lo in range(0, 2 * rows, 256):
        both = lines[lo // 128 : lo // 128 + 2]
        cell = jnp.concatenate([x[2] for x in both], axis=1)
        blk[:, lo : lo + 256] = pair_blocks(
            spill[lo : lo + 256, :], cell, w_in_t[...], bias_t[...], w_out_t[...]
        )
    band[...] = own_band[...]
    for m in range(2):
        mine = lines[3 * m : 3 * m + 3]
        atom = jnp.concatenate([x[0] for x in mine], axis=1)
        target = jnp.concatenate([x[1] for x in mine], axis=1) + TILE_ATOMS * odd_tile(atom)
        lowest, highest = ends[m]
        for first in range(0, ATOM_Q, GROUP):

            @pl.when((lowest < first + GROUP) & (highest >= first))
            def _(m=m, first=first, atom=atom, target=target):
                dense = dense_of(blk[:, m * rows : (m + 1) * rows], atom, target, first)
                put_dense(band, dense, first, True)


def apply_band(band, wide, pair):
    height = PAIR_ATOMS * ORB
    pieces = [
        wide[pl.ds(pair * height + q, WIN_ATOMS, stride=ORB), :] for q in range(ORB)
    ]
    rhs = jnp.concatenate(pieces, axis=0).astype(BF)
    return jnp.dot(band[pair], rhs, preferred_element_type=F32)


def fill_wide(own, blue, red, wide):
    side = device_side()
    rows = own.shape[0]
    end = HALO + rows
    off = pl.multiple_of(side * end, 128)
    wide[pl.ds(off, HALO), :] = blue
    wide[pl.ds(pl.multiple_of(end - off, 128), HALO), :] = red
    wide[HALO:end, :] = own


def put_sends(value_ref, to_blue, to_red):
    side = device_side()
    inner = value_ref.shape[0] - HALO
    off = pl.multiple_of(side * inner, 128)
    to_blue[...] = value_ref[pl.ds(off, HALO), :].astype(BF)
    to_red[...] = value_ref[pl.ds(pl.multiple_of(inner - off, 128), HALO), :].astype(BF)


def first_kernel(band, t0, blue, red, t1, to_blue, to_red, wide):
    fill_wide(t0[...], blue[...].astype(F32), red[...].astype(F32), wide)
    height = PAIR_ATOMS * ORB
    for pair in range(band.shape[0]):
        t1[pair * height : (pair + 1) * height, :] = apply_band(band, wide, pair)
    put_sends(t1, to_blue, to_red)


def next_kernel(band, before, now, blue, red, after, to_blue, to_red, wide):
    fill_wide(now[...], blue[...].astype(F32), red[...].astype(F32), wide)
    height = PAIR_ATOMS * ORB
    for pair in range(band.shape[0]):
        span = slice(pair * height, (pair + 1) * height)
        after[span, :] = 2.0 * apply_band(band, wide, pair) - before[span, :]
    put_sends(after, to_blue, to_red)


def mix_kernel(coef, t0, t1, t2, t3, base):
    total = coef[0] * t0[...] + coef[1] * t1[...] + (coef[2] - coef[4]) * t2[...] + coef[3] * t3[...]
    base[...] = total.T


def last_kernel(coef, band, base, t3, blue, red, p0, p1, p2, p3, wide, out):
    member = lax.axis_index("edges")
    fill_wide(t3[...], blue[...].astype(F32), red[...].astype(F32), wide)
    height = PAIR_ATOMS * ORB
    for pair in range(band.shape[0]):
        span = slice(pair * height, (pair + 1) * height)
        out[:, span] = base[:, span] + (2.0 * coef[4] * apply_band(band, wide, pair)).T
    for k, piece in enumerate((p0, p1, p2, p3)):
        high = piece.shape[0]
        piece[...] = out[pl.ds(pl.multiple_of((member ^ k) * high, high), high), :].astype(BF)


def join_kernel(p0, p1, p2, p3, out):
    member = lax.axis_index("edges")
    for k, piece in enumerate((p0, p1, p2, p3)):
        width = piece.shape[1]
        at = pl.multiple_of((member ^ k) * width, width)
        out[:, pl.ds(at, width)] = piece[...].astype(F32)


VMEM = pl.BlockSpec(memory_space=pltpu.VMEM)
SMEM = pl.BlockSpec(memory_space=pltpu.SMEM)
IN_HBM = pl.BlockSpec(memory_space=pltpu.HBM)
FULL, PART = 60 * 1024 * 1024, 32 * 1024 * 1024


def shape(dims, dtype):
    return jax.ShapeDtypeStruct(dims, dtype)


def call(kernel, name, outs, scratch, *args, smem=(), in_hbm=(), alias=None, limit=PART):
    spaces = [SMEM if k in smem else IN_HBM if k in in_hbm else VMEM for k in range(len(args))]
    return pl.pallas_call(
        kernel,
        name=name,
        out_shape=outs,
        in_specs=spaces,
        out_specs=(VMEM,) * len(outs),
        scratch_shapes=scratch,
        input_output_aliases=alias or {},
        compiler_params=pltpu.CompilerParams(vmem_limit_bytes=limit),
    )(*args)


def per_device(features, edge_src, edge_dst, edge_cell, cell_bias, w_in, w_out, vectors, cheb_coef):
    axes = ("rows", "edges")
    nedge = lax.axis_size("edges")
    ndev = lax.axis_size("rows") * nedge
    red_pairs = [(i, i ^ 1) for i in range(ndev)]
    blue_pairs = [(i, (i + 1) % ndev if i % 2 else (i - 1) % ndev) for i in range(ndev)]
    nown, nfeat = features.shape
    high, ncol = vectors.shape
    nrow = ncol // nedge

    def swap(first, last):
        return (
            lax.ppermute(first, axes, blue_pairs),
            lax.ppermute(last, axes, red_pairs),
        )

    def exchange(pieces):
        return [pieces[0]] + [
            lax.ppermute(pieces[k], "edges", [(i, i ^ k) for i in range(nedge)]) for k in (1, 2, 3)
        ]

    msg = shape((SPILL + ID_ROWS, nfeat), BF)
    piece = shape((high, nrow), BF)
    lines = (nown // 128, 128)
    pieces = call(
        split_kernel,
        "split",
        (piece,) * 4,
        [pltpu.VMEM((high, ncol), F32), pltpu.SemaphoreType.DMA],
        vectors,
        in_hbm=(0,),
        limit=FULL,
    )
    pieces = exchange(pieces)
    blue_msg, red_msg, ids = call(
        message_kernel,
        "message",
        (msg, msg, shape((3,) + lines, F32)),
        [pltpu.VMEM(lines, jnp.int32)] * 3 + [pltpu.SemaphoreType.DMA((5,))],
        features,
        edge_src.reshape(lines),
        edge_dst.reshape(lines),
        edge_cell.reshape(lines),
        pieces[0],
        in_hbm=range(5),
        limit=FULL,
    )
    blue_msg, red_msg = swap(blue_msg, red_msg)
    full, part = shape((nrow, VEC), F32), shape((HALO, VEC), BF)
    t0, to_blue, to_red = call(
        field_kernel, "field", (full, part, part), [pltpu.VMEM((VEC, nrow), F32)], *pieces
    )
    blue, red = swap(to_blue, to_red)

    band_shape = shape((ATOM_Q // PAIR_ATOMS, PAIR_ATOMS * ORB, WIN_ATOMS * ORB), BF)
    width = w_in.shape[1]
    band, *weights = call(
        own_kernel,
        "own",
        (band_shape, shape((width, nfeat), BF), shape((width, 8), BF), shape((ORB * ORB, HID), BF)),
        [pltpu.VMEM((ORB * ORB, nown), BF), pltpu.VMEM((8, width), F32), pltpu.VMEM((8, nown), F32)],
        features,
        ids,
        cell_bias,
        w_in,
        w_out,
    )
    spill_len = 2 * (SPILL + 64)
    (band,) = call(
        spill_kernel,
        "spill",
        (band_shape,),
        [pltpu.VMEM((ORB * ORB, spill_len), BF), pltpu.VMEM((spill_len, nfeat), BF)],
        band,
        blue_msg,
        red_msg,
        *weights,
        alias={0: 0},
    )

    wide = pltpu.VMEM((nrow + 2 * HALO, VEC), F32)
    t1, to_blue, to_red = call(first_kernel, "first", (full, part, part), [wide], band, t0, blue, red)
    fields = [t0, t1]
    for _ in range(2, STEPS):
        blue, red = swap(to_blue, to_red)
        following, to_blue, to_red = call(
            next_kernel, "next", (full, part, part), [wide], band, fields[-2], fields[-1], blue, red
        )
        fields.append(following)
    blue, red = swap(to_blue, to_red)
    (base,) = call(mix_kernel, "mix", (shape((VEC, nrow), F32),), [], cheb_coef, *fields, smem=(0,))
    pieces = call(
        last_kernel,
        "last",
        (piece,) * 4,
        [wide, pltpu.VMEM((VEC, nrow), F32)],
        cheb_coef,
        band,
        base,
        fields[-1],
        blue,
        red,
        smem=(0,),
    )
    (result,) = call(join_kernel, "join", (shape((high, ncol), F32),), [], *exchange(pieces))
    return result


def solution(mesh):
    placed = (
        P(("rows", "edges"), None),
        P(("rows", "edges")),
        P(("rows", "edges")),
        P(("rows", "edges")),
        P(),
        P(),
        P(),
        P("edges", "rows"),
        P(),
    )
    return jax.shard_map(
        per_device, mesh=mesh, in_specs=placed, out_specs=P("edges", "rows"), check_vma=False
    )
```

```python
import functools

import jax
import jax.numpy as jnp
from jax import lax
from jax.experimental import pallas as pl
from jax.experimental.pallas import tpu as pltpu
from jax.sharding import PartitionSpec as P

ORB = 16
TILE_ATOMS = 8
BAND = 3
HID = 256
VEC = 128
STEPS = 4
ATOM_Q = 32
SPILL = 320
ID_ROWS = 16
PAIR_ATOMS = 2 * TILE_ATOMS
WIN_ATOMS = (2 * BAND + 2) * TILE_ATOMS
HALO = BAND * TILE_ATOMS * ORB
GROUP = 4
GROUP_SPAN = 384
BF = jnp.bfloat16
F32 = jnp.float32
NT = (((1,), (1,)), ((), ()))


def nt_dot(a, b):
    return lax.dot_general(a, b, NT, preferred_element_type=F32)


def iota(shape, dim):
    return lax.broadcasted_iota(jnp.int32, shape, dim)


def device_side():
    return (lax.axis_index("rows") * lax.axis_size("edges") + lax.axis_index("edges")) % 2


def split_kernel(vec_hbm, p0, p1, p2, p3, vectors, sems):
    member = lax.axis_index("edges")
    pieces = (p0, p1, p2, p3)
    loads = []
    for k, piece in enumerate(pieces):
        width = piece.shape[1]
        at = pl.multiple_of((member ^ k) * width, width)
        loads.append(pltpu.make_async_copy(vec_hbm.at[:, pl.ds(at, width)], vectors.at[k], sems.at[k]))
    for k in (2, 3, 1, 0):
        loads[k].start()
    for k in (2, 3, 1, 0):
        loads[k].wait()
        pieces[k][...] = vectors[k].astype(BF)


def message_kernel(feat, src_hbm, dst_hbm, cell_hbm, _, blue, red, ids, src, dst, cell, lines, sems):
    ndev = lax.axis_size("rows") * lax.axis_size("edges")
    quarter = lax.axis_index("rows") * lax.axis_size("edges") + lax.axis_index("edges")
    side = quarter % 2
    high = feat.shape[0] - SPILL
    off = pl.multiple_of(side * high, 64)
    copies = [
        pltpu.make_async_copy(feat.at[pl.ds(off, SPILL)], blue.at[pl.ds(0, SPILL)], sems.at[0]),
        pltpu.make_async_copy(
            feat.at[pl.ds(pl.multiple_of(high - off, 64), SPILL)], red.at[pl.ds(0, SPILL)], sems.at[1]
        ),
    ]
    loads = [
        pltpu.make_async_copy(x, y, sems.at[2 + n])
        for n, (x, y) in enumerate(((src_hbm, src), (dst_hbm, dst), (cell_hbm, cell)))
    ]
    for copy in loads + copies:
        copy.start()
    for copy in loads:
        copy.wait()
    natom = ATOM_Q * ndev
    ntiles = natom // TILE_ATOMS
    rel = src[...] - quarter * ATOM_Q
    rel = jnp.where(rel > natom // 2, rel - natom, jnp.where(rel < -(natom // 2), rel + natom, rel))
    shift = (dst[...] >> 3) - (src[...] >> 3) + BAND
    shift = jnp.where(shift < 0, shift + ntiles, jnp.where(shift >= ntiles, shift - ntiles, shift))
    three = [x.astype(F32) for x in (rel, shift * TILE_ATOMS + (dst[...] & 7), cell[...])]
    for k in range(3):
        ids[k] = three[k]
    lane, line = iota((3, 128), 1), iota((3, 128), 0)
    nrow = src.shape[0]
    starts = [x[0:3] for x in three]
    ends = [x[nrow - 3 : nrow] for x in three]
    starts[0] = jnp.where((line == 2) & (lane >= 64), -64.0, starts[0] + ATOM_Q)
    ends[0] = jnp.where((line == 0) & (lane < 64), -64.0, ends[0] - ATOM_Q)
    pad = jnp.zeros((ID_ROWS - 9, 128), F32)
    low_ids = jnp.concatenate(starts + [pad], axis=0)
    high_ids = jnp.concatenate(ends + [pad], axis=0)
    none = jnp.zeros((ID_ROWS, 128), BF)
    for m, (msg, ids_of) in enumerate(
        (
            (blue, jnp.where(side == 0, low_ids, high_ids)),
            (red, jnp.where(side == 0, high_ids, low_ids)),
        )
    ):
        lines[m, :, 0:128] = ids_of.astype(BF)
        lines[m, :, 128:256] = none
        copy = pltpu.make_async_copy(lines.at[m], msg.at[pl.ds(SPILL, ID_ROWS)], sems.at[5 + m])
        copy.start()
        copies.append(copy)
    for copy in copies:
        copy.wait()


def field_kernel(p0, p1, p2, p3, _, t0, to_blue, to_red, field):
    member = lax.axis_index("edges")
    for k, piece in enumerate((p0, p1, p2, p3)):
        high = piece.shape[0]
        field[pl.ds(pl.multiple_of((member ^ k) * high, high), high), :] = piece[...].astype(F32)
    t0[...] = field[...].T
    put_sends(t0, to_blue, to_red)


def pair_blocks(x, cell, w_in_t, bias_t, w_out_t):
    cell1 = (iota((8, x.shape[0]), 0).astype(F32) == cell).astype(BF)
    pre = nt_dot(w_in_t, x) + jnp.dot(bias_t, cell1, preferred_element_type=F32)
    gate, up = pre[:HID], pre[HID:]
    hidden = (gate * (0.5 + 0.5 * jnp.tanh(0.5 * gate)) * up).astype(BF)
    return jnp.dot(w_out_t, hidden, preferred_element_type=F32).astype(BF)


def dense_of(blocks, atom, target, first):
    span = atom.shape[1]
    column = (iota((WIN_ATOMS, span), 0).astype(F32) == target).astype(BF)
    onehot = [
        jnp.broadcast_to((atom == float(s)).astype(F32), (WIN_ATOMS, span)).astype(BF) * column
        for s in range(first, first + GROUP)
    ]
    return nt_dot(blocks, jnp.concatenate(onehot, axis=0))


def put_dense(band, dense, first, add):
    low = iota((ORB, 128), 1) < WIN_ATOMS
    for sp in range(GROUP // 2):
        s = first + 2 * sp
        pair, at_row = s // PAIR_ATOMS, s % PAIR_ATOMS * ORB
        for j in range(ORB // 2):
            x = dense[2 * j * ORB : (2 * j + 1) * ORB, sp * 128 : sp * 128 + 128]
            y = dense[(2 * j + 1) * ORB : (2 * j + 2) * ORB, sp * 128 : sp * 128 + 128]
            lanes = slice(j * 128, j * 128 + 128)
            both = (
                jnp.where(low, x, pltpu.roll(y, WIN_ATOMS, 1)),
                jnp.where(low, pltpu.roll(x, WIN_ATOMS, 1), y),
            )
            for n, value in enumerate(both):
                rows = slice(at_row + n * ORB, at_row + (n + 1) * ORB)
                if add:
                    value = value + band[pair, rows, lanes].astype(F32)
                band[pair, rows, lanes] = value.astype(BF)


def odd_tile(atom):
    return jnp.floor(atom * (1.0 / TILE_ATOMS)) - 2.0 * jnp.floor(atom * (0.5 / TILE_ATOMS))


def own_kernel(feat, ids, cell_bias, w_in, w_out, band, w_in_t, bias_t, w_out_t, blk, bias8, rows):
    nfeat, width = w_in.shape
    nblk = w_out.shape[1]
    eye = (iota((width, width), 0) == iota((width, width), 1)).astype(BF)
    w_in_t[...] = nt_dot(eye, w_in[...]).astype(BF)
    bias8[...] = jnp.zeros(bias8.shape, F32)
    bias8[0:3, :] = cell_bias[...].astype(F32)
    bias_t[...] = nt_dot(eye, bias8[...].astype(BF)).astype(BF)
    row, col = iota((nblk, nblk), 0), iota((nblk, nblk), 1)
    swap = (col == (row % ORB) * ORB + row // ORB).astype(BF)
    w_out_t[...] = nt_dot(swap, w_out[...]).astype(BF)
    own = feat.shape[0]
    for lo in range(0, own, 256):
        span = slice(lo, lo + 256)
        line = lo // 128
        a, b, c = [
            jnp.concatenate([ids[k, line : line + 1], ids[k, line + 1 : line + 2]], axis=1) for k in range(3)
        ]
        blk[:, span] = pair_blocks(feat[span, :], c, w_in_t[...], bias_t[...], w_out_t[...])
        rows[0:1, span] = a
        rows[1:2, span] = b + TILE_ATOMS * odd_tile(a)
    for first in range(0, ATOM_Q, GROUP):
        start = jnp.sum((ids[0] < float(first)).astype(F32)).astype(jnp.int32)
        at = pl.multiple_of(jnp.minimum(start // 128 * 128, own - GROUP_SPAN), 128)
        span = pl.ds(at, GROUP_SPAN)
        put_dense(band, dense_of(blk[:, span], rows[0:1, span], rows[1:2, span], first), first, False)


def spill_kernel(own_band, blue, red, w_in_t, bias_t, w_out_t, band, blk, spill):
    side = device_side()
    nfeat = spill.shape[1]
    rows = spill.shape[0] // 2
    for m, (msg, gap) in enumerate(((blue, side == 0), (red, side == 1))):
        base = m * rows
        spill[base : base + 64, :] = jnp.zeros((64, nfeat), BF)
        spill[base + rows - 64 : base + rows, :] = jnp.zeros((64, nfeat), BF)
        at = pl.multiple_of(base + jnp.where(gap, 64, 0), 64)
        spill[pl.ds(at, SPILL), :] = msg[0:SPILL, :]
    lines, ends = [], []
    for msg in (blue, red):
        block = msg[SPILL : SPILL + ID_ROWS, 0:128].astype(F32)
        lines.extend([[block[3 * k + n : 3 * k + n + 1] for k in range(3)] for n in range(3)])
        a = block[0:3]
        mine = (a >= 0.0) & (a < float(ATOM_Q))
        ends.append(
            (
                jnp.min(jnp.where(mine, a, float(ATOM_Q))).astype(jnp.int32),
                jnp.max(jnp.where(mine, a, -1.0)).astype(jnp.int32),
            )
        )
    for lo in range(0, 2 * rows, 256):
        both = lines[lo // 128 : lo // 128 + 2]
        cell = jnp.concatenate([x[2] for x in both], axis=1)
        blk[:, lo : lo + 256] = pair_blocks(
            spill[lo : lo + 256, :], cell, w_in_t[...], bias_t[...], w_out_t[...]
        )
    band[...] = own_band[...]
    for m in range(2):
        mine = lines[3 * m : 3 * m + 3]
        atom = jnp.concatenate([x[0] for x in mine], axis=1)
        target = jnp.concatenate([x[1] for x in mine], axis=1) + TILE_ATOMS * odd_tile(atom)
        lowest, highest = ends[m]
        for first in range(0, ATOM_Q, GROUP):

            @pl.when((lowest < first + GROUP) & (highest >= first))
            def _(m=m, first=first, atom=atom, target=target):
                dense = dense_of(blk[:, m * rows : (m + 1) * rows], atom, target, first)
                put_dense(band, dense, first, True)


def apply_band(band, wide, pair):
    height = PAIR_ATOMS * ORB
    pieces = [
        wide[pl.ds(pair * height + q, WIN_ATOMS, stride=ORB), :] for q in range(ORB)
    ]
    rhs = jnp.concatenate(pieces, axis=0).astype(BF)
    return jnp.dot(band[pair], rhs, preferred_element_type=F32)


def fill_wide(own, blue, red, wide):
    side = device_side()
    rows = own.shape[0]
    end = HALO + rows
    off = pl.multiple_of(side * end, 128)
    wide[pl.ds(off, HALO), :] = blue
    wide[pl.ds(pl.multiple_of(end - off, 128), HALO), :] = red
    wide[HALO:end, :] = own


def put_sends(value_ref, to_blue, to_red):
    side = device_side()
    inner = value_ref.shape[0] - HALO
    off = pl.multiple_of(side * inner, 128)
    to_blue[...] = value_ref[pl.ds(off, HALO), :].astype(BF)
    to_red[...] = value_ref[pl.ds(pl.multiple_of(inner - off, 128), HALO), :].astype(BF)


def first_kernel(band, t0, blue, red, t1, to_blue, to_red, wide):
    fill_wide(t0[...], blue[...].astype(F32), red[...].astype(F32), wide)
    height = PAIR_ATOMS * ORB
    for pair in range(band.shape[0]):
        t1[pair * height : (pair + 1) * height, :] = apply_band(band, wide, pair)
    put_sends(t1, to_blue, to_red)


def next_kernel(band, before, now, blue, red, after, to_blue, to_red, wide):
    fill_wide(now[...], blue[...].astype(F32), red[...].astype(F32), wide)
    height = PAIR_ATOMS * ORB
    for pair in range(band.shape[0]):
        span = slice(pair * height, (pair + 1) * height)
        after[span, :] = 2.0 * apply_band(band, wide, pair) - before[span, :]
    put_sends(after, to_blue, to_red)


def mix_kernel(coef, t0, t1, t2, t3, base, final):
    total = coef[0] * t0[...] + coef[1] * t1[...] + (coef[2] - coef[4]) * t2[...] + coef[3] * t3[...]
    base[...] = total.T
    final[...] = jnp.full(final.shape, 2.0 * coef[4], F32)


def last_kernel(final, band, base, t3, blue, red, p0, p1, p2, p3, wide, out):
    member = lax.axis_index("edges")
    fill_wide(t3[...], blue[...].astype(F32), red[...].astype(F32), wide)
    height = PAIR_ATOMS * ORB
    for pair in range(band.shape[0]):
        span = slice(pair * height, (pair + 1) * height)
        out[:, span] = base[:, span] + (final[0:1, :] * apply_band(band, wide, pair)).T
    for k, piece in enumerate((p0, p1, p2, p3)):
        high = piece.shape[0]
        piece[...] = out[pl.ds(pl.multiple_of((member ^ k) * high, high), high), :].astype(BF)


def join_kernel(p0, p1, p2, p3, out):
    member = lax.axis_index("edges")
    for k, piece in enumerate((p0, p1, p2, p3)):
        width = piece.shape[1]
        at = pl.multiple_of((member ^ k) * width, width)
        out[:, pl.ds(at, width)] = piece[...].astype(F32)


VMEM = pl.BlockSpec(memory_space=pltpu.VMEM)
SMEM = pl.BlockSpec(memory_space=pltpu.SMEM)
IN_HBM = pl.BlockSpec(memory_space=pltpu.HBM)
FULL, PART = 60 * 1024 * 1024, 32 * 1024 * 1024


def shape(dims, dtype):
    return jax.ShapeDtypeStruct(dims, dtype)


def call(kernel, name, outs, scratch, *args, smem=(), in_hbm=(), out_hbm=(), alias=None, limit=PART, micros=1):
    spaces = [SMEM if k in smem else IN_HBM if k in in_hbm else VMEM for k in range(len(args))]
    return pl.pallas_call(
        kernel,
        name=name,
        out_shape=outs,
        in_specs=spaces,
        out_specs=tuple(IN_HBM if k in out_hbm else VMEM for k in range(len(outs))),
        scratch_shapes=scratch,
        input_output_aliases=alias or {},
        cost_estimate=pl.CostEstimate(flops=micros * 10**9, bytes_accessed=0, transcendentals=0),
        compiler_params=pltpu.CompilerParams(vmem_limit_bytes=limit),
    )(*args)


def per_device(features, edge_src, edge_dst, edge_cell, cell_bias, w_in, w_out, vectors, cheb_coef):
    axes = ("rows", "edges")
    nedge = lax.axis_size("edges")
    ndev = lax.axis_size("rows") * nedge
    red_pairs = [(i, i ^ 1) for i in range(ndev)]
    blue_pairs = [(i, (i + 1) % ndev if i % 2 else (i - 1) % ndev) for i in range(ndev)]
    nown, nfeat = features.shape
    high, ncol = vectors.shape
    nrow = ncol // nedge

    def swap(first, last):
        return (
            lax.ppermute(first, axes, blue_pairs),
            lax.ppermute(last, axes, red_pairs),
        )

    def exchange(pieces):
        return [pieces[0]] + [
            lax.ppermute(pieces[k], "edges", [(i, i ^ k) for i in range(nedge)]) for k in (1, 2, 3)
        ]

    msg = shape((SPILL + ID_ROWS, nfeat), BF)
    piece = shape((high, nrow), BF)
    lines = (nown // 128, 128)
    pieces = call(
        split_kernel,
        "split",
        (piece,) * 4,
        [pltpu.VMEM((nedge, high, nrow), F32), pltpu.SemaphoreType.DMA((4,))],
        vectors,
        in_hbm=(0,),
        limit=FULL,
    )
    pieces = exchange(pieces)
    blue_msg, red_msg, ids = call(
        message_kernel,
        "message",
        (msg, msg, shape((3,) + lines, F32)),
        [pltpu.VMEM(lines, jnp.int32)] * 3
        + [pltpu.VMEM((2, ID_ROWS, nfeat), BF), pltpu.SemaphoreType.DMA((7,))],
        features,
        edge_src.reshape(lines),
        edge_dst.reshape(lines),
        edge_cell.reshape(lines),
        pieces[0],
        in_hbm=range(5),
        out_hbm=(0, 1),
        limit=FULL,
        micros=3,
    )
    blue_msg, red_msg = swap(blue_msg, red_msg)
    full, part = shape((nrow, VEC), F32), shape((HALO, VEC), BF)
    band_shape = shape((ATOM_Q // PAIR_ATOMS, PAIR_ATOMS * ORB, WIN_ATOMS * ORB), BF)
    width = w_in.shape[1]
    band, *weights = call(
        own_kernel,
        "own",
        (band_shape, shape((width, nfeat), BF), shape((width, 8), BF), shape((ORB * ORB, HID), BF)),
        [pltpu.VMEM((ORB * ORB, nown), BF), pltpu.VMEM((8, width), F32), pltpu.VMEM((8, nown), F32)],
        features,
        ids,
        cell_bias,
        w_in,
        w_out,
        micros=4,
    )
    t0, to_blue, to_red = call(
        field_kernel, "field", (full, part, part), [pltpu.VMEM((VEC, nrow), F32)], *pieces, weights[1], in_hbm=(4,)
    )
    blue, red = swap(to_blue, to_red)

    spill_len = 2 * (SPILL + 64)
    (band,) = call(
        spill_kernel,
        "spill",
        (band_shape,),
        [pltpu.VMEM((ORB * ORB, spill_len), BF), pltpu.VMEM((spill_len, nfeat), BF)],
        band,
        blue_msg,
        red_msg,
        *weights,
        alias={0: 0},
    )

    wide = pltpu.VMEM((nrow + 2 * HALO, VEC), F32)
    t1, to_blue, to_red = call(first_kernel, "first", (full, part, part), [wide], band, t0, blue, red)
    fields = [t0, t1]
    for _ in range(2, STEPS):
        blue, red = swap(to_blue, to_red)
        following, to_blue, to_red = call(
            next_kernel, "next", (full, part, part), [wide], band, fields[-2], fields[-1], blue, red
        )
        fields.append(following)
    blue, red = swap(to_blue, to_red)
    base, final = call(
        mix_kernel, "mix", (shape((VEC, nrow), F32), shape((8, VEC), F32)), [], cheb_coef, *fields, smem=(0,)
    )
    pieces = call(
        last_kernel,
        "last",
        (piece,) * 4,
        [wide, pltpu.VMEM((VEC, nrow), F32)],
        final,
        band,
        base,
        fields[-1],
        blue,
        red,
    )
    (result,) = call(join_kernel, "join", (shape((high, ncol), F32),), [], *exchange(pieces))
    return result


def solution(mesh):
    placed = (
        P(("rows", "edges"), None),
        P(("rows", "edges")),
        P(("rows", "edges")),
        P(("rows", "edges")),
        P(),
        P(),
        P(),
        P("edges", "rows"),
        P(),
    )
    return jax.shard_map(
        per_device, mesh=mesh, in_specs=placed, out_specs=P("edges", "rows"), check_vma=False
    )
```

```python
import functools

import jax
import jax.numpy as jnp
from jax import lax
from jax.experimental import pallas as pl
from jax.experimental.pallas import tpu as pltpu
from jax.sharding import PartitionSpec as P

ORB = 16
TILE_ATOMS = 8
BAND = 3
HID = 256
VEC = 128
STEPS = 4
ATOM_Q = 32
SPILL = 320
ID_ROWS = 16
PAIR_ATOMS = 2 * TILE_ATOMS
WIN_ATOMS = (2 * BAND + 2) * TILE_ATOMS
HALO = BAND * TILE_ATOMS * ORB
GROUP = 4
GROUP_SPAN = 384
BF = jnp.bfloat16
F32 = jnp.float32
NT = (((1,), (1,)), ((), ()))


def nt_dot(a, b):
    return lax.dot_general(a, b, NT, preferred_element_type=F32)


def iota(shape, dim):
    return lax.broadcasted_iota(jnp.int32, shape, dim)


def device_side():
    return (lax.axis_index("rows") * lax.axis_size("edges") + lax.axis_index("edges")) % 2


def edge_ids(src, dst, cell):
    ndev = lax.axis_size("rows") * lax.axis_size("edges")
    quarter = lax.axis_index("rows") * lax.axis_size("edges") + lax.axis_index("edges")
    natom = ATOM_Q * ndev
    ntiles = natom // TILE_ATOMS
    rel = src - quarter * ATOM_Q
    rel = jnp.where(rel > natom // 2, rel - natom, jnp.where(rel < -(natom // 2), rel + natom, rel))
    shift = (dst >> 3) - (src >> 3) + BAND
    shift = jnp.where(shift < 0, shift + ntiles, jnp.where(shift >= ntiles, shift - ntiles, shift))
    return [x.astype(F32) for x in (rel, shift * TILE_ATOMS + (dst & 7), cell)]


def split_kernel(vec_hbm, p0, p1, p2, p3, vectors, sems):
    member = lax.axis_index("edges")
    pieces = (p0, p1, p2, p3)
    loads = []
    for k, piece in enumerate(pieces):
        width = piece.shape[1]
        at = pl.multiple_of((member ^ k) * width, width)
        loads.append(pltpu.make_async_copy(vec_hbm.at[:, pl.ds(at, width)], vectors.at[k], sems.at[k]))
    for k in (2, 3, 1, 0):
        loads[k].start()
    for k in (2, 3, 1, 0):
        loads[k].wait()
        pieces[k][...] = vectors[k].astype(BF)


def message_kernel(feat, src_hbm, dst_hbm, cell_hbm, _, blue, red, src, dst, cell, sems):
    side = device_side()
    high = feat.shape[0] - SPILL
    off = pl.multiple_of(side * high, 64)
    copies = [
        pltpu.make_async_copy(feat.at[pl.ds(off, SPILL)], blue.at[pl.ds(0, SPILL)], sems.at[0]),
        pltpu.make_async_copy(
            feat.at[pl.ds(pl.multiple_of(high - off, 64), SPILL)], red.at[pl.ds(0, SPILL)], sems.at[1]
        ),
    ]
    loads = [
        pltpu.make_async_copy(x, y, sems.at[2 + n])
        for n, (x, y) in enumerate(((src_hbm, src), (dst_hbm, dst), (cell_hbm, cell)))
    ]
    for copy in loads + copies:
        copy.start()
    for copy in loads:
        copy.wait()
    three = edge_ids(src[...], dst[...], cell[...])
    lane, line = iota((3, 128), 1), iota((3, 128), 0)
    nrow = src.shape[0]
    starts = [x[0:3] for x in three]
    ends = [x[nrow - 3 : nrow] for x in three]
    starts[0] = jnp.where((line == 2) & (lane >= 64), -64.0, starts[0] + ATOM_Q)
    ends[0] = jnp.where((line == 0) & (lane < 64), -64.0, ends[0] - ATOM_Q)
    pad = jnp.zeros((ID_ROWS - 9, 128), F32)
    low_ids = jnp.concatenate(starts + [pad], axis=0)
    high_ids = jnp.concatenate(ends + [pad], axis=0)
    none = jnp.zeros((ID_ROWS, 128), BF)
    for msg, ids_of in (
        (blue, jnp.where(side == 0, low_ids, high_ids)),
        (red, jnp.where(side == 0, high_ids, low_ids)),
    ):
        msg[SPILL : SPILL + ID_ROWS, 0:128] = ids_of.astype(BF)
        msg[SPILL : SPILL + ID_ROWS, 128:256] = none
    for copy in copies:
        copy.wait()


def field_kernel(p0, p1, p2, p3, t0, to_blue, to_red, field):
    member = lax.axis_index("edges")
    for k, piece in enumerate((p0, p1, p2, p3)):
        high = piece.shape[0]
        field[pl.ds(pl.multiple_of((member ^ k) * high, high), high), :] = piece[...].astype(F32)
    t0[...] = field[...].T
    put_sends(t0, to_blue, to_red)


def pair_blocks(x, cell, w_in_t, bias_t, w_out_t):
    bias = [bias_t[:, k : k + 1].astype(F32) for k in range(3)]
    pre = nt_dot(w_in_t[...], x)
    pre = pre + jnp.where(cell == 1.0, bias[1], jnp.where(cell == 2.0, bias[2], bias[0]))
    gate, up = pre[:HID], pre[HID:]
    hidden = (gate * (0.5 + 0.5 * jnp.tanh(0.5 * gate)) * up).astype(BF)
    return jnp.dot(w_out_t[...], hidden, preferred_element_type=F32).astype(BF)


def row_of(x):
    return jnp.concatenate([x[k : k + 1] for k in range(x.shape[0])], axis=1)


def dense_of(blocks, atom, target, first):
    span = atom.shape[1]
    column = (iota((WIN_ATOMS, span), 0).astype(F32) == target).astype(BF)
    onehot = [
        jnp.broadcast_to((atom == float(s)).astype(F32), (WIN_ATOMS, span)).astype(BF) * column
        for s in range(first, first + GROUP)
    ]
    return nt_dot(blocks, jnp.concatenate(onehot, axis=0))


def put_dense(band, dense, first, add):
    low = iota((ORB, 128), 1) < WIN_ATOMS
    for sp in range(GROUP // 2):
        s = first + 2 * sp
        pair, at_row = s // PAIR_ATOMS, s % PAIR_ATOMS * ORB
        for j in range(ORB // 2):
            x = dense[2 * j * ORB : (2 * j + 1) * ORB, sp * 128 : sp * 128 + 128]
            y = dense[(2 * j + 1) * ORB : (2 * j + 2) * ORB, sp * 128 : sp * 128 + 128]
            lanes = slice(j * 128, j * 128 + 128)
            both = (
                jnp.where(low, x, pltpu.roll(y, WIN_ATOMS, 1)),
                jnp.where(low, pltpu.roll(x, WIN_ATOMS, 1), y),
            )
            for n, value in enumerate(both):
                rows = slice(at_row + n * ORB, at_row + (n + 1) * ORB)
                if add:
                    value = value + band[pair, rows, lanes].astype(F32)
                band[pair, rows, lanes] = value.astype(BF)


def odd_tile(atom):
    return jnp.floor(atom * (1.0 / TILE_ATOMS)) - 2.0 * jnp.floor(atom * (0.5 / TILE_ATOMS))


def own_kernel(feat, src, dst, cell, cell_bias, w_in, w_out, band, w_in_t, bias_t, w_out_t, blk, bias8, rows):
    nfeat, width = w_in.shape
    nblk = w_out.shape[1]
    eye = (iota((width, width), 0) == iota((width, width), 1)).astype(BF)
    w_in_t[...] = nt_dot(eye, w_in[...]).astype(BF)
    bias8[...] = jnp.zeros(bias8.shape, F32)
    bias8[0:3, :] = cell_bias[...].astype(F32)
    bias_t[...] = nt_dot(eye, bias8[...].astype(BF)).astype(BF)
    row, col = iota((nblk, nblk), 0), iota((nblk, nblk), 1)
    swap = (col == (row % ORB) * ORB + row // ORB).astype(BF)
    w_out_t[...] = nt_dot(swap, w_out[...]).astype(BF)
    own = feat.shape[0]
    ids = edge_ids(src[...], dst[...], cell[...])
    atom = row_of(ids[0])
    rows[0:1, :] = atom
    rows[1:2, :] = row_of(ids[1]) + TILE_ATOMS * odd_tile(atom)
    blk[...] = pair_blocks(feat[...], row_of(ids[2]), w_in_t, bias_t, w_out_t)
    for first in range(0, ATOM_Q, GROUP):
        start = jnp.sum((ids[0] < float(first)).astype(F32)).astype(jnp.int32)
        at = pl.multiple_of(jnp.minimum(start // 128 * 128, own - GROUP_SPAN), 128)
        span = pl.ds(at, GROUP_SPAN)
        put_dense(band, dense_of(blk[:, span], rows[0:1, span], rows[1:2, span], first), first, False)


def spill_kernel(own_band, blue, red, w_in_t, bias_t, w_out_t, band, blk, spill):
    side = device_side()
    nfeat = spill.shape[1]
    rows = spill.shape[0] // 2
    for m, (msg, gap) in enumerate(((blue, side == 0), (red, side == 1))):
        base = m * rows
        spill[base : base + 64, :] = jnp.zeros((64, nfeat), BF)
        spill[base + rows - 64 : base + rows, :] = jnp.zeros((64, nfeat), BF)
        at = pl.multiple_of(base + jnp.where(gap, 64, 0), 64)
        spill[pl.ds(at, SPILL), :] = msg[0:SPILL, :]
    ids, ends = [], []
    for msg in (blue, red):
        block = msg[SPILL : SPILL + ID_ROWS, 0:128].astype(F32)
        a = block[0:3]
        mine = (a >= 0.0) & (a < float(ATOM_Q))
        ids.append([row_of(block[3 * k : 3 * k + 3]) for k in range(3)])
        ends.append(
            (
                jnp.min(jnp.where(mine, a, float(ATOM_Q))).astype(jnp.int32),
                jnp.max(jnp.where(mine, a, -1.0)).astype(jnp.int32),
            )
        )
    cells = jnp.concatenate([x[2] for x in ids], axis=1)
    blk[...] = pair_blocks(spill[...], cells, w_in_t, bias_t, w_out_t)
    band[...] = own_band[...]
    for m in range(2):
        atom, target = ids[m][0], ids[m][1] + TILE_ATOMS * odd_tile(ids[m][0])
        lowest, highest = ends[m]
        for first in range(0, ATOM_Q, GROUP):

            @pl.when((lowest < first + GROUP) & (highest >= first))
            def _(m=m, first=first, atom=atom, target=target):
                dense = dense_of(blk[:, m * rows : (m + 1) * rows], atom, target, first)
                put_dense(band, dense, first, True)


def apply_band(band, wide, pair):
    height = PAIR_ATOMS * ORB
    pieces = [
        wide[pl.ds(pair * height + q, WIN_ATOMS, stride=ORB), :] for q in range(ORB)
    ]
    rhs = jnp.concatenate(pieces, axis=0).astype(BF)
    return jnp.dot(band[pair], rhs, preferred_element_type=F32)


def fill_wide(own, blue, red, wide):
    side = device_side()
    rows = own.shape[0]
    end = HALO + rows
    off = pl.multiple_of(side * end, 128)
    wide[pl.ds(off, HALO), :] = blue
    wide[pl.ds(pl.multiple_of(end - off, 128), HALO), :] = red
    wide[HALO:end, :] = own


def put_sends(value_ref, to_blue, to_red):
    side = device_side()
    inner = value_ref.shape[0] - HALO
    off = pl.multiple_of(side * inner, 128)
    to_blue[...] = value_ref[pl.ds(off, HALO), :].astype(BF)
    to_red[...] = value_ref[pl.ds(pl.multiple_of(inner - off, 128), HALO), :].astype(BF)


def first_kernel(band, t0, blue, red, t1, to_blue, to_red, wide):
    fill_wide(t0[...], blue[...].astype(F32), red[...].astype(F32), wide)
    height = PAIR_ATOMS * ORB
    for pair in range(band.shape[0]):
        t1[pair * height : (pair + 1) * height, :] = apply_band(band, wide, pair)
    put_sends(t1, to_blue, to_red)


def next_kernel(band, before, now, blue, red, after, to_blue, to_red, wide):
    fill_wide(now[...], blue[...].astype(F32), red[...].astype(F32), wide)
    height = PAIR_ATOMS * ORB
    for pair in range(band.shape[0]):
        span = slice(pair * height, (pair + 1) * height)
        after[span, :] = 2.0 * apply_band(band, wide, pair) - before[span, :]
    put_sends(after, to_blue, to_red)


def mix_kernel(coef, t0, t1, t2, t3, base, final):
    total = coef[0] * t0[...] + coef[1] * t1[...] + (coef[2] - coef[4]) * t2[...] + coef[3] * t3[...]
    base[...] = total.T
    final[...] = jnp.full(final.shape, 2.0 * coef[4], F32)


def last_kernel(final, band, base, t3, blue, red, p0, p1, p2, p3, wide, out):
    member = lax.axis_index("edges")
    fill_wide(t3[...], blue[...].astype(F32), red[...].astype(F32), wide)
    height = PAIR_ATOMS * ORB
    for pair in range(band.shape[0]):
        span = slice(pair * height, (pair + 1) * height)
        out[:, span] = base[:, span] + (final[0:1, :] * apply_band(band, wide, pair)).T
    for k, piece in enumerate((p0, p1, p2, p3)):
        high = piece.shape[0]
        piece[...] = out[pl.ds(pl.multiple_of((member ^ k) * high, high), high), :].astype(BF)


def join_kernel(p0, p1, p2, p3, out):
    member = lax.axis_index("edges")
    for k, piece in enumerate((p0, p1, p2, p3)):
        width = piece.shape[1]
        at = pl.multiple_of((member ^ k) * width, width)
        out[:, pl.ds(at, width)] = piece[...].astype(F32)


VMEM = pl.BlockSpec(memory_space=pltpu.VMEM)
SMEM = pl.BlockSpec(memory_space=pltpu.SMEM)
IN_HBM = pl.BlockSpec(memory_space=pltpu.HBM)
FULL, PART = 60 * 1024 * 1024, 32 * 1024 * 1024


def shape(dims, dtype):
    return jax.ShapeDtypeStruct(dims, dtype)


def call(kernel, name, outs, scratch, *args, smem=(), in_hbm=(), out_hbm=(), alias=None, limit=PART, micros=1):
    spaces = [SMEM if k in smem else IN_HBM if k in in_hbm else VMEM for k in range(len(args))]
    return pl.pallas_call(
        kernel,
        name=name,
        out_shape=outs,
        in_specs=spaces,
        out_specs=tuple(IN_HBM if k in out_hbm else VMEM for k in range(len(outs))),
        scratch_shapes=scratch,
        input_output_aliases=alias or {},
        cost_estimate=pl.CostEstimate(flops=micros * 10**9, bytes_accessed=0, transcendentals=0),
        compiler_params=pltpu.CompilerParams(vmem_limit_bytes=limit),
    )(*args)


def per_device(features, edge_src, edge_dst, edge_cell, cell_bias, w_in, w_out, vectors, cheb_coef):
    axes = ("rows", "edges")
    nedge = lax.axis_size("edges")
    ndev = lax.axis_size("rows") * nedge
    red_pairs = [(i, i ^ 1) for i in range(ndev)]
    blue_pairs = [(i, (i + 1) % ndev if i % 2 else (i - 1) % ndev) for i in range(ndev)]
    nown, nfeat = features.shape
    high, ncol = vectors.shape
    nrow = ncol // nedge

    def swap(first, last):
        return (
            lax.ppermute(first, axes, blue_pairs),
            lax.ppermute(last, axes, red_pairs),
        )

    def exchange(pieces):
        return [pieces[0]] + [
            lax.ppermute(pieces[k], "edges", [(i, i ^ k) for i in range(nedge)]) for k in (1, 2, 3)
        ]

    msg = shape((SPILL + ID_ROWS, nfeat), BF)
    piece = shape((high, nrow), BF)
    lines = (nown // 128, 128)
    edges = [x.reshape(lines) for x in (edge_src, edge_dst, edge_cell)]
    pieces = call(
        split_kernel,
        "split",
        (piece,) * 4,
        [pltpu.VMEM((nedge, high, nrow), F32), pltpu.SemaphoreType.DMA((4,))],
        vectors,
        in_hbm=(0,),
        limit=FULL,
    )
    pieces = exchange(pieces)
    blue_msg, red_msg = call(
        message_kernel,
        "message",
        (msg, msg),
        [pltpu.VMEM(lines, jnp.int32)] * 3
        + [pltpu.SemaphoreType.DMA((5,))],
        features,
        *edges,
        pieces[0],
        in_hbm=range(5),
        limit=FULL,
        micros=3,
    )
    blue_msg, red_msg = swap(blue_msg, red_msg)
    full, part = shape((nrow, VEC), F32), shape((HALO, VEC), BF)
    band_shape = shape((ATOM_Q // PAIR_ATOMS, PAIR_ATOMS * ORB, WIN_ATOMS * ORB), BF)
    width = w_in.shape[1]
    band, *weights = call(
        own_kernel,
        "own",
        (band_shape, shape((width, nfeat), BF), shape((width, 8), BF), shape((ORB * ORB, HID), BF)),
        [pltpu.VMEM((ORB * ORB, nown), BF), pltpu.VMEM((8, width), F32), pltpu.VMEM((8, nown), F32)],
        features,
        *edges,
        cell_bias,
        w_in,
        w_out,
        micros=4,
    )
    t0, to_blue, to_red = call(
        field_kernel, "field", (full, part, part), [pltpu.VMEM((VEC, nrow), F32)], *pieces
    )
    blue, red = swap(to_blue, to_red)

    spill_len = 2 * (SPILL + 64)
    (band,) = call(
        spill_kernel,
        "spill",
        (band_shape,),
        [pltpu.VMEM((ORB * ORB, spill_len), BF), pltpu.VMEM((spill_len, nfeat), BF)],
        band,
        blue_msg,
        red_msg,
        *weights,
        alias={0: 0},
    )

    wide = pltpu.VMEM((nrow + 2 * HALO, VEC), F32)
    t1, to_blue, to_red = call(first_kernel, "first", (full, part, part), [wide], band, t0, blue, red)
    fields = [t0, t1]
    for _ in range(2, STEPS):
        blue, red = swap(to_blue, to_red)
        following, to_blue, to_red = call(
            next_kernel, "next", (full, part, part), [wide], band, fields[-2], fields[-1], blue, red
        )
        fields.append(following)
    blue, red = swap(to_blue, to_red)
    base, final = call(
        mix_kernel, "mix", (shape((VEC, nrow), F32), shape((8, VEC), F32)), [], cheb_coef, *fields, smem=(0,)
    )
    pieces = call(
        last_kernel,
        "last",
        (piece,) * 4,
        [wide, pltpu.VMEM((VEC, nrow), F32)],
        final,
        band,
        base,
        fields[-1],
        blue,
        red,
    )
    (result,) = call(join_kernel, "join", (shape((high, ncol), F32),), [], *exchange(pieces))
    return result


def solution(mesh):
    placed = (
        P(("rows", "edges"), None),
        P(("rows", "edges")),
        P(("rows", "edges")),
        P(("rows", "edges")),
        P(),
        P(),
        P(),
        P("edges", "rows"),
        P(),
    )
    return jax.shard_map(
        per_device, mesh=mesh, in_specs=placed, out_specs=P("edges", "rows"), check_vma=False
    )
```

```python
import functools

import jax
import jax.numpy as jnp
from jax import lax
from jax.experimental import pallas as pl
from jax.experimental.pallas import tpu as pltpu
from jax.sharding import PartitionSpec as P

ORB = 16
TILE_ATOMS = 8
BAND = 3
HID = 256
VEC = 128
STEPS = 4
ATOM_Q = 32
SPILL = 320
ID_ROWS = 16
PAIR_ATOMS = 2 * TILE_ATOMS
WIN_ATOMS = (2 * BAND + 2) * TILE_ATOMS
HALO = BAND * TILE_ATOMS * ORB
GROUP = 4
GROUP_SPAN = 384
BF = jnp.bfloat16
F32 = jnp.float32
NT = (((1,), (1,)), ((), ()))


def nt_dot(a, b):
    return lax.dot_general(a, b, NT, preferred_element_type=F32)


def iota(shape, dim):
    return lax.broadcasted_iota(jnp.int32, shape, dim)


def device_side():
    return (lax.axis_index("rows") * lax.axis_size("edges") + lax.axis_index("edges")) % 2


def edge_ids(src, dst, cell):
    ndev = lax.axis_size("rows") * lax.axis_size("edges")
    quarter = lax.axis_index("rows") * lax.axis_size("edges") + lax.axis_index("edges")
    natom = ATOM_Q * ndev
    ntiles = natom // TILE_ATOMS
    rel = src - quarter * ATOM_Q
    rel = jnp.where(rel > natom // 2, rel - natom, jnp.where(rel < -(natom // 2), rel + natom, rel))
    shift = (dst >> 3) - (src >> 3) + BAND
    shift = jnp.where(shift < 0, shift + ntiles, jnp.where(shift >= ntiles, shift - ntiles, shift))
    return [x.astype(F32) for x in (rel, shift * TILE_ATOMS + (dst & 7), cell)]


def prep_kernel(
    vec_hbm, feat, src_hbm, dst_hbm, cell_hbm, p0, p1, p2, p3, blue, red, vectors, src, dst, cell, sems
):
    member, side = lax.axis_index("edges"), device_side()
    pieces = (p0, p1, p2, p3)
    loads = []
    for k, piece in enumerate(pieces):
        width = piece.shape[1]
        at = pl.multiple_of((member ^ k) * width, width)
        loads.append(pltpu.make_async_copy(vec_hbm.at[:, pl.ds(at, width)], vectors.at[k], sems.at[k]))
    high = feat.shape[0] - SPILL
    off = pl.multiple_of(side * high, 64)
    copies = [
        pltpu.make_async_copy(feat.at[pl.ds(off, SPILL)], blue.at[pl.ds(0, SPILL)], sems.at[4]),
        pltpu.make_async_copy(
            feat.at[pl.ds(pl.multiple_of(high - off, 64), SPILL)], red.at[pl.ds(0, SPILL)], sems.at[5]
        ),
    ]
    lists = [
        pltpu.make_async_copy(x, y, sems.at[6 + n])
        for n, (x, y) in enumerate(((src_hbm, src), (dst_hbm, dst), (cell_hbm, cell)))
    ]
    for copy in lists + loads + copies:
        copy.start()
    for copy in lists:
        copy.wait()
    three = edge_ids(src[...], dst[...], cell[...])
    lane, line = iota((3, 128), 1), iota((3, 128), 0)
    nrow = src.shape[0]
    starts = [x[0:3] for x in three]
    ends = [x[nrow - 3 : nrow] for x in three]
    starts[0] = jnp.where((line == 2) & (lane >= 64), -64.0, starts[0] + ATOM_Q)
    ends[0] = jnp.where((line == 0) & (lane < 64), -64.0, ends[0] - ATOM_Q)
    pad = jnp.zeros((ID_ROWS - 9, 128), F32)
    low_ids = jnp.concatenate(starts + [pad], axis=0)
    high_ids = jnp.concatenate(ends + [pad], axis=0)
    none = jnp.zeros((ID_ROWS, 128), BF)
    for msg, ids_of in (
        (blue, jnp.where(side == 0, low_ids, high_ids)),
        (red, jnp.where(side == 0, high_ids, low_ids)),
    ):
        msg[SPILL : SPILL + ID_ROWS, 0:128] = ids_of.astype(BF)
        msg[SPILL : SPILL + ID_ROWS, 128:256] = none
    for k, piece in enumerate(pieces):
        loads[k].wait()
        piece[...] = vectors[k].astype(BF)
    for copy in copies:
        copy.wait()


def field_kernel(p0, p1, p2, p3, t0, to_blue, to_red, field):
    member = lax.axis_index("edges")
    for k, piece in enumerate((p0, p1, p2, p3)):
        high = piece.shape[0]
        field[pl.ds(pl.multiple_of((member ^ k) * high, high), high), :] = piece[...].astype(F32)
    t0[...] = field[...].T
    put_sends(t0, to_blue, to_red)


def pair_blocks(x, cell, w_in_t, bias_t, w_out_t):
    bias = [bias_t[:, k : k + 1].astype(F32) for k in range(3)]
    pre = nt_dot(w_in_t[...], x)
    pre = pre + jnp.where(cell == 1.0, bias[1], jnp.where(cell == 2.0, bias[2], bias[0]))
    gate, up = pre[:HID], pre[HID:]
    hidden = (gate * (0.5 + 0.5 * jnp.tanh(0.5 * gate)) * up).astype(BF)
    return jnp.dot(w_out_t[...], hidden, preferred_element_type=F32).astype(BF)


def row_of(x):
    return jnp.concatenate([x[k : k + 1] for k in range(x.shape[0])], axis=1)


def dense_of(blocks, atom, target, first):
    span = atom.shape[1]
    column = (iota((WIN_ATOMS, span), 0).astype(F32) == target).astype(BF)
    onehot = [
        jnp.broadcast_to((atom == float(s)).astype(F32), (WIN_ATOMS, span)).astype(BF) * column
        for s in range(first, first + GROUP)
    ]
    return nt_dot(blocks, jnp.concatenate(onehot, axis=0))


def put_dense(band, dense, first, add):
    low = iota((ORB, 128), 1) < WIN_ATOMS
    for sp in range(GROUP // 2):
        s = first + 2 * sp
        pair, at_row = s // PAIR_ATOMS, s % PAIR_ATOMS * ORB
        for j in range(ORB // 2):
            x = dense[2 * j * ORB : (2 * j + 1) * ORB, sp * 128 : sp * 128 + 128]
            y = dense[(2 * j + 1) * ORB : (2 * j + 2) * ORB, sp * 128 : sp * 128 + 128]
            lanes = slice(j * 128, j * 128 + 128)
            both = (
                jnp.where(low, x, pltpu.roll(y, WIN_ATOMS, 1)),
                jnp.where(low, pltpu.roll(x, WIN_ATOMS, 1), y),
            )
            for n, value in enumerate(both):
                rows = slice(at_row + n * ORB, at_row + (n + 1) * ORB)
                if add:
                    value = value + band[pair, rows, lanes].astype(F32)
                band[pair, rows, lanes] = value.astype(BF)


def odd_tile(atom):
    return jnp.floor(atom * (1.0 / TILE_ATOMS)) - 2.0 * jnp.floor(atom * (0.5 / TILE_ATOMS))


def own_kernel(feat, src, dst, cell, cell_bias, w_in, w_out, band, w_in_t, bias_t, w_out_t, blk, bias8, rows):
    nfeat, width = w_in.shape
    nblk = w_out.shape[1]
    eye = (iota((width, width), 0) == iota((width, width), 1)).astype(BF)
    w_in_t[...] = nt_dot(eye, w_in[...]).astype(BF)
    bias8[...] = jnp.zeros(bias8.shape, F32)
    bias8[0:3, :] = cell_bias[...].astype(F32)
    bias_t[...] = nt_dot(eye, bias8[...].astype(BF)).astype(BF)
    row, col = iota((nblk, nblk), 0), iota((nblk, nblk), 1)
    swap = (col == (row % ORB) * ORB + row // ORB).astype(BF)
    w_out_t[...] = nt_dot(swap, w_out[...]).astype(BF)
    own = feat.shape[0]
    ids = edge_ids(src[...], dst[...], cell[...])
    atom = row_of(ids[0])
    rows[0:1, :] = atom
    rows[1:2, :] = row_of(ids[1]) + TILE_ATOMS * odd_tile(atom)
    blk[...] = pair_blocks(feat[...], row_of(ids[2]), w_in_t, bias_t, w_out_t)
    for first in range(0, ATOM_Q, GROUP):
        start = jnp.sum((ids[0] < float(first)).astype(F32)).astype(jnp.int32)
        at = pl.multiple_of(jnp.minimum(start // 128 * 128, own - GROUP_SPAN), 128)
        span = pl.ds(at, GROUP_SPAN)
        put_dense(band, dense_of(blk[:, span], rows[0:1, span], rows[1:2, span], first), first, False)


def spill_kernel(own_band, blue, red, w_in_t, bias_t, w_out_t, band, blk, spill):
    side = device_side()
    nfeat = spill.shape[1]
    rows = spill.shape[0] // 2
    for m, (msg, gap) in enumerate(((blue, side == 0), (red, side == 1))):
        base = m * rows
        spill[base : base + 64, :] = jnp.zeros((64, nfeat), BF)
        spill[base + rows - 64 : base + rows, :] = jnp.zeros((64, nfeat), BF)
        at = pl.multiple_of(base + jnp.where(gap, 64, 0), 64)
        spill[pl.ds(at, SPILL), :] = msg[0:SPILL, :]
    ids, ends = [], []
    for msg in (blue, red):
        block = msg[SPILL : SPILL + ID_ROWS, 0:128].astype(F32)
        a = block[0:3]
        mine = (a >= 0.0) & (a < float(ATOM_Q))
        ids.append([row_of(block[3 * k : 3 * k + 3]) for k in range(3)])
        ends.append(
            (
                jnp.min(jnp.where(mine, a, float(ATOM_Q))).astype(jnp.int32),
                jnp.max(jnp.where(mine, a, -1.0)).astype(jnp.int32),
            )
        )
    cells = jnp.concatenate([x[2] for x in ids], axis=1)
    blk[...] = pair_blocks(spill[...], cells, w_in_t, bias_t, w_out_t)
    band[...] = own_band[...]
    for m in range(2):
        atom, target = ids[m][0], ids[m][1] + TILE_ATOMS * odd_tile(ids[m][0])
        lowest, highest = ends[m]
        for first in range(0, ATOM_Q, GROUP):

            @pl.when((lowest < first + GROUP) & (highest >= first))
            def _(m=m, first=first, atom=atom, target=target):
                dense = dense_of(blk[:, m * rows : (m + 1) * rows], atom, target, first)
                put_dense(band, dense, first, True)


def apply_band(band, wide, pair):
    height = PAIR_ATOMS * ORB
    pieces = [
        wide[pl.ds(pair * height + q, WIN_ATOMS, stride=ORB), :] for q in range(ORB)
    ]
    rhs = jnp.concatenate(pieces, axis=0).astype(BF)
    return jnp.dot(band[pair], rhs, preferred_element_type=F32)


def fill_wide(own, blue, red, wide):
    side = device_side()
    rows = own.shape[0]
    end = HALO + rows
    off = pl.multiple_of(side * end, 128)
    wide[pl.ds(off, HALO), :] = blue
    wide[pl.ds(pl.multiple_of(end - off, 128), HALO), :] = red
    wide[HALO:end, :] = own


def put_sends(value_ref, to_blue, to_red):
    side = device_side()
    inner = value_ref.shape[0] - HALO
    off = pl.multiple_of(side * inner, 128)
    to_blue[...] = value_ref[pl.ds(off, HALO), :].astype(BF)
    to_red[...] = value_ref[pl.ds(pl.multiple_of(inner - off, 128), HALO), :].astype(BF)


def first_kernel(band, t0, blue, red, t1, to_blue, to_red, wide):
    fill_wide(t0[...], blue[...].astype(F32), red[...].astype(F32), wide)
    height = PAIR_ATOMS * ORB
    for pair in range(band.shape[0]):
        t1[pair * height : (pair + 1) * height, :] = apply_band(band, wide, pair)
    put_sends(t1, to_blue, to_red)


def next_kernel(band, before, now, blue, red, after, to_blue, to_red, wide):
    fill_wide(now[...], blue[...].astype(F32), red[...].astype(F32), wide)
    height = PAIR_ATOMS * ORB
    for pair in range(band.shape[0]):
        span = slice(pair * height, (pair + 1) * height)
        after[span, :] = 2.0 * apply_band(band, wide, pair) - before[span, :]
    put_sends(after, to_blue, to_red)


def mix_kernel(coef, t0, t1, t2, t3, base, final):
    total = coef[0] * t0[...] + coef[1] * t1[...] + (coef[2] - coef[4]) * t2[...] + coef[3] * t3[...]
    base[...] = total.T
    final[...] = jnp.full(final.shape, 2.0 * coef[4], F32)


def last_kernel(final, band, base, t3, blue, red, p0, p1, p2, p3, wide, out):
    member = lax.axis_index("edges")
    fill_wide(t3[...], blue[...].astype(F32), red[...].astype(F32), wide)
    height = PAIR_ATOMS * ORB
    for pair in range(band.shape[0]):
        span = slice(pair * height, (pair + 1) * height)
        out[:, span] = base[:, span] + (final[0:1, :] * apply_band(band, wide, pair)).T
    for k, piece in enumerate((p0, p1, p2, p3)):
        high = piece.shape[0]
        piece[...] = out[pl.ds(pl.multiple_of((member ^ k) * high, high), high), :].astype(BF)


def join_kernel(p0, p1, p2, p3, out):
    member = lax.axis_index("edges")
    for k, piece in enumerate((p0, p1, p2, p3)):
        width = piece.shape[1]
        at = pl.multiple_of((member ^ k) * width, width)
        out[:, pl.ds(at, width)] = piece[...].astype(F32)


VMEM = pl.BlockSpec(memory_space=pltpu.VMEM)
SMEM = pl.BlockSpec(memory_space=pltpu.SMEM)
IN_HBM = pl.BlockSpec(memory_space=pltpu.HBM)
FULL, PART = 60 * 1024 * 1024, 32 * 1024 * 1024


def shape(dims, dtype):
    return jax.ShapeDtypeStruct(dims, dtype)


def call(kernel, name, outs, scratch, *args, smem=(), in_hbm=(), out_hbm=(), alias=None, limit=PART, micros=1):
    spaces = [SMEM if k in smem else IN_HBM if k in in_hbm else VMEM for k in range(len(args))]
    return pl.pallas_call(
        kernel,
        name=name,
        out_shape=outs,
        in_specs=spaces,
        out_specs=tuple(IN_HBM if k in out_hbm else VMEM for k in range(len(outs))),
        scratch_shapes=scratch,
        input_output_aliases=alias or {},
        cost_estimate=pl.CostEstimate(flops=micros * 10**9, bytes_accessed=0, transcendentals=0),
        compiler_params=pltpu.CompilerParams(vmem_limit_bytes=limit),
    )(*args)


def per_device(features, edge_src, edge_dst, edge_cell, cell_bias, w_in, w_out, vectors, cheb_coef):
    axes = ("rows", "edges")
    nedge = lax.axis_size("edges")
    ndev = lax.axis_size("rows") * nedge
    red_pairs = [(i, i ^ 1) for i in range(ndev)]
    blue_pairs = [(i, (i + 1) % ndev if i % 2 else (i - 1) % ndev) for i in range(ndev)]
    nown, nfeat = features.shape
    high, ncol = vectors.shape
    nrow = ncol // nedge

    def swap(first, last):
        return (
            lax.ppermute(first, axes, blue_pairs),
            lax.ppermute(last, axes, red_pairs),
        )

    def exchange(pieces):
        return [pieces[0]] + [
            lax.ppermute(pieces[k], "edges", [(i, i ^ k) for i in range(nedge)]) for k in (1, 2, 3)
        ]

    msg = shape((SPILL + ID_ROWS, nfeat), BF)
    piece = shape((high, nrow), BF)
    lines = (nown // 128, 128)
    edges = [x.reshape(lines) for x in (edge_src, edge_dst, edge_cell)]
    *pieces, blue_msg, red_msg = call(
        prep_kernel,
        "prep",
        (piece,) * 4 + (msg, msg),
        [pltpu.VMEM((nedge, high, nrow), F32)]
        + [pltpu.VMEM(lines, jnp.int32)] * 3
        + [pltpu.SemaphoreType.DMA((9,))],
        vectors,
        features,
        *edges,
        in_hbm=range(5),
        limit=FULL,
    )
    pieces = exchange(pieces)
    blue_msg, red_msg = swap(blue_msg, red_msg)
    full, part = shape((nrow, VEC), F32), shape((HALO, VEC), BF)
    band_shape = shape((ATOM_Q // PAIR_ATOMS, PAIR_ATOMS * ORB, WIN_ATOMS * ORB), BF)
    width = w_in.shape[1]
    band, *weights = call(
        own_kernel,
        "own",
        (band_shape, shape((width, nfeat), BF), shape((width, 8), BF), shape((ORB * ORB, HID), BF)),
        [pltpu.VMEM((ORB * ORB, nown), BF), pltpu.VMEM((8, width), F32), pltpu.VMEM((8, nown), F32)],
        features,
        *edges,
        cell_bias,
        w_in,
        w_out,
        micros=4,
    )
    t0, to_blue, to_red = call(
        field_kernel, "field", (full, part, part), [pltpu.VMEM((VEC, nrow), F32)], *pieces
    )
    blue, red = swap(to_blue, to_red)

    spill_len = 2 * (SPILL + 64)
    (band,) = call(
        spill_kernel,
        "spill",
        (band_shape,),
        [pltpu.VMEM((ORB * ORB, spill_len), BF), pltpu.VMEM((spill_len, nfeat), BF)],
        band,
        blue_msg,
        red_msg,
        *weights,
        alias={0: 0},
        micros=0,
    )

    wide = pltpu.VMEM((nrow + 2 * HALO, VEC), F32)
    t1, to_blue, to_red = call(first_kernel, "first", (full, part, part), [wide], band, t0, blue, red)
    fields = [t0, t1]
    for _ in range(2, STEPS):
        blue, red = swap(to_blue, to_red)
        following, to_blue, to_red = call(
            next_kernel, "next", (full, part, part), [wide], band, fields[-2], fields[-1], blue, red
        )
        fields.append(following)
    blue, red = swap(to_blue, to_red)
    base, final = call(
        mix_kernel, "mix", (shape((VEC, nrow), F32), shape((8, VEC), F32)), [], cheb_coef, *fields, smem=(0,)
    )
    pieces = call(
        last_kernel,
        "last",
        (piece,) * 4,
        [wide, pltpu.VMEM((VEC, nrow), F32)],
        final,
        band,
        base,
        fields[-1],
        blue,
        red,
    )
    (result,) = call(join_kernel, "join", (shape((high, ncol), F32),), [], *exchange(pieces))
    return result


def solution(mesh):
    placed = (
        P(("rows", "edges"), None),
        P(("rows", "edges")),
        P(("rows", "edges")),
        P(("rows", "edges")),
        P(),
        P(),
        P(),
        P("edges", "rows"),
        P(),
    )
    return jax.shard_map(
        per_device, mesh=mesh, in_specs=placed, out_specs=P("edges", "rows"), check_vma=False
    )
```

```python
import functools

import jax
import jax.numpy as jnp
from jax import lax
from jax.experimental import pallas as pl
from jax.experimental.pallas import tpu as pltpu
from jax.sharding import PartitionSpec as P

ORB = 16
TILE_ATOMS = 8
BAND = 3
HID = 256
VEC = 128
STEPS = 4
ATOM_Q = 32
SPILL = 320
ID_ROWS = 16
PAIR_ATOMS = 2 * TILE_ATOMS
WIN_ATOMS = (2 * BAND + 2) * TILE_ATOMS
HALO = BAND * TILE_ATOMS * ORB
GROUP = 4
GROUP_SPAN = 384
HALF = ATOM_Q * ORB
NEAR = 3
BF = jnp.bfloat16
F32 = jnp.float32
NT = (((1,), (1,)), ((), ()))


def nt_dot(a, b):
    return lax.dot_general(a, b, NT, preferred_element_type=F32)


def iota(shape, dim):
    return lax.broadcasted_iota(jnp.int32, shape, dim)


def device_side():
    return (lax.axis_index("rows") * lax.axis_size("edges") + lax.axis_index("edges")) % 2


def edge_ids(src, dst, cell):
    ndev = lax.axis_size("rows") * lax.axis_size("edges")
    quarter = lax.axis_index("rows") * lax.axis_size("edges") + lax.axis_index("edges")
    natom = ATOM_Q * ndev
    ntiles = natom // TILE_ATOMS
    rel = src - quarter * ATOM_Q
    rel = jnp.where(rel > natom // 2, rel - natom, jnp.where(rel < -(natom // 2), rel + natom, rel))
    shift = (dst >> 3) - (src >> 3) + BAND
    shift = jnp.where(shift < 0, shift + ntiles, jnp.where(shift >= ntiles, shift - ntiles, shift))
    return [x.astype(F32) for x in (rel, shift * TILE_ATOMS + (dst & 7), cell)]


def prep_kernel(
    vec_hbm, feat, src_hbm, dst_hbm, cell_hbm, p0, p1, p2, p3, blue, red, vectors, src, dst, cell, sems
):
    member, side = lax.axis_index("edges"), device_side()
    pieces = (p0, p1, p2, p3)
    loads = []
    for k, piece in enumerate(pieces):
        width = piece.shape[1]
        at = pl.multiple_of((member ^ k) * width, width)
        loads.append(pltpu.make_async_copy(vec_hbm.at[:, pl.ds(at, width)], vectors.at[k], sems.at[k]))
    high = feat.shape[0] - SPILL
    off = pl.multiple_of(side * high, 64)
    copies = [
        pltpu.make_async_copy(feat.at[pl.ds(off, SPILL)], blue.at[pl.ds(0, SPILL)], sems.at[4]),
        pltpu.make_async_copy(
            feat.at[pl.ds(pl.multiple_of(high - off, 64), SPILL)], red.at[pl.ds(0, SPILL)], sems.at[5]
        ),
    ]
    lists = [
        pltpu.make_async_copy(x, y, sems.at[6 + n])
        for n, (x, y) in enumerate(((src_hbm, src), (dst_hbm, dst), (cell_hbm, cell)))
    ]
    for copy in lists + loads + copies:
        copy.start()
    for copy in lists:
        copy.wait()
    three = edge_ids(src[...], dst[...], cell[...])
    lane, line = iota((3, 128), 1), iota((3, 128), 0)
    nrow = src.shape[0]
    starts = [x[0:3] for x in three]
    ends = [x[nrow - 3 : nrow] for x in three]
    starts[0] = jnp.where((line == 2) & (lane >= 64), -64.0, starts[0] + ATOM_Q)
    ends[0] = jnp.where((line == 0) & (lane < 64), -64.0, ends[0] - ATOM_Q)
    pad = jnp.zeros((ID_ROWS - 9, 128), F32)
    low_ids = jnp.concatenate(starts + [pad], axis=0)
    high_ids = jnp.concatenate(ends + [pad], axis=0)
    none = jnp.zeros((ID_ROWS, 128), BF)
    for msg, ids_of in (
        (blue, jnp.where(side == 0, low_ids, high_ids)),
        (red, jnp.where(side == 0, high_ids, low_ids)),
    ):
        msg[SPILL : SPILL + ID_ROWS, 0:128] = ids_of.astype(BF)
        msg[SPILL : SPILL + ID_ROWS, 128:256] = none
    for k, piece in enumerate(pieces):
        loads[k].wait()
        piece[...] = vectors[k].astype(BF)
    for copy in copies:
        copy.wait()


def field_kernel(p0, p1, p2, p3, t0, to_blue, to_red, field):
    member = lax.axis_index("edges")
    for k, piece in enumerate((p0, p1, p2, p3)):
        high = piece.shape[0]
        field[pl.ds(pl.multiple_of((member ^ k) * high, high), high), :] = piece[...].astype(F32)
    t0[...] = field[...].T
    put_sends(t0, to_blue, to_red)


def pair_blocks(x, cell, w_in_t, bias_t, w_out_t):
    bias = [bias_t[:, k : k + 1].astype(F32) for k in range(3)]
    pre = nt_dot(w_in_t[...], x)
    pre = pre + jnp.where(cell == 1.0, bias[1], jnp.where(cell == 2.0, bias[2], bias[0]))
    gate, up = pre[:HID], pre[HID:]
    hidden = (gate * (0.5 + 0.5 * jnp.tanh(0.5 * gate)) * up).astype(BF)
    return jnp.dot(w_out_t[...], hidden, preferred_element_type=F32).astype(BF)


def row_of(x):
    return jnp.concatenate([x[k : k + 1] for k in range(x.shape[0])], axis=1)


def dense_of(blocks, atom, target, first):
    span = atom.shape[1]
    column = (iota((WIN_ATOMS, span), 0).astype(F32) == target).astype(BF)
    onehot = [
        jnp.broadcast_to((atom == float(s)).astype(F32), (WIN_ATOMS, span)).astype(BF) * column
        for s in range(first, first + GROUP)
    ]
    return nt_dot(blocks, jnp.concatenate(onehot, axis=0))


def put_dense(band, dense, first, base=None):
    quarter_lane = iota((ORB, 128), 1) // ATOM_Q
    for sp in range(GROUP // 2):
        s = first + 2 * sp
        pair, at_row = s // PAIR_ATOMS, s % PAIR_ATOMS * ORB
        for m in range(ORB // 4):
            x = [
                dense[(4 * m + i) * ORB : (4 * m + i + 1) * ORB, sp * 128 : sp * 128 + 128] for i in range(4)
            ]
            for c in range(4):
                turned = [pltpu.roll(x[i], (i - c) % 4 * ATOM_Q, 1) if i != c else x[i] for i in range(4)]
                value = turned[0]
                for i in range(1, 4):
                    value = jnp.where(quarter_lane == i, turned[i], value)
                rows = slice(at_row + c // 2 * ORB, at_row + (c // 2 + 1) * ORB)
                lo = c % 2 * HALF + m * 128
                if base is not None:
                    value = value + base[pair, rows, lo : lo + 128].astype(F32)
                band[pair, rows, lo : lo + 128] = value.astype(BF)


def column_of(atom, offset):
    target = TILE_ATOMS * (jnp.floor(atom * (1.0 / TILE_ATOMS)) - BAND) + offset
    base = BAND * TILE_ATOMS - PAIR_ATOMS * jnp.floor(atom * (1.0 / PAIR_ATOMS))
    outside = jnp.where(target < 0.0, target + (base + ATOM_Q), target + base)
    return jnp.where((target >= 0.0) & (target < float(ATOM_Q)), target, outside)


def own_kernel(feat, src, dst, cell, cell_bias, w_in, w_out, band, w_in_t, bias_t, w_out_t, blk, bias8, rows):
    nfeat, width = w_in.shape
    nblk = w_out.shape[1]
    eye = (iota((width, width), 0) == iota((width, width), 1)).astype(BF)
    w_in_t[...] = nt_dot(eye, w_in[...]).astype(BF)
    bias8[...] = jnp.zeros(bias8.shape, F32)
    bias8[0:3, :] = cell_bias[...].astype(F32)
    bias_t[...] = nt_dot(eye, bias8[...].astype(BF)).astype(BF)
    row, col = iota((nblk, nblk), 0), iota((nblk, nblk), 1)
    swap = (col == (row % ORB) * ORB + row // ORB).astype(BF)
    w_out_t[...] = nt_dot(swap, w_out[...]).astype(BF)
    own = feat.shape[0]
    ids = edge_ids(src[...], dst[...], cell[...])
    atom = row_of(ids[0])
    rows[0:1, :] = atom
    rows[1:2, :] = column_of(atom, row_of(ids[1]))
    blk[...] = pair_blocks(feat[...], row_of(ids[2]), w_in_t, bias_t, w_out_t)
    for first in range(0, ATOM_Q, GROUP):
        start = jnp.sum((ids[0] < float(first)).astype(F32)).astype(jnp.int32)
        at = pl.multiple_of(jnp.minimum(start // 128 * 128, own - GROUP_SPAN), 128)
        span = pl.ds(at, GROUP_SPAN)
        put_dense(band, dense_of(blk[:, span], rows[0:1, span], rows[1:2, span], first), first)


def spill_kernel(own_band, blue, red, w_in_t, bias_t, w_out_t, band, blk, spill):
    even = device_side() == 0
    nfeat = spill.shape[1]
    rows = spill.shape[0] // 2
    left, right = [jnp.where(even, x, y) for x, y in ((blue[...], red[...]), (red[...], blue[...]))]
    spill[0:64, :] = jnp.zeros((64, nfeat), BF)
    spill[64 : rows + SPILL, :] = jnp.concatenate([left[0:SPILL], right[0:SPILL]], axis=0)
    spill[rows + SPILL :, :] = jnp.zeros((64, nfeat), BF)
    ids = []
    for msg in (left, right):
        block = msg[SPILL : SPILL + ID_ROWS, 0:128].astype(F32)
        ids.append([row_of(block[3 * k : 3 * k + 3]) for k in range(3)])
    atoms = [x[0] for x in ids]
    cols = [column_of(x[0], x[1]) for x in ids]
    mine = [(a >= 0.0) & (a < float(ATOM_Q)) for a in atoms]
    highest = jnp.max(jnp.where(mine[0], atoms[0], -1.0)).astype(jnp.int32)
    lowest = jnp.min(jnp.where(mine[1], atoms[1], float(ATOM_Q))).astype(jnp.int32)
    cells = jnp.concatenate([x[2] for x in ids], axis=1)
    blk[...] = pair_blocks(spill[...], cells, w_in_t, bias_t, w_out_t)
    spans = [slice(0, rows), slice(rows, 2 * rows)]
    ngroup = ATOM_Q // GROUP
    for g in range(ngroup):
        first = g * GROUP
        sides = [m for m in range(2) if (g < NEAR, g >= ngroup - NEAR)[m]]
        if sides:
            (m,) = sides
            put_dense(band, dense_of(blk[:, spans[m]], atoms[m], cols[m], first), first, own_band)
        else:
            pair, at = first // PAIR_ATOMS, first % PAIR_ATOMS * ORB
            band[pair, at : at + GROUP * ORB, :] = own_band[pair, at : at + GROUP * ORB, :]
    for m, far in ((0, range(NEAR, ngroup)), (1, range(ngroup - NEAR))):
        for g in far:
            first = g * GROUP

            @pl.when(highest >= first if m == 0 else lowest < first + GROUP)
            def _(m=m, first=first):
                put_dense(band, dense_of(blk[:, spans[m]], atoms[m], cols[m], first), first, band)


def own_part(band, field):
    pieces = [field[pl.ds(q, ATOM_Q, stride=ORB), :].astype(BF) for q in range(ORB)]
    rhs = jnp.concatenate(pieces, axis=0)
    return [jnp.dot(band[k, :, :HALF], rhs, preferred_element_type=F32) for k in range(band.shape[0])]


def halo_part(band, blue, red, wide):
    even = device_side() == 0
    wide[0:HALO, :] = jnp.where(even, blue[...], red[...]).astype(F32)
    wide[HALO : 2 * HALO, :] = jnp.where(even, red[...], blue[...]).astype(F32)
    atoms = BAND * TILE_ATOMS
    pieces = [[], []]
    for q in range(ORB):
        left = wide[pl.ds(q, atoms, stride=ORB), :]
        right = wide[pl.ds(HALO + q, atoms, stride=ORB), :]
        pieces[0].append(jnp.concatenate([left, right[:TILE_ATOMS]], axis=0).astype(BF))
        pieces[1].append(jnp.concatenate([left[atoms - TILE_ATOMS :], right], axis=0).astype(BF))
    return [
        jnp.dot(band[k, :, HALF:], jnp.concatenate(pieces[k], axis=0), preferred_element_type=F32)
        for k in range(band.shape[0])
    ]


def put_sends(value_ref, to_blue, to_red):
    side = device_side()
    inner = value_ref.shape[0] - HALO
    off = pl.multiple_of(side * inner, 128)
    to_blue[...] = value_ref[pl.ds(off, HALO), :].astype(BF)
    to_red[...] = value_ref[pl.ds(pl.multiple_of(inner - off, 128), HALO), :].astype(BF)


def spans_of(band):
    height = band.shape[1]
    return [slice(k * height, (k + 1) * height) for k in range(band.shape[0])]


def first_kernel(band, t0, blue, red, t1, to_blue, to_red, wide):
    inner, outer = own_part(band, t0), halo_part(band, blue, red, wide)
    for k, span in enumerate(spans_of(band)):
        t1[span, :] = inner[k] + outer[k]
    put_sends(t1, to_blue, to_red)


def inner_kernel(band, before, now, part):
    inner = own_part(band, now)
    for k, span in enumerate(spans_of(band)):
        part[span, :] = 2.0 * inner[k] - before[span, :]


def outer_kernel(band, part, blue, red, after, to_blue, to_red, wide):
    outer = halo_part(band, blue, red, wide)
    for k, span in enumerate(spans_of(band)):
        after[span, :] = 2.0 * outer[k] + part[span, :]
    put_sends(after, to_blue, to_red)


def mix_kernel(coef, band, t0, t1, t2, t3, base, final):
    inner = own_part(band, t3)
    for k, span in enumerate(spans_of(band)):
        total = coef[0] * t0[span, :] + coef[1] * t1[span, :] + (coef[2] - coef[4]) * t2[span, :]
        total = total + coef[3] * t3[span, :] + 2.0 * coef[4] * inner[k]
        base[:, span] = total.T
    final[...] = jnp.full(final.shape, 2.0 * coef[4], F32)


def last_kernel(final, band, base, blue, red, p0, p1, p2, p3, wide, out):
    member = lax.axis_index("edges")
    outer = halo_part(band, blue, red, wide)
    for k, span in enumerate(spans_of(band)):
        out[:, span] = base[:, span] + (final[0:1, :] * outer[k]).T
    for k, piece in enumerate((p0, p1, p2, p3)):
        high = piece.shape[0]
        piece[...] = out[pl.ds(pl.multiple_of((member ^ k) * high, high), high), :].astype(BF)


def join_kernel(p0, p1, p2, p3, out):
    member = lax.axis_index("edges")
    for k, piece in enumerate((p0, p1, p2, p3)):
        width = piece.shape[1]
        at = pl.multiple_of((member ^ k) * width, width)
        out[:, pl.ds(at, width)] = piece[...].astype(F32)


VMEM = pl.BlockSpec(memory_space=pltpu.VMEM)
SMEM = pl.BlockSpec(memory_space=pltpu.SMEM)
IN_HBM = pl.BlockSpec(memory_space=pltpu.HBM)
FULL, PART = 60 * 1024 * 1024, 32 * 1024 * 1024


def shape(dims, dtype):
    return jax.ShapeDtypeStruct(dims, dtype)


def call(kernel, name, outs, scratch, *args, smem=(), in_hbm=(), out_hbm=(), alias=None, limit=PART, micros=1):
    spaces = [SMEM if k in smem else IN_HBM if k in in_hbm else VMEM for k in range(len(args))]
    return pl.pallas_call(
        kernel,
        name=name,
        out_shape=outs,
        in_specs=spaces,
        out_specs=tuple(IN_HBM if k in out_hbm else VMEM for k in range(len(outs))),
        scratch_shapes=scratch,
        input_output_aliases=alias or {},
        cost_estimate=pl.CostEstimate(flops=micros * 10**9, bytes_accessed=0, transcendentals=0),
        compiler_params=pltpu.CompilerParams(vmem_limit_bytes=limit),
    )(*args)


def per_device(features, edge_src, edge_dst, edge_cell, cell_bias, w_in, w_out, vectors, cheb_coef):
    axes = ("rows", "edges")
    nedge = lax.axis_size("edges")
    ndev = lax.axis_size("rows") * nedge
    red_pairs = [(i, i ^ 1) for i in range(ndev)]
    blue_pairs = [(i, (i + 1) % ndev if i % 2 else (i - 1) % ndev) for i in range(ndev)]
    nown, nfeat = features.shape
    high, ncol = vectors.shape
    nrow = ncol // nedge

    def swap(first, last):
        return (
            lax.ppermute(first, axes, blue_pairs),
            lax.ppermute(last, axes, red_pairs),
        )

    def exchange(pieces):
        return [pieces[0]] + [
            lax.ppermute(pieces[k], "edges", [(i, i ^ k) for i in range(nedge)]) for k in (1, 2, 3)
        ]

    msg = shape((SPILL + ID_ROWS, nfeat), BF)
    piece = shape((high, nrow), BF)
    lines = (nown // 128, 128)
    edges = [x.reshape(lines) for x in (edge_src, edge_dst, edge_cell)]
    *pieces, blue_msg, red_msg = call(
        prep_kernel,
        "prep",
        (piece,) * 4 + (msg, msg),
        [pltpu.VMEM((nedge, high, nrow), F32)]
        + [pltpu.VMEM(lines, jnp.int32)] * 3
        + [pltpu.SemaphoreType.DMA((9,))],
        vectors,
        features,
        *edges,
        in_hbm=range(5),
        limit=FULL,
    )
    pieces = exchange(pieces)
    blue_msg, red_msg = swap(blue_msg, red_msg)
    full, part = shape((nrow, VEC), F32), shape((HALO, VEC), BF)
    band_shape = shape((ATOM_Q // PAIR_ATOMS, PAIR_ATOMS * ORB, WIN_ATOMS * ORB), BF)
    width = w_in.shape[1]
    band, *weights = call(
        own_kernel,
        "own",
        (band_shape, shape((width, nfeat), BF), shape((width, 8), BF), shape((ORB * ORB, HID), BF)),
        [pltpu.VMEM((ORB * ORB, nown), BF), pltpu.VMEM((8, width), F32), pltpu.VMEM((8, nown), F32)],
        features,
        *edges,
        cell_bias,
        w_in,
        w_out,
        micros=4,
    )
    t0, to_blue, to_red = call(
        field_kernel, "field", (full, part, part), [pltpu.VMEM((VEC, nrow), F32)], *pieces
    )
    blue, red = swap(to_blue, to_red)

    spill_len = 2 * (SPILL + 64)
    (band,) = call(
        spill_kernel,
        "spill",
        (band_shape,),
        [pltpu.VMEM((ORB * ORB, spill_len), BF), pltpu.VMEM((spill_len, nfeat), BF)],
        band,
        blue_msg,
        red_msg,
        *weights,
        alias={0: 0},
        micros=0,
    )

    wide = pltpu.VMEM((2 * HALO, VEC), F32)
    t1, to_blue, to_red = call(first_kernel, "first", (full, part, part), [wide], band, t0, blue, red)
    fields = [t0, t1]
    for _ in range(2, STEPS):
        blue, red = swap(to_blue, to_red)
        (inner,) = call(inner_kernel, "inner", (full,), [], band, fields[-2], fields[-1])
        following, to_blue, to_red = call(
            outer_kernel, "outer", (full, part, part), [wide], band, inner, blue, red
        )
        fields.append(following)
    blue, red = swap(to_blue, to_red)
    base, final = call(
        mix_kernel,
        "mix",
        (shape((VEC, nrow), F32), shape((8, VEC), F32)),
        [],
        cheb_coef,
        band,
        *fields,
        smem=(0,),
    )
    pieces = call(
        last_kernel,
        "last",
        (piece,) * 4,
        [wide, pltpu.VMEM((VEC, nrow), F32)],
        final,
        band,
        base,
        blue,
        red,
    )
    (result,) = call(join_kernel, "join", (shape((high, ncol), F32),), [], *exchange(pieces))
    return result


def solution(mesh):
    placed = (
        P(("rows", "edges"), None),
        P(("rows", "edges")),
        P(("rows", "edges")),
        P(("rows", "edges")),
        P(),
        P(),
        P(),
        P("edges", "rows"),
        P(),
    )
    return jax.shard_map(
        per_device, mesh=mesh, in_specs=placed, out_specs=P("edges", "rows"), check_vma=False
    )
```

```python
import functools

import jax
import jax.numpy as jnp
from jax import lax
from jax.experimental import pallas as pl
from jax.experimental.pallas import tpu as pltpu
from jax.sharding import PartitionSpec as P

ORB = 16
TILE_ATOMS = 8
BAND = 3
HID = 256
VEC = 128
STEPS = 4
ATOM_Q = 32
SPILL = 320
ID_ROWS = 16
PAIR_ATOMS = 2 * TILE_ATOMS
WIN_ATOMS = (2 * BAND + 2) * TILE_ATOMS
HALO = BAND * TILE_ATOMS * ORB
GROUP = 4
GROUP_SPAN = 384
HALF = ATOM_Q * ORB
NEAR = 3
BF = jnp.bfloat16
F32 = jnp.float32
NT = (((1,), (1,)), ((), ()))


def nt_dot(a, b):
    return lax.dot_general(a, b, NT, preferred_element_type=F32)


def iota(shape, dim):
    return lax.broadcasted_iota(jnp.int32, shape, dim)


def device_side():
    return (lax.axis_index("rows") * lax.axis_size("edges") + lax.axis_index("edges")) % 2


def edge_ids(src, dst, cell):
    ndev = lax.axis_size("rows") * lax.axis_size("edges")
    quarter = lax.axis_index("rows") * lax.axis_size("edges") + lax.axis_index("edges")
    natom = ATOM_Q * ndev
    ntiles = natom // TILE_ATOMS
    rel = src - quarter * ATOM_Q
    rel = jnp.where(rel > natom // 2, rel - natom, jnp.where(rel < -(natom // 2), rel + natom, rel))
    shift = (dst >> 3) - (src >> 3) + BAND
    shift = jnp.where(shift < 0, shift + ntiles, jnp.where(shift >= ntiles, shift - ntiles, shift))
    return [x.astype(F32) for x in (rel, shift * TILE_ATOMS + (dst & 7), cell)]


def prep_kernel(
    vec_hbm, feat, src_hbm, dst_hbm, cell_hbm, p0, p1, far, blue, red, vectors, src, dst, cell, sems
):
    member, side = lax.axis_index("edges"), device_side()
    pieces = (p0, p1, far.at[0], far.at[1])
    loads = []
    width = p0.shape[1]
    for k in range(4):
        at = pl.multiple_of((member ^ k) * width, width)
        loads.append(pltpu.make_async_copy(vec_hbm.at[:, pl.ds(at, width)], vectors.at[k], sems.at[k]))
    high = feat.shape[0] - SPILL
    off = pl.multiple_of(side * high, 64)
    copies = [
        pltpu.make_async_copy(feat.at[pl.ds(off, SPILL)], blue.at[pl.ds(0, SPILL)], sems.at[4]),
        pltpu.make_async_copy(
            feat.at[pl.ds(pl.multiple_of(high - off, 64), SPILL)], red.at[pl.ds(0, SPILL)], sems.at[5]
        ),
    ]
    lists = [
        pltpu.make_async_copy(x, y, sems.at[6 + n])
        for n, (x, y) in enumerate(((src_hbm, src), (dst_hbm, dst), (cell_hbm, cell)))
    ]
    for copy in lists + loads + copies:
        copy.start()
    for copy in lists:
        copy.wait()
    three = edge_ids(src[...], dst[...], cell[...])
    lane, line = iota((3, 128), 1), iota((3, 128), 0)
    nrow = src.shape[0]
    starts = [x[0:3] for x in three]
    ends = [x[nrow - 3 : nrow] for x in three]
    starts[0] = jnp.where((line == 2) & (lane >= 64), -64.0, starts[0] + ATOM_Q)
    ends[0] = jnp.where((line == 0) & (lane < 64), -64.0, ends[0] - ATOM_Q)
    pad = jnp.zeros((ID_ROWS - 9, 128), F32)
    low_ids = jnp.concatenate(starts + [pad], axis=0)
    high_ids = jnp.concatenate(ends + [pad], axis=0)
    none = jnp.zeros((ID_ROWS, 128), BF)
    for msg, ids_of in (
        (blue, jnp.where(side == 0, low_ids, high_ids)),
        (red, jnp.where(side == 0, high_ids, low_ids)),
    ):
        msg[SPILL : SPILL + ID_ROWS, 0:128] = ids_of.astype(BF)
        msg[SPILL : SPILL + ID_ROWS, 128:256] = none
    for k, piece in enumerate(pieces):
        loads[k].wait()
        piece[...] = vectors[k].astype(BF)
    for copy in copies:
        copy.wait()


def relay_kernel(far, onward):
    onward[...] = far[1]


def field_kernel(p0, p1, far, p3, t0, to_blue, to_red, token, field):
    member = lax.axis_index("edges")
    for k, piece in enumerate((p0, p1, far.at[0], p3)):
        high = piece.shape[0]
        field[pl.ds(pl.multiple_of((member ^ k) * high, high), high), :] = piece[...].astype(F32)
    t0[...] = field[...].T
    token[...] = jnp.zeros(token.shape, F32)
    put_sends(t0, to_blue, to_red)


def pair_blocks(x, cell, w_in_t, bias_t, w_out_t):
    bias = [bias_t[:, k : k + 1].astype(F32) for k in range(3)]
    pre = nt_dot(w_in_t[...], x)
    pre = pre + jnp.where(cell == 1.0, bias[1], jnp.where(cell == 2.0, bias[2], bias[0]))
    gate, up = pre[:HID], pre[HID:]
    hidden = (gate * (0.5 + 0.5 * jnp.tanh(0.5 * gate)) * up).astype(BF)
    return jnp.dot(w_out_t[...], hidden, preferred_element_type=F32).astype(BF)


def row_of(x):
    return jnp.concatenate([x[k : k + 1] for k in range(x.shape[0])], axis=1)


def dense_of(blocks, atom, target, first):
    span = atom.shape[1]
    column = (iota((WIN_ATOMS, span), 0).astype(F32) == target).astype(BF)
    onehot = [
        jnp.broadcast_to((atom == float(s)).astype(F32), (WIN_ATOMS, span)).astype(BF) * column
        for s in range(first, first + GROUP)
    ]
    return nt_dot(blocks, jnp.concatenate(onehot, axis=0))


def put_dense(band, dense, first, base=None):
    lane = iota((ORB, 128), 1)
    low, even = lane < 64, lane % 64 < ATOM_Q
    for sp in range(GROUP // 2):
        s = first + 2 * sp
        pair, at_row = s // PAIR_ATOMS, s % PAIR_ATOMS * ORB
        for m in range(ORB // 4):
            x = [
                dense[(4 * m + i) * ORB : (4 * m + i + 1) * ORB, sp * 128 : sp * 128 + 128].astype(BF)
                for i in range(4)
            ]
            for half in range(2):
                if half == 0:
                    u = [jnp.where(low, x[i], pltpu.roll(x[i + 2], 64, 1)) for i in range(2)]
                else:
                    u = [jnp.where(low, pltpu.roll(x[i], 64, 1), x[i + 2]) for i in range(2)]
                both = (
                    jnp.where(even, u[0], pltpu.roll(u[1], ATOM_Q, 1)),
                    jnp.where(even, pltpu.roll(u[0], 128 - ATOM_Q, 1), u[1]),
                )
                rows = slice(at_row + half * ORB, at_row + (half + 1) * ORB)
                for n, value in enumerate(both):
                    lo = n * HALF + m * 128
                    if base is not None:
                        value = value + base[pair, rows, lo : lo + 128]
                    band[pair, rows, lo : lo + 128] = value


def column_of(atom, offset):
    target = TILE_ATOMS * (jnp.floor(atom * (1.0 / TILE_ATOMS)) - BAND) + offset
    base = BAND * TILE_ATOMS - PAIR_ATOMS * jnp.floor(atom * (1.0 / PAIR_ATOMS))
    outside = jnp.where(target < 0.0, target + (base + ATOM_Q), target + base)
    return jnp.where((target >= 0.0) & (target < float(ATOM_Q)), target, outside)


def own_kernel(feat, src, dst, cell, cell_bias, w_in, w_out, _, band, w_in_t, bias_t, w_out_t, blk, bias8, rows):
    nfeat, width = w_in.shape
    nblk = w_out.shape[1]
    eye = (iota((width, width), 0) == iota((width, width), 1)).astype(BF)
    w_in_t[...] = nt_dot(eye, w_in[...]).astype(BF)
    bias8[...] = jnp.zeros(bias8.shape, F32)
    bias8[0:3, :] = cell_bias[...].astype(F32)
    bias_t[...] = nt_dot(eye, bias8[...].astype(BF)).astype(BF)
    row, col = iota((nblk, nblk), 0), iota((nblk, nblk), 1)
    swap = (col == (row % ORB) * ORB + row // ORB).astype(BF)
    w_out_t[...] = nt_dot(swap, w_out[...]).astype(BF)
    own = feat.shape[0]
    ids = edge_ids(src[...], dst[...], cell[...])
    atom = row_of(ids[0])
    rows[0:1, :] = atom
    rows[1:2, :] = column_of(atom, row_of(ids[1]))
    blk[...] = pair_blocks(feat[...], row_of(ids[2]), w_in_t, bias_t, w_out_t)
    for first in range(0, ATOM_Q, GROUP):
        start = jnp.sum((ids[0] < float(first)).astype(F32)).astype(jnp.int32)
        at = pl.multiple_of(jnp.minimum(start // 128 * 128, own - GROUP_SPAN), 128)
        span = pl.ds(at, GROUP_SPAN)
        put_dense(band, dense_of(blk[:, span], rows[0:1, span], rows[1:2, span], first), first)


def spill_kernel(own_band, blue, red, w_in_t, bias_t, w_out_t, band, blk, spill):
    even = device_side() == 0
    nfeat = spill.shape[1]
    rows = spill.shape[0] // 2
    left, right = [jnp.where(even, x, y) for x, y in ((blue[...], red[...]), (red[...], blue[...]))]
    spill[0:64, :] = jnp.zeros((64, nfeat), BF)
    spill[64 : rows + SPILL, :] = jnp.concatenate([left[0:SPILL], right[0:SPILL]], axis=0)
    spill[rows + SPILL :, :] = jnp.zeros((64, nfeat), BF)
    ids = []
    for msg in (left, right):
        block = msg[SPILL : SPILL + ID_ROWS, 0:128].astype(F32)
        ids.append([row_of(block[3 * k : 3 * k + 3]) for k in range(3)])
    atoms = [x[0] for x in ids]
    cols = [column_of(x[0], x[1]) for x in ids]
    mine = [(a >= 0.0) & (a < float(ATOM_Q)) for a in atoms]
    highest = jnp.max(jnp.where(mine[0], atoms[0], -1.0)).astype(jnp.int32)
    lowest = jnp.min(jnp.where(mine[1], atoms[1], float(ATOM_Q))).astype(jnp.int32)
    cells = jnp.concatenate([x[2] for x in ids], axis=1)
    blk[...] = pair_blocks(spill[...], cells, w_in_t, bias_t, w_out_t)
    spans = [slice(0, rows), slice(rows, 2 * rows)]
    ngroup = ATOM_Q // GROUP
    for g in range(ngroup):
        first = g * GROUP
        sides = [m for m in range(2) if (g < NEAR, g >= ngroup - NEAR)[m]]
        if sides:
            (m,) = sides
            put_dense(band, dense_of(blk[:, spans[m]], atoms[m], cols[m], first), first, own_band)
        else:
            pair, at = first // PAIR_ATOMS, first % PAIR_ATOMS * ORB
            band[pair, at : at + GROUP * ORB, :] = own_band[pair, at : at + GROUP * ORB, :]
    for m, far in ((0, range(NEAR, ngroup)), (1, range(ngroup - NEAR))):
        for g in far:
            first = g * GROUP

            @pl.when(highest >= first if m == 0 else lowest < first + GROUP)
            def _(m=m, first=first):
                put_dense(band, dense_of(blk[:, spans[m]], atoms[m], cols[m], first), first, band)


def own_part(band, field):
    pieces = [field[pl.ds(q, ATOM_Q, stride=ORB), :].astype(BF) for q in range(ORB)]
    rhs = jnp.concatenate(pieces, axis=0)
    return [jnp.dot(band[k, :, :HALF], rhs, preferred_element_type=F32) for k in range(band.shape[0])]


def halo_part(band, blue, red, wide):
    even = device_side() == 0
    wide[0:HALO, :] = jnp.where(even, blue[...], red[...]).astype(F32)
    wide[HALO : 2 * HALO, :] = jnp.where(even, red[...], blue[...]).astype(F32)
    atoms = BAND * TILE_ATOMS
    pieces = [[], []]
    for q in range(ORB):
        left = wide[pl.ds(q, atoms, stride=ORB), :]
        right = wide[pl.ds(HALO + q, atoms, stride=ORB), :]
        pieces[0].append(jnp.concatenate([left, right[:TILE_ATOMS]], axis=0).astype(BF))
        pieces[1].append(jnp.concatenate([left[atoms - TILE_ATOMS :], right], axis=0).astype(BF))
    return [
        jnp.dot(band[k, :, HALF:], jnp.concatenate(pieces[k], axis=0), preferred_element_type=F32)
        for k in range(band.shape[0])
    ]


def put_sends(value_ref, to_blue, to_red):
    side = device_side()
    inner = value_ref.shape[0] - HALO
    off = pl.multiple_of(side * inner, 128)
    to_blue[...] = value_ref[pl.ds(off, HALO), :].astype(BF)
    to_red[...] = value_ref[pl.ds(pl.multiple_of(inner - off, 128), HALO), :].astype(BF)


def spans_of(band):
    height = band.shape[1]
    return [slice(k * height, (k + 1) * height) for k in range(band.shape[0])]


def first_kernel(band, t0, blue, red, t1, to_blue, to_red, wide):
    inner, outer = own_part(band, t0), halo_part(band, blue, red, wide)
    for k, span in enumerate(spans_of(band)):
        t1[span, :] = inner[k] + outer[k]
    put_sends(t1, to_blue, to_red)


def inner_kernel(band, before, now, part):
    inner = own_part(band, now)
    for k, span in enumerate(spans_of(band)):
        part[span, :] = 2.0 * inner[k] - before[span, :]


def outer_kernel(band, part, blue, red, after, to_blue, to_red, wide):
    outer = halo_part(band, blue, red, wide)
    for k, span in enumerate(spans_of(band)):
        after[span, :] = 2.0 * outer[k] + part[span, :]
    put_sends(after, to_blue, to_red)


def mix_kernel(coef, band, t0, t1, t2, t3, base, final):
    inner = own_part(band, t3)
    for k, span in enumerate(spans_of(band)):
        total = coef[0] * t0[span, :] + coef[1] * t1[span, :] + (coef[2] - coef[4]) * t2[span, :]
        total = total + coef[3] * t3[span, :] + 2.0 * coef[4] * inner[k]
        base[:, span] = total.T
    final[...] = jnp.full(final.shape, 2.0 * coef[4], F32)


def last_kernel(final, band, base, blue, red, p0, p1, p2, p3, wide, out):
    member = lax.axis_index("edges")
    outer = halo_part(band, blue, red, wide)
    for k, span in enumerate(spans_of(band)):
        out[:, span] = base[:, span] + (final[0:1, :] * outer[k]).T
    for k, piece in enumerate((p0, p1, p2, p3)):
        high = piece.shape[0]
        piece[...] = out[pl.ds(pl.multiple_of((member ^ k) * high, high), high), :].astype(BF)


def join_kernel(p0, p1, p2, p3, out):
    member = lax.axis_index("edges")
    for k, piece in enumerate((p0, p1, p2, p3)):
        width = piece.shape[1]
        at = pl.multiple_of((member ^ k) * width, width)
        out[:, pl.ds(at, width)] = piece[...].astype(F32)


VMEM = pl.BlockSpec(memory_space=pltpu.VMEM)
SMEM = pl.BlockSpec(memory_space=pltpu.SMEM)
IN_HBM = pl.BlockSpec(memory_space=pltpu.HBM)
FULL, PART = 60 * 1024 * 1024, 32 * 1024 * 1024


def shape(dims, dtype):
    return jax.ShapeDtypeStruct(dims, dtype)


def call(kernel, name, outs, scratch, *args, smem=(), in_hbm=(), out_hbm=(), alias=None, limit=PART, micros=1):
    spaces = [SMEM if k in smem else IN_HBM if k in in_hbm else VMEM for k in range(len(args))]
    return pl.pallas_call(
        kernel,
        name=name,
        out_shape=outs,
        in_specs=spaces,
        out_specs=tuple(IN_HBM if k in out_hbm else VMEM for k in range(len(outs))),
        scratch_shapes=scratch,
        input_output_aliases=alias or {},
        cost_estimate=pl.CostEstimate(flops=micros * 10**9, bytes_accessed=0, transcendentals=0),
        compiler_params=pltpu.CompilerParams(vmem_limit_bytes=limit),
    )(*args)


def per_device(features, edge_src, edge_dst, edge_cell, cell_bias, w_in, w_out, vectors, cheb_coef):
    axes = ("rows", "edges")
    nedge = lax.axis_size("edges")
    ndev = lax.axis_size("rows") * nedge
    red_pairs = [(i, i ^ 1) for i in range(ndev)]
    blue_pairs = [(i, (i + 1) % ndev if i % 2 else (i - 1) % ndev) for i in range(ndev)]
    nown, nfeat = features.shape
    high, ncol = vectors.shape
    nrow = ncol // nedge

    def swap(first, last):
        return (
            lax.ppermute(first, axes, blue_pairs),
            lax.ppermute(last, axes, red_pairs),
        )

    def exchange(pieces):
        return [pieces[0]] + [
            lax.ppermute(pieces[k], "edges", [(i, i ^ k) for i in range(nedge)]) for k in (3, 2, 1)
        ][::-1]

    msg = shape((SPILL + ID_ROWS, nfeat), BF)
    piece = shape((high, nrow), BF)
    lines = (nown // 128, 128)
    edges = [x.reshape(lines) for x in (edge_src, edge_dst, edge_cell)]
    own_piece, near, far, blue_msg, red_msg = call(
        prep_kernel,
        "prep",
        (piece, piece, shape((2, high, nrow), BF), msg, msg),
        [pltpu.VMEM((nedge, high, nrow), F32)]
        + [pltpu.VMEM(lines, jnp.int32)] * 3
        + [pltpu.SemaphoreType.DMA((9,))],
        vectors,
        features,
        *edges,
        in_hbm=range(5),
        limit=FULL,
    )
    far = lax.ppermute(far, "edges", [(i, i ^ 2) for i in range(nedge)])
    blue_msg, red_msg = swap(blue_msg, red_msg)
    near = lax.ppermute(near, "edges", [(i, i ^ 1) for i in range(nedge)])
    (onward,) = call(relay_kernel, "relay", (piece,), [], far, micros=0)
    onward = lax.ppermute(onward, "edges", [(i, i ^ 1) for i in range(nedge)])
    pieces = [own_piece, near, far, onward]
    full, part = shape((nrow, VEC), F32), shape((HALO, VEC), BF)
    t0, to_blue, to_red, token = call(
        field_kernel, "field", (full, part, part, shape((8, VEC), F32)), [pltpu.VMEM((VEC, nrow), F32)], *pieces
    )
    blue, red = swap(to_blue, to_red)

    band_shape = shape((ATOM_Q // PAIR_ATOMS, PAIR_ATOMS * ORB, WIN_ATOMS * ORB), BF)
    width = w_in.shape[1]
    band, *weights = call(
        own_kernel,
        "own",
        (band_shape, shape((width, nfeat), BF), shape((width, 8), BF), shape((ORB * ORB, HID), BF)),
        [pltpu.VMEM((ORB * ORB, nown), BF), pltpu.VMEM((8, width), F32), pltpu.VMEM((8, nown), F32)],
        features,
        *edges,
        cell_bias,
        w_in,
        w_out,
        token,
        micros=0,
    )
    spill_len = 2 * (SPILL + 64)
    (band,) = call(
        spill_kernel,
        "spill",
        (band_shape,),
        [pltpu.VMEM((ORB * ORB, spill_len), BF), pltpu.VMEM((spill_len, nfeat), BF)],
        band,
        blue_msg,
        red_msg,
        *weights,
        alias={0: 0},
        micros=3,
    )

    wide = pltpu.VMEM((2 * HALO, VEC), F32)
    t1, to_blue, to_red = call(first_kernel, "first", (full, part, part), [wide], band, t0, blue, red)
    fields = [t0, t1]
    for _ in range(2, STEPS):
        blue, red = swap(to_blue, to_red)
        (inner,) = call(inner_kernel, "inner", (full,), [], band, fields[-2], fields[-1])
        following, to_blue, to_red = call(
            outer_kernel, "outer", (full, part, part), [wide], band, inner, blue, red
        )
        fields.append(following)
    blue, red = swap(to_blue, to_red)
    base, final = call(
        mix_kernel,
        "mix",
        (shape((VEC, nrow), F32), shape((8, VEC), F32)),
        [],
        cheb_coef,
        band,
        *fields,
        smem=(0,),
    )
    pieces = call(
        last_kernel,
        "last",
        (piece,) * 4,
        [wide, pltpu.VMEM((VEC, nrow), F32)],
        final,
        band,
        base,
        blue,
        red,
    )
    (result,) = call(join_kernel, "join", (shape((high, ncol), F32),), [], *exchange(pieces))
    return result


def solution(mesh):
    placed = (
        P(("rows", "edges"), None),
        P(("rows", "edges")),
        P(("rows", "edges")),
        P(("rows", "edges")),
        P(),
        P(),
        P(),
        P("edges", "rows"),
        P(),
    )
    return jax.shard_map(
        per_device, mesh=mesh, in_specs=placed, out_specs=P("edges", "rows"), check_vma=False
    )
```

```python
import functools

import jax
import jax.numpy as jnp
from jax import lax
from jax.experimental import pallas as pl
from jax.experimental.pallas import tpu as pltpu
from jax.sharding import PartitionSpec as P

ORB = 16
TILE_ATOMS = 8
BAND = 3
HID = 256
VEC = 128
STEPS = 4
ATOM_Q = 32
SPILL = 320
ID_ROWS = 16
PAIR_ATOMS = 2 * TILE_ATOMS
WIN_ATOMS = (2 * BAND + 2) * TILE_ATOMS
HALO = BAND * TILE_ATOMS * ORB
GROUP = 4
GROUP_SPAN = 384
HALF = ATOM_Q * ORB
NEAR = 3
BF = jnp.bfloat16
F32 = jnp.float32
NT = (((1,), (1,)), ((), ()))


def nt_dot(a, b):
    return lax.dot_general(a, b, NT, preferred_element_type=F32)


def iota(shape, dim):
    return lax.broadcasted_iota(jnp.int32, shape, dim)


def device_side():
    return (lax.axis_index("rows") * lax.axis_size("edges") + lax.axis_index("edges")) % 2


def edge_ids(src, dst, cell):
    ndev = lax.axis_size("rows") * lax.axis_size("edges")
    quarter = lax.axis_index("rows") * lax.axis_size("edges") + lax.axis_index("edges")
    natom = ATOM_Q * ndev
    ntiles = natom // TILE_ATOMS
    rel = src - quarter * ATOM_Q
    rel = jnp.where(rel > natom // 2, rel - natom, jnp.where(rel < -(natom // 2), rel + natom, rel))
    shift = (dst >> 3) - (src >> 3) + BAND
    shift = jnp.where(shift < 0, shift + ntiles, jnp.where(shift >= ntiles, shift - ntiles, shift))
    return [x.astype(F32) for x in (rel, shift * TILE_ATOMS + (dst & 7), cell)]


def prep_kernel(
    vec_hbm, feat, src_hbm, dst_hbm, cell_hbm, p0, p1, p2, p3, blue, red, vectors, src, dst, cell, sems
):
    member, side = lax.axis_index("edges"), device_side()
    pieces = (p0, p1, p2, p3)
    loads = []
    for k, piece in enumerate(pieces):
        width = piece.shape[1]
        at = pl.multiple_of((member ^ k) * width, width)
        loads.append(pltpu.make_async_copy(vec_hbm.at[:, pl.ds(at, width)], vectors.at[k], sems.at[k]))
    high = feat.shape[0] - SPILL
    off = pl.multiple_of(side * high, 64)
    copies = [
        pltpu.make_async_copy(feat.at[pl.ds(off, SPILL)], blue.at[pl.ds(0, SPILL)], sems.at[4]),
        pltpu.make_async_copy(
            feat.at[pl.ds(pl.multiple_of(high - off, 64), SPILL)], red.at[pl.ds(0, SPILL)], sems.at[5]
        ),
    ]
    lists = [
        pltpu.make_async_copy(x, y, sems.at[6 + n])
        for n, (x, y) in enumerate(((src_hbm, src), (dst_hbm, dst), (cell_hbm, cell)))
    ]
    for copy in lists + loads + copies:
        copy.start()
    for copy in lists:
        copy.wait()
    three = edge_ids(src[...], dst[...], cell[...])
    lane, line = iota((3, 128), 1), iota((3, 128), 0)
    nrow = src.shape[0]
    starts = [x[0:3] for x in three]
    ends = [x[nrow - 3 : nrow] for x in three]
    starts[0] = jnp.where((line == 2) & (lane >= 64), -64.0, starts[0] + ATOM_Q)
    ends[0] = jnp.where((line == 0) & (lane < 64), -64.0, ends[0] - ATOM_Q)
    pad = jnp.zeros((ID_ROWS - 9, 128), F32)
    low_ids = jnp.concatenate(starts + [pad], axis=0)
    high_ids = jnp.concatenate(ends + [pad], axis=0)
    none = jnp.zeros((ID_ROWS, 128), BF)
    for msg, ids_of in (
        (blue, jnp.where(side == 0, low_ids, high_ids)),
        (red, jnp.where(side == 0, high_ids, low_ids)),
    ):
        msg[SPILL : SPILL + ID_ROWS, 0:128] = ids_of.astype(BF)
        msg[SPILL : SPILL + ID_ROWS, 128:256] = none
    for k, piece in enumerate(pieces):
        loads[k].wait()
        piece[...] = vectors[k].astype(BF)
    for copy in copies:
        copy.wait()


def pass_kernel(x, y):
    y[...] = x[...]


def field_kernel(p0, p1, p2, p3, t0, to_blue, to_red, token, field):
    member = lax.axis_index("edges")
    for k, piece in enumerate((p0, p1, p2, p3)):
        high = piece.shape[0]
        field[pl.ds(pl.multiple_of((member ^ k) * high, high), high), :] = piece[...].astype(F32)
    t0[...] = field[...].T
    token[...] = jnp.zeros(token.shape, F32)
    put_sends(t0, to_blue, to_red)


def pair_blocks(x, cell, w_in_t, bias_t, w_out_t):
    bias = [bias_t[:, k : k + 1].astype(F32) for k in range(3)]
    pre = nt_dot(w_in_t[...], x)
    pre = pre + jnp.where(cell == 1.0, bias[1], jnp.where(cell == 2.0, bias[2], bias[0]))
    gate, up = pre[:HID], pre[HID:]
    hidden = (gate * (0.5 + 0.5 * jnp.tanh(0.5 * gate)) * up).astype(BF)
    return jnp.dot(w_out_t[...], hidden, preferred_element_type=F32).astype(BF)


def row_of(x):
    return jnp.concatenate([x[k : k + 1] for k in range(x.shape[0])], axis=1)


def dense_of(blocks, atom, target, first):
    span = atom.shape[1]
    column = (iota((WIN_ATOMS, span), 0).astype(F32) == target).astype(BF)
    onehot = [
        jnp.broadcast_to((atom == float(s)).astype(F32), (WIN_ATOMS, span)).astype(BF) * column
        for s in range(first, first + GROUP)
    ]
    return nt_dot(blocks, jnp.concatenate(onehot, axis=0))


def put_dense(band, dense, first, base=None):
    lane = iota((ORB, 128), 1)
    low, even = lane < 64, lane % 64 < ATOM_Q
    for sp in range(GROUP // 2):
        s = first + 2 * sp
        pair, at_row = s // PAIR_ATOMS, s % PAIR_ATOMS * ORB
        for m in range(ORB // 4):
            x = [
                dense[(4 * m + i) * ORB : (4 * m + i + 1) * ORB, sp * 128 : sp * 128 + 128].astype(BF)
                for i in range(4)
            ]
            for half in range(2):
                if half == 0:
                    u = [jnp.where(low, x[i], pltpu.roll(x[i + 2], 64, 1)) for i in range(2)]
                else:
                    u = [jnp.where(low, pltpu.roll(x[i], 64, 1), x[i + 2]) for i in range(2)]
                both = (
                    jnp.where(even, u[0], pltpu.roll(u[1], ATOM_Q, 1)),
                    jnp.where(even, pltpu.roll(u[0], 128 - ATOM_Q, 1), u[1]),
                )
                rows = slice(at_row + half * ORB, at_row + (half + 1) * ORB)
                for n, value in enumerate(both):
                    lo = n * HALF + m * 128
                    if base is not None:
                        value = value + base[pair, rows, lo : lo + 128]
                    band[pair, rows, lo : lo + 128] = value


def column_of(atom, offset):
    target = TILE_ATOMS * (jnp.floor(atom * (1.0 / TILE_ATOMS)) - BAND) + offset
    base = BAND * TILE_ATOMS - PAIR_ATOMS * jnp.floor(atom * (1.0 / PAIR_ATOMS))
    outside = jnp.where(target < 0.0, target + (base + ATOM_Q), target + base)
    return jnp.where((target >= 0.0) & (target < float(ATOM_Q)), target, outside)


def own_kernel(feat, src, dst, cell, cell_bias, w_in, w_out, _, band, w_in_t, bias_t, w_out_t, blk, bias8, rows):
    nfeat, width = w_in.shape
    nblk = w_out.shape[1]
    eye = (iota((width, width), 0) == iota((width, width), 1)).astype(BF)
    w_in_t[...] = nt_dot(eye, w_in[...]).astype(BF)
    bias8[...] = jnp.zeros(bias8.shape, F32)
    bias8[0:3, :] = cell_bias[...].astype(F32)
    bias_t[...] = nt_dot(eye, bias8[...].astype(BF)).astype(BF)
    row, col = iota((nblk, nblk), 0), iota((nblk, nblk), 1)
    swap = (col == (row % ORB) * ORB + row // ORB).astype(BF)
    w_out_t[...] = nt_dot(swap, w_out[...]).astype(BF)
    own = feat.shape[0]
    ids = edge_ids(src[...], dst[...], cell[...])
    atom = row_of(ids[0])
    rows[0:1, :] = atom
    rows[1:2, :] = column_of(atom, row_of(ids[1]))
    blk[...] = pair_blocks(feat[...], row_of(ids[2]), w_in_t, bias_t, w_out_t)
    for first in range(0, ATOM_Q, GROUP):
        start = jnp.sum((ids[0] < float(first)).astype(F32)).astype(jnp.int32)
        at = pl.multiple_of(jnp.minimum(start // 128 * 128, own - GROUP_SPAN), 128)
        span = pl.ds(at, GROUP_SPAN)
        put_dense(band, dense_of(blk[:, span], rows[0:1, span], rows[1:2, span], first), first)


def spill_kernel(own_band, blue, red, w_in_t, bias_t, w_out_t, band, blk, spill):
    even = device_side() == 0
    nfeat = spill.shape[1]
    rows = spill.shape[0] // 2
    left, right = [jnp.where(even, x, y) for x, y in ((blue[...], red[...]), (red[...], blue[...]))]
    spill[0:64, :] = jnp.zeros((64, nfeat), BF)
    spill[64 : rows + SPILL, :] = jnp.concatenate([left[0:SPILL], right[0:SPILL]], axis=0)
    spill[rows + SPILL :, :] = jnp.zeros((64, nfeat), BF)
    ids = []
    for msg in (left, right):
        block = msg[SPILL : SPILL + ID_ROWS, 0:128].astype(F32)
        ids.append([row_of(block[3 * k : 3 * k + 3]) for k in range(3)])
    atoms = [x[0] for x in ids]
    cols = [column_of(x[0], x[1]) for x in ids]
    mine = [(a >= 0.0) & (a < float(ATOM_Q)) for a in atoms]
    highest = jnp.max(jnp.where(mine[0], atoms[0], -1.0)).astype(jnp.int32)
    lowest = jnp.min(jnp.where(mine[1], atoms[1], float(ATOM_Q))).astype(jnp.int32)
    cells = jnp.concatenate([x[2] for x in ids], axis=1)
    blk[...] = pair_blocks(spill[...], cells, w_in_t, bias_t, w_out_t)
    spans = [slice(0, rows), slice(rows, 2 * rows)]
    ngroup = ATOM_Q // GROUP
    for g in range(ngroup):
        first = g * GROUP
        sides = [m for m in range(2) if (g < NEAR, g >= ngroup - NEAR)[m]]
        if sides:
            (m,) = sides
            put_dense(band, dense_of(blk[:, spans[m]], atoms[m], cols[m], first), first, own_band)
        else:
            pair, at = first // PAIR_ATOMS, first % PAIR_ATOMS * ORB
            band[pair, at : at + GROUP * ORB, :] = own_band[pair, at : at + GROUP * ORB, :]
    for m, far in ((0, range(NEAR, ngroup)), (1, range(ngroup - NEAR))):
        for g in far:
            first = g * GROUP

            @pl.when(highest >= first if m == 0 else lowest < first + GROUP)
            def _(m=m, first=first):
                put_dense(band, dense_of(blk[:, spans[m]], atoms[m], cols[m], first), first, band)


def own_part(band, field):
    pieces = [field[pl.ds(q, ATOM_Q, stride=ORB), :].astype(BF) for q in range(ORB)]
    rhs = jnp.concatenate(pieces, axis=0)
    return [jnp.dot(band[k, :, :HALF], rhs, preferred_element_type=F32) for k in range(band.shape[0])]


def halo_part(band, blue, red, wide):
    even = device_side() == 0
    wide[0:HALO, :] = jnp.where(even, blue[...], red[...]).astype(F32)
    wide[HALO : 2 * HALO, :] = jnp.where(even, red[...], blue[...]).astype(F32)
    atoms = BAND * TILE_ATOMS
    pieces = [[], []]
    for q in range(ORB):
        left = wide[pl.ds(q, atoms, stride=ORB), :]
        right = wide[pl.ds(HALO + q, atoms, stride=ORB), :]
        pieces[0].append(jnp.concatenate([left, right[:TILE_ATOMS]], axis=0).astype(BF))
        pieces[1].append(jnp.concatenate([left[atoms - TILE_ATOMS :], right], axis=0).astype(BF))
    return [
        jnp.dot(band[k, :, HALF:], jnp.concatenate(pieces[k], axis=0), preferred_element_type=F32)
        for k in range(band.shape[0])
    ]


def put_sends(value_ref, to_blue, to_red):
    side = device_side()
    inner = value_ref.shape[0] - HALO
    off = pl.multiple_of(side * inner, 128)
    to_blue[...] = value_ref[pl.ds(off, HALO), :].astype(BF)
    to_red[...] = value_ref[pl.ds(pl.multiple_of(inner - off, 128), HALO), :].astype(BF)


def spans_of(band):
    height = band.shape[1]
    return [slice(k * height, (k + 1) * height) for k in range(band.shape[0])]


def first_kernel(band, t0, blue, red, t1, to_blue, to_red, wide):
    inner, outer = own_part(band, t0), halo_part(band, blue, red, wide)
    for k, span in enumerate(spans_of(band)):
        t1[span, :] = inner[k] + outer[k]
    put_sends(t1, to_blue, to_red)


def inner_kernel(band, before, now, part):
    inner = own_part(band, now)
    for k, span in enumerate(spans_of(band)):
        part[span, :] = 2.0 * inner[k] - before[span, :]


def outer_kernel(band, part, blue, red, after, to_blue, to_red, wide):
    outer = halo_part(band, blue, red, wide)
    for k, span in enumerate(spans_of(band)):
        after[span, :] = 2.0 * outer[k] + part[span, :]
    put_sends(after, to_blue, to_red)


def mix_kernel(coef, band, t0, t1, t2, t3, base, final):
    inner = own_part(band, t3)
    for k, span in enumerate(spans_of(band)):
        total = coef[0] * t0[span, :] + coef[1] * t1[span, :] + (coef[2] - coef[4]) * t2[span, :]
        total = total + coef[3] * t3[span, :] + 2.0 * coef[4] * inner[k]
        base[:, span] = total.T
    final[...] = jnp.full(final.shape, 2.0 * coef[4], F32)


def last_kernel(final, band, base, blue, red, p0, p1, p2, p3, wide, out):
    member = lax.axis_index("edges")
    outer = halo_part(band, blue, red, wide)
    for k, span in enumerate(spans_of(band)):
        out[:, span] = base[:, span] + (final[0:1, :] * outer[k]).T
    for k, piece in enumerate((p0, p1, p2, p3)):
        high = piece.shape[0]
        piece[...] = out[pl.ds(pl.multiple_of((member ^ k) * high, high), high), :].astype(BF)


def join_kernel(p0, p1, p2, p3, out):
    member = lax.axis_index("edges")
    for k, piece in enumerate((p0, p1, p2, p3)):
        width = piece.shape[1]
        at = pl.multiple_of((member ^ k) * width, width)
        out[:, pl.ds(at, width)] = piece[...].astype(F32)


VMEM = pl.BlockSpec(memory_space=pltpu.VMEM)
SMEM = pl.BlockSpec(memory_space=pltpu.SMEM)
IN_HBM = pl.BlockSpec(memory_space=pltpu.HBM)
FULL, PART = 60 * 1024 * 1024, 32 * 1024 * 1024


def shape(dims, dtype):
    return jax.ShapeDtypeStruct(dims, dtype)


def call(kernel, name, outs, scratch, *args, smem=(), in_hbm=(), out_hbm=(), alias=None, limit=PART, micros=1):
    spaces = [SMEM if k in smem else IN_HBM if k in in_hbm else VMEM for k in range(len(args))]
    return pl.pallas_call(
        kernel,
        name=name,
        out_shape=outs,
        in_specs=spaces,
        out_specs=tuple(IN_HBM if k in out_hbm else VMEM for k in range(len(outs))),
        scratch_shapes=scratch,
        input_output_aliases=alias or {},
        cost_estimate=pl.CostEstimate(flops=micros * 10**9, bytes_accessed=0, transcendentals=0),
        compiler_params=pltpu.CompilerParams(vmem_limit_bytes=limit),
    )(*args)


def per_device(features, edge_src, edge_dst, edge_cell, cell_bias, w_in, w_out, vectors, cheb_coef):
    axes = ("rows", "edges")
    nedge = lax.axis_size("edges")
    ndev = lax.axis_size("rows") * nedge
    red_pairs = [(i, i ^ 1) for i in range(ndev)]
    blue_pairs = [(i, (i + 1) % ndev if i % 2 else (i - 1) % ndev) for i in range(ndev)]
    nown, nfeat = features.shape
    high, ncol = vectors.shape
    nrow = ncol // nedge

    def swap(first, last):
        return (
            lax.ppermute(first, axes, blue_pairs),
            lax.ppermute(last, axes, red_pairs),
        )

    def exchange(pieces):
        return [pieces[0]] + [
            lax.ppermute(pieces[k], "edges", [(i, i ^ k) for i in range(nedge)]) for k in (1, 2, 3)
        ]

    msg = shape((SPILL + ID_ROWS, nfeat), BF)
    piece = shape((high, nrow), BF)
    lines = (nown // 128, 128)
    edges = [x.reshape(lines) for x in (edge_src, edge_dst, edge_cell)]
    *pieces, blue_msg, red_msg = call(
        prep_kernel,
        "prep",
        (piece,) * 4 + (msg, msg),
        [pltpu.VMEM((nedge, high, nrow), F32)]
        + [pltpu.VMEM(lines, jnp.int32)] * 3
        + [pltpu.SemaphoreType.DMA((9,))],
        vectors,
        features,
        *edges,
        in_hbm=range(5),
        limit=FULL,
    )
    pieces = exchange(pieces)
    blue_msg, red_msg = swap(blue_msg, red_msg)
    pieces[3:4] = call(pass_kernel, "pass", (piece,), [], pieces[3], micros=0)
    full, part = shape((nrow, VEC), F32), shape((HALO, VEC), BF)
    t0, to_blue, to_red, token = call(
        field_kernel, "field", (full, part, part, shape((8, VEC), F32)), [pltpu.VMEM((VEC, nrow), F32)], *pieces
    )
    blue, red = swap(to_blue, to_red)

    band_shape = shape((ATOM_Q // PAIR_ATOMS, PAIR_ATOMS * ORB, WIN_ATOMS * ORB), BF)
    width = w_in.shape[1]
    band, *weights = call(
        own_kernel,
        "own",
        (band_shape, shape((width, nfeat), BF), shape((width, 8), BF), shape((ORB * ORB, HID), BF)),
        [pltpu.VMEM((ORB * ORB, nown), BF), pltpu.VMEM((8, width), F32), pltpu.VMEM((8, nown), F32)],
        features,
        *edges,
        cell_bias,
        w_in,
        w_out,
        token,
        micros=4,
    )
    spill_len = 2 * (SPILL + 64)
    (band,) = call(
        spill_kernel,
        "spill",
        (band_shape,),
        [pltpu.VMEM((ORB * ORB, spill_len), BF), pltpu.VMEM((spill_len, nfeat), BF)],
        band,
        blue_msg,
        red_msg,
        *weights,
        alias={0: 0},
        micros=0,
    )

    wide = pltpu.VMEM((2 * HALO, VEC), F32)
    t1, to_blue, to_red = call(first_kernel, "first", (full, part, part), [wide], band, t0, blue, red)
    fields = [t0, t1]
    for _ in range(2, STEPS):
        blue, red = swap(to_blue, to_red)
        (inner,) = call(inner_kernel, "inner", (full,), [], band, fields[-2], fields[-1])
        following, to_blue, to_red = call(
            outer_kernel, "outer", (full, part, part), [wide], band, inner, blue, red
        )
        fields.append(following)
    blue, red = swap(to_blue, to_red)
    base, final = call(
        mix_kernel,
        "mix",
        (shape((VEC, nrow), F32), shape((8, VEC), F32)),
        [],
        cheb_coef,
        band,
        *fields,
        smem=(0,),
    )
    pieces = call(
        last_kernel,
        "last",
        (piece,) * 4,
        [wide, pltpu.VMEM((VEC, nrow), F32)],
        final,
        band,
        base,
        blue,
        red,
    )
    (result,) = call(join_kernel, "join", (shape((high, ncol), F32),), [], *exchange(pieces))
    return result


def solution(mesh):
    placed = (
        P(("rows", "edges"), None),
        P(("rows", "edges")),
        P(("rows", "edges")),
        P(("rows", "edges")),
        P(),
        P(),
        P(),
        P("edges", "rows"),
        P(),
    )
    return jax.shard_map(
        per_device, mesh=mesh, in_specs=placed, out_specs=P("edges", "rows"), check_vma=False
    )
```

```python
import functools

import jax
import jax.numpy as jnp
from jax import lax
from jax.experimental import pallas as pl
from jax.experimental.pallas import tpu as pltpu
from jax.sharding import PartitionSpec as P

ORB = 16
TILE_ATOMS = 8
BAND = 3
HID = 256
VEC = 128
STEPS = 4
ATOM_Q = 32
SPILL = 320
ID_ROWS = 16
PAIR_ATOMS = 2 * TILE_ATOMS
WIN_ATOMS = (2 * BAND + 2) * TILE_ATOMS
HALO = BAND * TILE_ATOMS * ORB
GROUP = 4
GROUP_SPAN = 384
HALF = ATOM_Q * ORB
NEAR = 3
BF = jnp.bfloat16
F32 = jnp.float32
NT = (((1,), (1,)), ((), ()))


def nt_dot(a, b):
    return lax.dot_general(a, b, NT, preferred_element_type=F32)


def iota(shape, dim):
    return lax.broadcasted_iota(jnp.int32, shape, dim)


def device_side():
    return (lax.axis_index("rows") * lax.axis_size("edges") + lax.axis_index("edges")) % 2


def edge_ids(src, dst, cell):
    ndev = lax.axis_size("rows") * lax.axis_size("edges")
    quarter = lax.axis_index("rows") * lax.axis_size("edges") + lax.axis_index("edges")
    natom = ATOM_Q * ndev
    ntiles = natom // TILE_ATOMS
    rel = src - quarter * ATOM_Q
    rel = jnp.where(rel > natom // 2, rel - natom, jnp.where(rel < -(natom // 2), rel + natom, rel))
    shift = (dst >> 3) - (src >> 3) + BAND
    shift = jnp.where(shift < 0, shift + ntiles, jnp.where(shift >= ntiles, shift - ntiles, shift))
    return [x.astype(F32) for x in (rel, shift * TILE_ATOMS + (dst & 7), cell)]


def prep_kernel(
    vec_hbm, feat, src_hbm, dst_hbm, cell_hbm, p0, p2, p3, blue, red, vectors, src, dst, cell, sems
):
    member, side = lax.axis_index("edges"), device_side()
    pieces = (p0, None, p2, p3)
    loads = []
    high_rows, width = p0.shape
    for k in range(4):
        at = pl.multiple_of((member ^ k) * width, width)
        loads.append(pltpu.make_async_copy(vec_hbm.at[:, pl.ds(at, width)], vectors.at[k], sems.at[k]))
    high = feat.shape[0] - SPILL
    off = pl.multiple_of(side * high, 64)
    copies = [
        pltpu.make_async_copy(feat.at[pl.ds(off, SPILL)], blue.at[pl.ds(0, SPILL)], sems.at[4]),
        pltpu.make_async_copy(
            feat.at[pl.ds(pl.multiple_of(high - off, 64), SPILL)], red.at[pl.ds(0, SPILL)], sems.at[5]
        ),
    ]
    lists = [
        pltpu.make_async_copy(x, y, sems.at[6 + n])
        for n, (x, y) in enumerate(((src_hbm, src), (dst_hbm, dst), (cell_hbm, cell)))
    ]
    for copy in lists + loads + copies:
        copy.start()
    for copy in lists:
        copy.wait()
    three = edge_ids(src[...], dst[...], cell[...])
    lane, line = iota((3, 128), 1), iota((3, 128), 0)
    nrow = src.shape[0]
    starts = [x[0:3] for x in three]
    ends = [x[nrow - 3 : nrow] for x in three]
    starts[0] = jnp.where((line == 2) & (lane >= 64), -64.0, starts[0] + ATOM_Q)
    ends[0] = jnp.where((line == 0) & (lane < 64), -64.0, ends[0] - ATOM_Q)
    pad = jnp.zeros((ID_ROWS - 9, 128), F32)
    low_ids = jnp.concatenate(starts + [pad], axis=0)
    high_ids = jnp.concatenate(ends + [pad], axis=0)
    none = jnp.zeros((ID_ROWS, 128), BF)
    for msg, ids_of in (
        (blue, jnp.where(side == 0, low_ids, high_ids)),
        (red, jnp.where(side == 0, high_ids, low_ids)),
    ):
        msg[SPILL : SPILL + ID_ROWS, 0:128] = ids_of.astype(BF)
        msg[SPILL : SPILL + ID_ROWS, 128:256] = none
    for k, piece in enumerate(pieces):
        loads[k].wait()
        if k == 1:
            for n in range(width // red.shape[1]):
                at = SPILL + ID_ROWS + n * high_rows
                red[at : at + high_rows, :] = vectors[k, :, n * red.shape[1] : (n + 1) * red.shape[1]].astype(BF)
        else:
            piece[...] = vectors[k].astype(BF)
    for copy in copies:
        copy.wait()


def pass_kernel(x, y):
    y[...] = x[...]


def field_kernel(p0, near, p2, p3, t0, to_blue, to_red, token, field):
    member = lax.axis_index("edges")
    high = p0.shape[0]
    for k, piece in ((0, p0), (2, p2), (3, p3)):
        field[pl.ds(pl.multiple_of((member ^ k) * high, high), high), :] = piece[...].astype(F32)
    rows = pl.ds(pl.multiple_of((member ^ 1) * high, high), high)
    width = near.shape[1]
    for n in range(field.shape[1] // width):
        at = SPILL + ID_ROWS + n * high
        field[rows, n * width : (n + 1) * width] = near[at : at + high, :].astype(F32)
    t0[...] = field[...].T
    token[...] = jnp.zeros(token.shape, F32)
    put_sends(t0, to_blue, to_red)


def pair_blocks(x, cell, w_in_t, bias_t, w_out_t):
    bias = [bias_t[:, k : k + 1].astype(F32) for k in range(3)]
    pre = nt_dot(w_in_t[...], x)
    pre = pre + jnp.where(cell == 1.0, bias[1], jnp.where(cell == 2.0, bias[2], bias[0]))
    gate, up = pre[:HID], pre[HID:]
    hidden = (gate * (0.5 + 0.5 * jnp.tanh(0.5 * gate)) * up).astype(BF)
    return jnp.dot(w_out_t[...], hidden, preferred_element_type=F32).astype(BF)


def row_of(x):
    return jnp.concatenate([x[k : k + 1] for k in range(x.shape[0])], axis=1)


def dense_of(blocks, atom, target, first):
    span = atom.shape[1]
    column = (iota((WIN_ATOMS, span), 0).astype(F32) == target).astype(BF)
    onehot = [
        jnp.broadcast_to((atom == float(s)).astype(F32), (WIN_ATOMS, span)).astype(BF) * column
        for s in range(first, first + GROUP)
    ]
    return nt_dot(blocks, jnp.concatenate(onehot, axis=0))


def put_dense(band, dense, first, base=None):
    lane = iota((ORB, 128), 1)
    low, even = lane < 64, lane % 64 < ATOM_Q
    for sp in range(GROUP // 2):
        s = first + 2 * sp
        pair, at_row = s // PAIR_ATOMS, s % PAIR_ATOMS * ORB
        for m in range(ORB // 4):
            x = [
                dense[(4 * m + i) * ORB : (4 * m + i + 1) * ORB, sp * 128 : sp * 128 + 128].astype(BF)
                for i in range(4)
            ]
            for half in range(2):
                if half == 0:
                    u = [jnp.where(low, x[i], pltpu.roll(x[i + 2], 64, 1)) for i in range(2)]
                else:
                    u = [jnp.where(low, pltpu.roll(x[i], 64, 1), x[i + 2]) for i in range(2)]
                both = (
                    jnp.where(even, u[0], pltpu.roll(u[1], ATOM_Q, 1)),
                    jnp.where(even, pltpu.roll(u[0], 128 - ATOM_Q, 1), u[1]),
                )
                rows = slice(at_row + half * ORB, at_row + (half + 1) * ORB)
                for n, value in enumerate(both):
                    lo = n * HALF + m * 128
                    if base is not None:
                        value = value + base[pair, rows, lo : lo + 128]
                    band[pair, rows, lo : lo + 128] = value


def column_of(atom, offset):
    target = TILE_ATOMS * (jnp.floor(atom * (1.0 / TILE_ATOMS)) - BAND) + offset
    base = BAND * TILE_ATOMS - PAIR_ATOMS * jnp.floor(atom * (1.0 / PAIR_ATOMS))
    outside = jnp.where(target < 0.0, target + (base + ATOM_Q), target + base)
    return jnp.where((target >= 0.0) & (target < float(ATOM_Q)), target, outside)


def own_kernel(feat, src, dst, cell, cell_bias, w_in, w_out, _, band, w_in_t, bias_t, w_out_t, blk, bias8, rows):
    nfeat, width = w_in.shape
    nblk = w_out.shape[1]
    eye = (iota((width, width), 0) == iota((width, width), 1)).astype(BF)
    w_in_t[...] = nt_dot(eye, w_in[...]).astype(BF)
    bias8[...] = jnp.zeros(bias8.shape, F32)
    bias8[0:3, :] = cell_bias[...].astype(F32)
    bias_t[...] = nt_dot(eye, bias8[...].astype(BF)).astype(BF)
    row, col = iota((nblk, nblk), 0), iota((nblk, nblk), 1)
    swap = (col == (row % ORB) * ORB + row // ORB).astype(BF)
    w_out_t[...] = nt_dot(swap, w_out[...]).astype(BF)
    own = feat.shape[0]
    ids = edge_ids(src[...], dst[...], cell[...])
    atom = row_of(ids[0])
    rows[0:1, :] = atom
    rows[1:2, :] = column_of(atom, row_of(ids[1]))
    blk[...] = pair_blocks(feat[...], row_of(ids[2]), w_in_t, bias_t, w_out_t)
    for first in range(0, ATOM_Q, GROUP):
        start = jnp.sum((ids[0] < float(first)).astype(F32)).astype(jnp.int32)
        at = pl.multiple_of(jnp.minimum(start // 128 * 128, own - GROUP_SPAN), 128)
        span = pl.ds(at, GROUP_SPAN)
        put_dense(band, dense_of(blk[:, span], rows[0:1, span], rows[1:2, span], first), first)


def spill_kernel(own_band, blue, red, w_in_t, bias_t, w_out_t, band, blk, spill):
    even = device_side() == 0
    nfeat = spill.shape[1]
    rows = spill.shape[0] // 2
    near = red[0 : SPILL + ID_ROWS, :]
    left, right = [jnp.where(even, x, y) for x, y in ((blue[...], near), (near, blue[...]))]
    spill[0:64, :] = jnp.zeros((64, nfeat), BF)
    spill[64 : rows + SPILL, :] = jnp.concatenate([left[0:SPILL], right[0:SPILL]], axis=0)
    spill[rows + SPILL :, :] = jnp.zeros((64, nfeat), BF)
    ids = []
    for msg in (left, right):
        block = msg[SPILL : SPILL + ID_ROWS, 0:128].astype(F32)
        ids.append([row_of(block[3 * k : 3 * k + 3]) for k in range(3)])
    atoms = [x[0] for x in ids]
    cols = [column_of(x[0], x[1]) for x in ids]
    mine = [(a >= 0.0) & (a < float(ATOM_Q)) for a in atoms]
    highest = jnp.max(jnp.where(mine[0], atoms[0], -1.0)).astype(jnp.int32)
    lowest = jnp.min(jnp.where(mine[1], atoms[1], float(ATOM_Q))).astype(jnp.int32)
    cells = jnp.concatenate([x[2] for x in ids], axis=1)
    blk[...] = pair_blocks(spill[...], cells, w_in_t, bias_t, w_out_t)
    spans = [slice(0, rows), slice(rows, 2 * rows)]
    ngroup = ATOM_Q // GROUP
    for g in range(ngroup):
        first = g * GROUP
        sides = [m for m in range(2) if (g < NEAR, g >= ngroup - NEAR)[m]]
        if sides:
            (m,) = sides
            put_dense(band, dense_of(blk[:, spans[m]], atoms[m], cols[m], first), first, own_band)
        else:
            pair, at = first // PAIR_ATOMS, first % PAIR_ATOMS * ORB
            band[pair, at : at + GROUP * ORB, :] = own_band[pair, at : at + GROUP * ORB, :]
    for m, far in ((0, range(NEAR, ngroup)), (1, range(ngroup - NEAR))):
        for g in far:
            first = g * GROUP

            @pl.when(highest >= first if m == 0 else lowest < first + GROUP)
            def _(m=m, first=first):
                put_dense(band, dense_of(blk[:, spans[m]], atoms[m], cols[m], first), first, band)


def own_part(band, field):
    pieces = [field[pl.ds(q, ATOM_Q, stride=ORB), :].astype(BF) for q in range(ORB)]
    rhs = jnp.concatenate(pieces, axis=0)
    return [jnp.dot(band[k, :, :HALF], rhs, preferred_element_type=F32) for k in range(band.shape[0])]


def halo_part(band, blue, red, wide):
    even = device_side() == 0
    wide[0:HALO, :] = jnp.where(even, blue[...], red[...]).astype(F32)
    wide[HALO : 2 * HALO, :] = jnp.where(even, red[...], blue[...]).astype(F32)
    atoms = BAND * TILE_ATOMS
    pieces = [[], []]
    for q in range(ORB):
        left = wide[pl.ds(q, atoms, stride=ORB), :]
        right = wide[pl.ds(HALO + q, atoms, stride=ORB), :]
        pieces[0].append(jnp.concatenate([left, right[:TILE_ATOMS]], axis=0).astype(BF))
        pieces[1].append(jnp.concatenate([left[atoms - TILE_ATOMS :], right], axis=0).astype(BF))
    return [
        jnp.dot(band[k, :, HALF:], jnp.concatenate(pieces[k], axis=0), preferred_element_type=F32)
        for k in range(band.shape[0])
    ]


def put_sends(value_ref, to_blue, to_red):
    side = device_side()
    inner = value_ref.shape[0] - HALO
    off = pl.multiple_of(side * inner, 128)
    to_blue[...] = value_ref[pl.ds(off, HALO), :].astype(BF)
    to_red[...] = value_ref[pl.ds(pl.multiple_of(inner - off, 128), HALO), :].astype(BF)


def spans_of(band):
    height = band.shape[1]
    return [slice(k * height, (k + 1) * height) for k in range(band.shape[0])]


def first_kernel(band, t0, blue, red, t1, to_blue, to_red, wide):
    inner, outer = own_part(band, t0), halo_part(band, blue, red, wide)
    for k, span in enumerate(spans_of(band)):
        t1[span, :] = inner[k] + outer[k]
    put_sends(t1, to_blue, to_red)


def inner_kernel(band, before, now, part):
    inner = own_part(band, now)
    for k, span in enumerate(spans_of(band)):
        part[span, :] = 2.0 * inner[k] - before[span, :]


def outer_kernel(band, part, blue, red, after, to_blue, to_red, wide):
    outer = halo_part(band, blue, red, wide)
    for k, span in enumerate(spans_of(band)):
        after[span, :] = 2.0 * outer[k] + part[span, :]
    put_sends(after, to_blue, to_red)


def mix_kernel(coef, band, t0, t1, t2, t3, base, final):
    inner = own_part(band, t3)
    for k, span in enumerate(spans_of(band)):
        total = coef[0] * t0[span, :] + coef[1] * t1[span, :] + (coef[2] - coef[4]) * t2[span, :]
        total = total + coef[3] * t3[span, :] + 2.0 * coef[4] * inner[k]
        base[:, span] = total.T
    final[...] = jnp.full(final.shape, 2.0 * coef[4], F32)


def last_kernel(final, band, base, blue, red, p0, p1, p2, p3, wide, out):
    member = lax.axis_index("edges")
    outer = halo_part(band, blue, red, wide)
    for k, span in enumerate(spans_of(band)):
        out[:, span] = base[:, span] + (final[0:1, :] * outer[k]).T
    for k, piece in enumerate((p0, p1, p2, p3)):
        high = piece.shape[0]
        piece[...] = out[pl.ds(pl.multiple_of((member ^ k) * high, high), high), :].astype(BF)


def join_kernel(p0, p1, p2, p3, out):
    member = lax.axis_index("edges")
    for k, piece in enumerate((p0, p1, p2, p3)):
        width = piece.shape[1]
        at = pl.multiple_of((member ^ k) * width, width)
        out[:, pl.ds(at, width)] = piece[...].astype(F32)


VMEM = pl.BlockSpec(memory_space=pltpu.VMEM)
SMEM = pl.BlockSpec(memory_space=pltpu.SMEM)
IN_HBM = pl.BlockSpec(memory_space=pltpu.HBM)
FULL, PART = 60 * 1024 * 1024, 32 * 1024 * 1024


def shape(dims, dtype):
    return jax.ShapeDtypeStruct(dims, dtype)


def call(kernel, name, outs, scratch, *args, smem=(), in_hbm=(), out_hbm=(), alias=None, limit=PART, micros=1):
    spaces = [SMEM if k in smem else IN_HBM if k in in_hbm else VMEM for k in range(len(args))]
    return pl.pallas_call(
        kernel,
        name=name,
        out_shape=outs,
        in_specs=spaces,
        out_specs=tuple(IN_HBM if k in out_hbm else VMEM for k in range(len(outs))),
        scratch_shapes=scratch,
        input_output_aliases=alias or {},
        cost_estimate=pl.CostEstimate(flops=micros * 10**9, bytes_accessed=0, transcendentals=0),
        compiler_params=pltpu.CompilerParams(vmem_limit_bytes=limit),
    )(*args)


def per_device(features, edge_src, edge_dst, edge_cell, cell_bias, w_in, w_out, vectors, cheb_coef):
    axes = ("rows", "edges")
    nedge = lax.axis_size("edges")
    ndev = lax.axis_size("rows") * nedge
    red_pairs = [(i, i ^ 1) for i in range(ndev)]
    blue_pairs = [(i, (i + 1) % ndev if i % 2 else (i - 1) % ndev) for i in range(ndev)]
    nown, nfeat = features.shape
    high, ncol = vectors.shape
    nrow = ncol // nedge

    def swap(first, last):
        return (
            lax.ppermute(first, axes, blue_pairs),
            lax.ppermute(last, axes, red_pairs),
        )

    def exchange(pieces):
        return [pieces[0]] + [
            lax.ppermute(pieces[k], "edges", [(i, i ^ k) for i in range(nedge)]) for k in (1, 2, 3)
        ]

    msg = shape((SPILL + ID_ROWS, nfeat), BF)
    piece = shape((high, nrow), BF)
    lines = (nown // 128, 128)
    edges = [x.reshape(lines) for x in (edge_src, edge_dst, edge_cell)]
    near_msg = shape((SPILL + ID_ROWS + high * nrow // nfeat, nfeat), BF)
    own_piece, straight, across, blue_msg, near = call(
        prep_kernel,
        "prep",
        (piece,) * 3 + (msg, near_msg),
        [pltpu.VMEM((nedge, high, nrow), F32)]
        + [pltpu.VMEM(lines, jnp.int32)] * 3
        + [pltpu.SemaphoreType.DMA((9,))],
        vectors,
        features,
        *edges,
        in_hbm=range(5),
        limit=FULL,
    )
    across = lax.ppermute(across, "edges", [(i, i ^ 3) for i in range(nedge)])
    straight = lax.ppermute(straight, "edges", [(i, i ^ 2) for i in range(nedge)])
    near = lax.ppermute(near, axes, red_pairs)
    blue_msg = lax.ppermute(blue_msg, axes, blue_pairs)
    (across,) = call(pass_kernel, "pass", (piece,), [], across, micros=0)
    pieces = [own_piece, near, straight, across]
    full, part = shape((nrow, VEC), F32), shape((HALO, VEC), BF)
    t0, to_blue, to_red, token = call(
        field_kernel, "field", (full, part, part, shape((8, VEC), F32)), [pltpu.VMEM((VEC, nrow), F32)], *pieces
    )
    blue, red = swap(to_blue, to_red)

    band_shape = shape((ATOM_Q // PAIR_ATOMS, PAIR_ATOMS * ORB, WIN_ATOMS * ORB), BF)
    width = w_in.shape[1]
    band, *weights = call(
        own_kernel,
        "own",
        (band_shape, shape((width, nfeat), BF), shape((width, 8), BF), shape((ORB * ORB, HID), BF)),
        [pltpu.VMEM((ORB * ORB, nown), BF), pltpu.VMEM((8, width), F32), pltpu.VMEM((8, nown), F32)],
        features,
        *edges,
        cell_bias,
        w_in,
        w_out,
        token,
        micros=4,
    )
    spill_len = 2 * (SPILL + 64)
    (band,) = call(
        spill_kernel,
        "spill",
        (band_shape,),
        [pltpu.VMEM((ORB * ORB, spill_len), BF), pltpu.VMEM((spill_len, nfeat), BF)],
        band,
        blue_msg,
        near,
        *weights,
        alias={0: 0},
        micros=0,
    )

    wide = pltpu.VMEM((2 * HALO, VEC), F32)
    t1, to_blue, to_red = call(first_kernel, "first", (full, part, part), [wide], band, t0, blue, red)
    fields = [t0, t1]
    for _ in range(2, STEPS):
        blue, red = swap(to_blue, to_red)
        (inner,) = call(inner_kernel, "inner", (full,), [], band, fields[-2], fields[-1])
        following, to_blue, to_red = call(
            outer_kernel, "outer", (full, part, part), [wide], band, inner, blue, red
        )
        fields.append(following)
    blue, red = swap(to_blue, to_red)
    base, final = call(
        mix_kernel,
        "mix",
        (shape((VEC, nrow), F32), shape((8, VEC), F32)),
        [],
        cheb_coef,
        band,
        *fields,
        smem=(0,),
    )
    pieces = call(
        last_kernel,
        "last",
        (piece,) * 4,
        [wide, pltpu.VMEM((VEC, nrow), F32)],
        final,
        band,
        base,
        blue,
        red,
    )
    (result,) = call(join_kernel, "join", (shape((high, ncol), F32),), [], *exchange(pieces))
    return result


def solution(mesh):
    placed = (
        P(("rows", "edges"), None),
        P(("rows", "edges")),
        P(("rows", "edges")),
        P(("rows", "edges")),
        P(),
        P(),
        P(),
        P("edges", "rows"),
        P(),
    )
    return jax.shard_map(
        per_device, mesh=mesh, in_specs=placed, out_specs=P("edges", "rows"), check_vma=False
    )
```

```python
import functools

import jax
import jax.numpy as jnp
from jax import lax
from jax.experimental import pallas as pl
from jax.experimental.pallas import tpu as pltpu
from jax.sharding import PartitionSpec as P

ORB = 16
TILE_ATOMS = 8
BAND = 3
HID = 256
VEC = 128
STEPS = 4
ATOM_Q = 32
SPILL = 320
ID_ROWS = 16
PAIR_ATOMS = 2 * TILE_ATOMS
WIN_ATOMS = (2 * BAND + 2) * TILE_ATOMS
HALO = BAND * TILE_ATOMS * ORB
GROUP = 4
GROUP_SPAN = 384
HALF = ATOM_Q * ORB
NEAR = 3
BF = jnp.bfloat16
F32 = jnp.float32
NT = (((1,), (1,)), ((), ()))


def nt_dot(a, b):
    return lax.dot_general(a, b, NT, preferred_element_type=F32)


def iota(shape, dim):
    return lax.broadcasted_iota(jnp.int32, shape, dim)


def device_side():
    return (lax.axis_index("rows") * lax.axis_size("edges") + lax.axis_index("edges")) % 2


def edge_ids(src, dst, cell):
    ndev = lax.axis_size("rows") * lax.axis_size("edges")
    quarter = lax.axis_index("rows") * lax.axis_size("edges") + lax.axis_index("edges")
    natom = ATOM_Q * ndev
    ntiles = natom // TILE_ATOMS
    rel = src - quarter * ATOM_Q
    rel = jnp.where(rel > natom // 2, rel - natom, jnp.where(rel < -(natom // 2), rel + natom, rel))
    shift = (dst >> 3) - (src >> 3) + BAND
    shift = jnp.where(shift < 0, shift + ntiles, jnp.where(shift >= ntiles, shift - ntiles, shift))
    return [x.astype(F32) for x in (rel, shift * TILE_ATOMS + (dst & 7), cell)]


def prep_kernel(
    vec_hbm, feat, src_hbm, dst_hbm, cell_hbm, p0, p2, p3, blue, red, vectors, src, dst, cell, sems
):
    member, side = lax.axis_index("edges"), device_side()
    pieces = (p0, None, p2, p3)
    loads = []
    high_rows, width = p0.shape
    for k in range(4):
        at = pl.multiple_of((member ^ k) * width, width)
        loads.append(pltpu.make_async_copy(vec_hbm.at[:, pl.ds(at, width)], vectors.at[k], sems.at[k]))
    high = feat.shape[0] - SPILL
    off = pl.multiple_of(side * high, 64)
    copies = [
        pltpu.make_async_copy(feat.at[pl.ds(off, SPILL)], blue.at[pl.ds(0, SPILL)], sems.at[4]),
        pltpu.make_async_copy(
            feat.at[pl.ds(pl.multiple_of(high - off, 64), SPILL)], red.at[pl.ds(0, SPILL)], sems.at[5]
        ),
    ]
    lists = [
        pltpu.make_async_copy(x, y, sems.at[6 + n])
        for n, (x, y) in enumerate(((src_hbm, src), (dst_hbm, dst), (cell_hbm, cell)))
    ]
    for copy in lists + loads + copies:
        copy.start()
    for copy in lists:
        copy.wait()
    three = edge_ids(src[...], dst[...], cell[...])
    lane, line = iota((3, 128), 1), iota((3, 128), 0)
    nrow = src.shape[0]
    starts = [x[0:3] for x in three]
    ends = [x[nrow - 3 : nrow] for x in three]
    starts[0] = jnp.where((line == 2) & (lane >= 64), -64.0, starts[0] + ATOM_Q)
    ends[0] = jnp.where((line == 0) & (lane < 64), -64.0, ends[0] - ATOM_Q)
    pad = jnp.zeros((ID_ROWS - 9, 128), F32)
    low_ids = jnp.concatenate(starts + [pad], axis=0)
    high_ids = jnp.concatenate(ends + [pad], axis=0)
    none = jnp.zeros((ID_ROWS, 128), BF)
    for msg, ids_of in (
        (blue, jnp.where(side == 0, low_ids, high_ids)),
        (red, jnp.where(side == 0, high_ids, low_ids)),
    ):
        msg[SPILL : SPILL + ID_ROWS, 0:128] = ids_of.astype(BF)
        msg[SPILL : SPILL + ID_ROWS, 128:256] = none
    for k, piece in enumerate(pieces):
        loads[k].wait()
        if k == 1:
            for n in range(width // red.shape[1]):
                at = SPILL + ID_ROWS + n * high_rows
                red[at : at + high_rows, :] = vectors[k, :, n * red.shape[1] : (n + 1) * red.shape[1]].astype(BF)
        else:
            piece[...] = vectors[k].astype(BF)
    for copy in copies:
        copy.wait()


def pass_kernel(x, y):
    y[...] = x[...]


def field_kernel(p0, near, p2, p3, t0, to_blue, to_red, token, field):
    member = lax.axis_index("edges")
    high = p0.shape[0]
    for k, piece in ((0, p0), (2, p2), (3, p3)):
        field[pl.ds(pl.multiple_of((member ^ k) * high, high), high), :] = piece[...].astype(F32)
    rows = pl.ds(pl.multiple_of((member ^ 1) * high, high), high)
    width = near.shape[1]
    for n in range(field.shape[1] // width):
        at = SPILL + ID_ROWS + n * high
        field[rows, n * width : (n + 1) * width] = near[at : at + high, :].astype(F32)
    t0[...] = field[...].T
    token[...] = jnp.zeros(token.shape, F32)
    put_sends(t0, to_blue, to_red)


def pair_blocks(x, cell, w_in_t, bias_t, w_out_t):
    bias = [bias_t[:, k : k + 1].astype(F32) for k in range(3)]
    pre = nt_dot(w_in_t[...], x)
    pre = pre + jnp.where(cell == 1.0, bias[1], jnp.where(cell == 2.0, bias[2], bias[0]))
    gate, up = pre[:HID], pre[HID:]
    hidden = (gate * (0.5 + 0.5 * jnp.tanh(0.5 * gate)) * up).astype(BF)
    return jnp.dot(w_out_t[...], hidden, preferred_element_type=F32).astype(BF)


def row_of(x):
    return jnp.concatenate([x[k : k + 1] for k in range(x.shape[0])], axis=1)


def dense_of(blocks, atom, target, first):
    span = atom.shape[1]
    column = (iota((WIN_ATOMS, span), 0).astype(F32) == target).astype(BF)
    onehot = [
        jnp.broadcast_to((atom == as_float(first + s)).astype(F32), (WIN_ATOMS, span)).astype(BF) * column
        for s in range(GROUP)
    ]
    return nt_dot(blocks, jnp.concatenate(onehot, axis=0))


def put_dense(band, dense, first, base=None):
    lane = iota((ORB, 128), 1)
    low, even = lane < 64, lane % 64 < ATOM_Q
    for sp in range(GROUP // 2):
        s = first + 2 * sp
        pair, at_row = s // PAIR_ATOMS, s % PAIR_ATOMS * ORB
        if not isinstance(s, int):
            at_row = pl.multiple_of(at_row, 2 * ORB)
        for m in range(ORB // 4):
            x = [
                dense[(4 * m + i) * ORB : (4 * m + i + 1) * ORB, sp * 128 : sp * 128 + 128].astype(BF)
                for i in range(4)
            ]
            for half in range(2):
                if half == 0:
                    u = [jnp.where(low, x[i], pltpu.roll(x[i + 2], 64, 1)) for i in range(2)]
                else:
                    u = [jnp.where(low, pltpu.roll(x[i], 64, 1), x[i + 2]) for i in range(2)]
                both = (
                    jnp.where(even, u[0], pltpu.roll(u[1], ATOM_Q, 1)),
                    jnp.where(even, pltpu.roll(u[0], 128 - ATOM_Q, 1), u[1]),
                )
                rows = pl.ds(at_row + half * ORB, ORB)
                for n, value in enumerate(both):
                    lo = n * HALF + m * 128
                    if base is not None:
                        value = value + base[pair, rows, lo : lo + 128]
                    band[pair, rows, lo : lo + 128] = value


def column_of(atom, offset):
    target = TILE_ATOMS * (jnp.floor(atom * (1.0 / TILE_ATOMS)) - BAND) + offset
    base = BAND * TILE_ATOMS - PAIR_ATOMS * jnp.floor(atom * (1.0 / PAIR_ATOMS))
    outside = jnp.where(target < 0.0, target + (base + ATOM_Q), target + base)
    return jnp.where((target >= 0.0) & (target < float(ATOM_Q)), target, outside)


def as_float(x):
    return float(x) if isinstance(x, int) else x.astype(F32)


def place(message, is_left, rows):
    nfeat = rows.shape[1]
    gap = rows.shape[0] - SPILL
    rows[0:gap, :] = jnp.zeros((gap, nfeat), BF)
    rows[SPILL : SPILL + gap, :] = jnp.zeros((gap, nfeat), BF)
    rows[pl.ds(pl.multiple_of(jnp.where(is_left, gap, 0), 64), SPILL), :] = message[0:SPILL, :]
    block = message[SPILL : SPILL + ID_ROWS, 0:128].astype(F32)
    return [row_of(block[3 * k : 3 * k + 3]) for k in range(3)]


def add_message(band, blocks, atom, column, is_left):
    mine = (atom >= 0.0) & (atom < float(ATOM_Q))
    highest = jnp.max(jnp.where(mine, atom, -1.0)).astype(jnp.int32)
    lowest = jnp.min(jnp.where(mine, atom, float(ATOM_Q))).astype(jnp.int32)
    for k in range(NEAR):
        first = jnp.where(is_left, k * GROUP, ATOM_Q - (NEAR - k) * GROUP)
        put_dense(band, dense_of(blocks[...], atom, column, first), first, band)
    for k in range(ATOM_Q // GROUP - NEAR):
        first = jnp.where(is_left, (NEAR + k) * GROUP, k * GROUP)

        @pl.when(jnp.where(is_left, highest >= first, lowest < first + GROUP))
        def _(first=first):
            put_dense(band, dense_of(blocks[...], atom, column, first), first, band)


def own_kernel(
    feat, src, dst, cell, near, cell_bias, w_in, w_out, _, band, w_in_t, bias_t, w_out_t, blk, blk2, bias8, rows, more
):
    nfeat, width = w_in.shape
    nblk = w_out.shape[1]
    eye = (iota((width, width), 0) == iota((width, width), 1)).astype(BF)
    w_in_t[...] = nt_dot(eye, w_in[...]).astype(BF)
    bias8[...] = jnp.zeros(bias8.shape, F32)
    bias8[0:3, :] = cell_bias[...].astype(F32)
    bias_t[...] = nt_dot(eye, bias8[...].astype(BF)).astype(BF)
    row, col = iota((nblk, nblk), 0), iota((nblk, nblk), 1)
    swap = (col == (row % ORB) * ORB + row // ORB).astype(BF)
    w_out_t[...] = nt_dot(swap, w_out[...]).astype(BF)
    own = feat.shape[0]
    ids = edge_ids(src[...], dst[...], cell[...])
    atom = row_of(ids[0])
    rows[0:1, :] = atom
    rows[1:2, :] = column_of(atom, row_of(ids[1]))
    is_left = device_side() == 1
    other = place(near, is_left, more)
    blk[...] = pair_blocks(feat[...], row_of(ids[2]), w_in_t, bias_t, w_out_t)
    blk2[...] = pair_blocks(more[...], other[2], w_in_t, bias_t, w_out_t)
    for first in range(0, ATOM_Q, GROUP):
        start = jnp.sum((ids[0] < float(first)).astype(F32)).astype(jnp.int32)
        at = pl.multiple_of(jnp.minimum(start // 128 * 128, own - GROUP_SPAN), 128)
        span = pl.ds(at, GROUP_SPAN)
        put_dense(band, dense_of(blk[:, span], rows[0:1, span], rows[1:2, span], first), first)
    add_message(band, blk2, other[0], column_of(other[0], other[1]), is_left)


def spill_kernel(own_band, blue, w_in_t, bias_t, w_out_t, band, blk, more):
    is_left = device_side() == 0
    ids = place(blue, is_left, more)
    blk[...] = pair_blocks(more[...], ids[2], w_in_t, bias_t, w_out_t)
    band[...] = own_band[...]
    add_message(band, blk, ids[0], column_of(ids[0], ids[1]), is_left)


def own_part(band, field):
    pieces = [field[pl.ds(q, ATOM_Q, stride=ORB), :].astype(BF) for q in range(ORB)]
    rhs = jnp.concatenate(pieces, axis=0)
    return [jnp.dot(band[k, :, :HALF], rhs, preferred_element_type=F32) for k in range(band.shape[0])]


def halo_part(band, blue, red, wide):
    even = device_side() == 0
    wide[0:HALO, :] = jnp.where(even, blue[...], red[...]).astype(F32)
    wide[HALO : 2 * HALO, :] = jnp.where(even, red[...], blue[...]).astype(F32)
    atoms = BAND * TILE_ATOMS
    pieces = [[], []]
    for q in range(ORB):
        left = wide[pl.ds(q, atoms, stride=ORB), :]
        right = wide[pl.ds(HALO + q, atoms, stride=ORB), :]
        pieces[0].append(jnp.concatenate([left, right[:TILE_ATOMS]], axis=0).astype(BF))
        pieces[1].append(jnp.concatenate([left[atoms - TILE_ATOMS :], right], axis=0).astype(BF))
    return [
        jnp.dot(band[k, :, HALF:], jnp.concatenate(pieces[k], axis=0), preferred_element_type=F32)
        for k in range(band.shape[0])
    ]


def put_sends(value_ref, to_blue, to_red):
    side = device_side()
    inner = value_ref.shape[0] - HALO
    off = pl.multiple_of(side * inner, 128)
    to_blue[...] = value_ref[pl.ds(off, HALO), :].astype(BF)
    to_red[...] = value_ref[pl.ds(pl.multiple_of(inner - off, 128), HALO), :].astype(BF)


def spans_of(band):
    height = band.shape[1]
    return [slice(k * height, (k + 1) * height) for k in range(band.shape[0])]


def start_kernel(band, now, part):
    inner = own_part(band, now)
    for k, span in enumerate(spans_of(band)):
        part[span, :] = inner[k]


def inner_kernel(band, before, now, part):
    inner = own_part(band, now)
    for k, span in enumerate(spans_of(band)):
        part[span, :] = 2.0 * inner[k] - before[span, :]


def outer_kernel(scale, band, part, blue, red, after, to_blue, to_red, wide):
    outer = halo_part(band, blue, red, wide)
    for k, span in enumerate(spans_of(band)):
        after[span, :] = scale * outer[k] + part[span, :]
    put_sends(after, to_blue, to_red)


def mix_kernel(coef, band, t0, t1, t2, t3, base, final):
    inner = own_part(band, t3)
    for k, span in enumerate(spans_of(band)):
        total = coef[0] * t0[span, :] + coef[1] * t1[span, :] + (coef[2] - coef[4]) * t2[span, :]
        total = total + coef[3] * t3[span, :] + 2.0 * coef[4] * inner[k]
        base[:, span] = total.T
    final[...] = jnp.full(final.shape, 2.0 * coef[4], F32)


def last_kernel(final, band, base, blue, red, p0, p1, p2, p3, wide, out):
    member = lax.axis_index("edges")
    outer = halo_part(band, blue, red, wide)
    for k, span in enumerate(spans_of(band)):
        out[:, span] = base[:, span] + (final[0:1, :] * outer[k]).T
    for k, piece in enumerate((p0, p1, p2, p3)):
        high = piece.shape[0]
        piece[...] = out[pl.ds(pl.multiple_of((member ^ k) * high, high), high), :].astype(BF)


def join_kernel(p0, p1, p2, p3, out):
    member = lax.axis_index("edges")
    for k, piece in enumerate((p0, p1, p2, p3)):
        width = piece.shape[1]
        at = pl.multiple_of((member ^ k) * width, width)
        out[:, pl.ds(at, width)] = piece[...].astype(F32)


VMEM = pl.BlockSpec(memory_space=pltpu.VMEM)
SMEM = pl.BlockSpec(memory_space=pltpu.SMEM)
IN_HBM = pl.BlockSpec(memory_space=pltpu.HBM)
FULL, PART = 60 * 1024 * 1024, 32 * 1024 * 1024


def shape(dims, dtype):
    return jax.ShapeDtypeStruct(dims, dtype)


def call(kernel, name, outs, scratch, *args, smem=(), in_hbm=(), out_hbm=(), alias=None, limit=PART, micros=1):
    spaces = [SMEM if k in smem else IN_HBM if k in in_hbm else VMEM for k in range(len(args))]
    return pl.pallas_call(
        kernel,
        name=name,
        out_shape=outs,
        in_specs=spaces,
        out_specs=tuple(IN_HBM if k in out_hbm else VMEM for k in range(len(outs))),
        scratch_shapes=scratch,
        input_output_aliases=alias or {},
        cost_estimate=pl.CostEstimate(flops=micros * 10**9, bytes_accessed=0, transcendentals=0),
        compiler_params=pltpu.CompilerParams(vmem_limit_bytes=limit),
    )(*args)


def per_device(features, edge_src, edge_dst, edge_cell, cell_bias, w_in, w_out, vectors, cheb_coef):
    axes = ("rows", "edges")
    nedge = lax.axis_size("edges")
    ndev = lax.axis_size("rows") * nedge
    red_pairs = [(i, i ^ 1) for i in range(ndev)]
    blue_pairs = [(i, (i + 1) % ndev if i % 2 else (i - 1) % ndev) for i in range(ndev)]
    nown, nfeat = features.shape
    high, ncol = vectors.shape
    nrow = ncol // nedge

    def swap(first, last):
        return (
            lax.ppermute(first, axes, blue_pairs),
            lax.ppermute(last, axes, red_pairs),
        )

    def exchange(pieces):
        return [pieces[0]] + [
            lax.ppermute(pieces[k], "edges", [(i, i ^ k) for i in range(nedge)]) for k in (1, 2, 3)
        ]

    msg = shape((SPILL + ID_ROWS, nfeat), BF)
    piece = shape((high, nrow), BF)
    lines = (nown // 128, 128)
    edges = [x.reshape(lines) for x in (edge_src, edge_dst, edge_cell)]
    near_msg = shape((SPILL + ID_ROWS + high * nrow // nfeat, nfeat), BF)
    own_piece, straight, across, blue_msg, near = call(
        prep_kernel,
        "prep",
        (piece,) * 3 + (msg, near_msg),
        [pltpu.VMEM((nedge, high, nrow), F32)]
        + [pltpu.VMEM(lines, jnp.int32)] * 3
        + [pltpu.SemaphoreType.DMA((9,))],
        vectors,
        features,
        *edges,
        in_hbm=range(5),
        limit=FULL,
    )
    across = lax.ppermute(across, "edges", [(i, i ^ 3) for i in range(nedge)])
    straight = lax.ppermute(straight, "edges", [(i, i ^ 2) for i in range(nedge)])
    near = lax.ppermute(near, axes, red_pairs)
    blue_msg = lax.ppermute(blue_msg, axes, blue_pairs)
    (across,) = call(pass_kernel, "pass", (piece,), [], across, micros=0)
    pieces = [own_piece, near, straight, across]
    full, part = shape((nrow, VEC), F32), shape((HALO, VEC), BF)
    t0, to_blue, to_red, token = call(
        field_kernel, "field", (full, part, part, shape((8, VEC), F32)), [pltpu.VMEM((VEC, nrow), F32)], *pieces
    )
    blue, red = swap(to_blue, to_red)

    wide_spill = SPILL + 64
    band_shape = shape((ATOM_Q // PAIR_ATOMS, PAIR_ATOMS * ORB, WIN_ATOMS * ORB), BF)
    width = w_in.shape[1]
    band, *weights = call(
        own_kernel,
        "own",
        (band_shape, shape((width, nfeat), BF), shape((width, 8), BF), shape((ORB * ORB, HID), BF)),
        [
            pltpu.VMEM((ORB * ORB, nown), BF),
            pltpu.VMEM((ORB * ORB, wide_spill), BF),
            pltpu.VMEM((8, width), F32),
            pltpu.VMEM((8, nown), F32),
            pltpu.VMEM((wide_spill, nfeat), BF),
        ],
        features,
        *edges,
        near,
        cell_bias,
        w_in,
        w_out,
        token,
        micros=4,
    )
    (band,) = call(
        spill_kernel,
        "spill",
        (band_shape,),
        [pltpu.VMEM((ORB * ORB, wide_spill), BF), pltpu.VMEM((wide_spill, nfeat), BF)],
        band,
        blue_msg,
        *weights,
        alias={0: 0},
        micros=0,
    )

    wide = pltpu.VMEM((2 * HALO, VEC), F32)
    fields = [t0]
    for step in range(1, STEPS):
        if step > 1:
            blue, red = swap(to_blue, to_red)
        inner, name = (start_kernel, "start") if step == 1 else (inner_kernel, "inner")
        (inner,) = call(inner, name, (full,), [], band, *fields[-2:])
        following, to_blue, to_red = call(
            functools.partial(outer_kernel, 1.0 if step == 1 else 2.0),
            "outer",
            (full, part, part),
            [wide],
            band,
            inner,
            blue,
            red,
        )
        fields.append(following)
    blue, red = swap(to_blue, to_red)
    base, final = call(
        mix_kernel,
        "mix",
        (shape((VEC, nrow), F32), shape((8, VEC), F32)),
        [],
        cheb_coef,
        band,
        *fields,
        smem=(0,),
    )
    pieces = call(
        last_kernel,
        "last",
        (piece,) * 4,
        [wide, pltpu.VMEM((VEC, nrow), F32)],
        final,
        band,
        base,
        blue,
        red,
    )
    (result,) = call(join_kernel, "join", (shape((high, ncol), F32),), [], *exchange(pieces))
    return result


def solution(mesh):
    placed = (
        P(("rows", "edges"), None),
        P(("rows", "edges")),
        P(("rows", "edges")),
        P(("rows", "edges")),
        P(),
        P(),
        P(),
        P("edges", "rows"),
        P(),
    )
    return jax.shard_map(
        per_device, mesh=mesh, in_specs=placed, out_specs=P("edges", "rows"), check_vma=False
    )
```

```python
import functools

import jax
import jax.numpy as jnp
from jax import lax
from jax.experimental import pallas as pl
from jax.experimental.pallas import tpu as pltpu
from jax.sharding import PartitionSpec as P

ORB = 16
TILE_ATOMS = 8
BAND = 3
HID = 256
VEC = 128
STEPS = 4
ATOM_Q = 32
SPILL = 320
ID_ROWS = 16
PAIR_ATOMS = 2 * TILE_ATOMS
WIN_ATOMS = (2 * BAND + 2) * TILE_ATOMS
HALO = BAND * TILE_ATOMS * ORB
GROUP = 4
GROUP_SPAN = 384
HALF = ATOM_Q * ORB
NEAR = 3
BF = jnp.bfloat16
F32 = jnp.float32
NT = (((1,), (1,)), ((), ()))


def nt_dot(a, b):
    return lax.dot_general(a, b, NT, preferred_element_type=F32)


def iota(shape, dim):
    return lax.broadcasted_iota(jnp.int32, shape, dim)


def device_side():
    return (lax.axis_index("rows") * lax.axis_size("edges") + lax.axis_index("edges")) % 2


def edge_ids(src, dst, cell):
    ndev = lax.axis_size("rows") * lax.axis_size("edges")
    quarter = lax.axis_index("rows") * lax.axis_size("edges") + lax.axis_index("edges")
    natom = ATOM_Q * ndev
    ntiles = natom // TILE_ATOMS
    rel = src - quarter * ATOM_Q
    rel = jnp.where(rel > natom // 2, rel - natom, jnp.where(rel < -(natom // 2), rel + natom, rel))
    shift = (dst >> 3) - (src >> 3) + BAND
    shift = jnp.where(shift < 0, shift + ntiles, jnp.where(shift >= ntiles, shift - ntiles, shift))
    return [x.astype(F32) for x in (rel, shift * TILE_ATOMS + (dst & 7), cell)]


def prep_kernel(
    vec_hbm, feat, src_hbm, dst_hbm, cell_hbm, p0, p2, p3, blue, red, vectors, src, dst, cell, sems
):
    member, side = lax.axis_index("edges"), device_side()
    pieces = (p0, None, p2, p3)
    loads = []
    high_rows, width = p0.shape
    for k in range(4):
        at = pl.multiple_of((member ^ k) * width, width)
        loads.append(pltpu.make_async_copy(vec_hbm.at[:, pl.ds(at, width)], vectors.at[k], sems.at[k]))
    high = feat.shape[0] - SPILL
    off = pl.multiple_of(side * high, 64)
    copies = [
        pltpu.make_async_copy(feat.at[pl.ds(off, SPILL)], blue.at[pl.ds(0, SPILL)], sems.at[4]),
        pltpu.make_async_copy(
            feat.at[pl.ds(pl.multiple_of(high - off, 64), SPILL)], red.at[pl.ds(0, SPILL)], sems.at[5]
        ),
    ]
    lists = [
        pltpu.make_async_copy(x, y, sems.at[6 + n])
        for n, (x, y) in enumerate(((src_hbm, src), (dst_hbm, dst), (cell_hbm, cell)))
    ]
    for copy in lists + loads + copies:
        copy.start()
    for copy in lists:
        copy.wait()
    three = edge_ids(src[...], dst[...], cell[...])
    lane, line = iota((3, 128), 1), iota((3, 128), 0)
    nrow = src.shape[0]
    starts = [x[0:3] for x in three]
    ends = [x[nrow - 3 : nrow] for x in three]
    starts[0] = jnp.where((line == 2) & (lane >= 64), -64.0, starts[0] + ATOM_Q)
    ends[0] = jnp.where((line == 0) & (lane < 64), -64.0, ends[0] - ATOM_Q)
    pad = jnp.zeros((ID_ROWS - 9, 128), F32)
    low_ids = jnp.concatenate(starts + [pad], axis=0)
    high_ids = jnp.concatenate(ends + [pad], axis=0)
    none = jnp.zeros((ID_ROWS, 128), BF)
    for msg, ids_of in (
        (blue, jnp.where(side == 0, low_ids, high_ids)),
        (red, jnp.where(side == 0, high_ids, low_ids)),
    ):
        msg[SPILL : SPILL + ID_ROWS, 0:128] = ids_of.astype(BF)
        msg[SPILL : SPILL + ID_ROWS, 128:256] = none
    for k, piece in enumerate(pieces):
        loads[k].wait()
        if k == 1:
            for n in range(width // red.shape[1]):
                at = SPILL + ID_ROWS + n * high_rows
                red[at : at + high_rows, :] = vectors[k, :, n * red.shape[1] : (n + 1) * red.shape[1]].astype(BF)
        else:
            piece[...] = vectors[k].astype(BF)
    for copy in copies:
        copy.wait()


def pass_kernel(x, y):
    y[...] = x[...]


def field_kernel(p0, near, p2, p3, t0, to_blue, to_red, token, field):
    member = lax.axis_index("edges")
    high = p0.shape[0]
    for k, piece in ((0, p0), (2, p2), (3, p3)):
        field[pl.ds(pl.multiple_of((member ^ k) * high, high), high), :] = piece[...].astype(F32)
    rows = pl.ds(pl.multiple_of((member ^ 1) * high, high), high)
    width = near.shape[1]
    for n in range(field.shape[1] // width):
        at = SPILL + ID_ROWS + n * high
        field[rows, n * width : (n + 1) * width] = near[at : at + high, :].astype(F32)
    t0[...] = field[...].T
    token[...] = jnp.zeros(token.shape, F32)
    put_sends(t0, to_blue, to_red)


def pair_blocks(x, cell, w_in_t, bias_t, w_out_t):
    bias = [bias_t[:, k : k + 1].astype(F32) for k in range(3)]
    pre = nt_dot(w_in_t[...], x)
    pre = pre + jnp.where(cell == 1.0, bias[1], jnp.where(cell == 2.0, bias[2], bias[0]))
    gate, up = pre[:HID], pre[HID:]
    hidden = (gate * (0.5 + 0.5 * jnp.tanh(0.5 * gate)) * up).astype(BF)
    return jnp.dot(w_out_t[...], hidden, preferred_element_type=F32).astype(BF)


def row_of(x):
    return jnp.concatenate([x[k : k + 1] for k in range(x.shape[0])], axis=1)


def dense_of(blocks, atom, target, first):
    span = atom.shape[1]
    column = (iota((WIN_ATOMS, span), 0).astype(F32) == target).astype(BF)
    onehot = [
        jnp.broadcast_to((atom == as_float(first + s)).astype(F32), (WIN_ATOMS, span)).astype(BF) * column
        for s in range(GROUP)
    ]
    return nt_dot(blocks, jnp.concatenate(onehot, axis=0))


def put_dense(band, dense, first, base=None):
    lane = iota((ORB, 128), 1)
    low, even = lane < 64, lane % 64 < ATOM_Q
    for sp in range(GROUP // 2):
        s = first + 2 * sp
        pair, at_row = s // PAIR_ATOMS, s % PAIR_ATOMS * ORB
        if not isinstance(s, int):
            at_row = pl.multiple_of(at_row, 2 * ORB)
        for m in range(ORB // 4):
            x = [
                dense[(4 * m + i) * ORB : (4 * m + i + 1) * ORB, sp * 128 : sp * 128 + 128].astype(BF)
                for i in range(4)
            ]
            for half in range(2):
                if half == 0:
                    u = [jnp.where(low, x[i], pltpu.roll(x[i + 2], 64, 1)) for i in range(2)]
                else:
                    u = [jnp.where(low, pltpu.roll(x[i], 64, 1), x[i + 2]) for i in range(2)]
                both = (
                    jnp.where(even, u[0], pltpu.roll(u[1], ATOM_Q, 1)),
                    jnp.where(even, pltpu.roll(u[0], 128 - ATOM_Q, 1), u[1]),
                )
                rows = pl.ds(at_row + half * ORB, ORB)
                for n, value in enumerate(both):
                    lo = n * HALF + m * 128
                    if base is not None:
                        value = value + base[pair, rows, lo : lo + 128]
                    band[pair, rows, lo : lo + 128] = value


def column_of(atom, offset):
    target = TILE_ATOMS * (jnp.floor(atom * (1.0 / TILE_ATOMS)) - BAND) + offset
    base = BAND * TILE_ATOMS - PAIR_ATOMS * jnp.floor(atom * (1.0 / PAIR_ATOMS))
    outside = jnp.where(target < 0.0, target + (base + ATOM_Q), target + base)
    return jnp.where((target >= 0.0) & (target < float(ATOM_Q)), target, outside)


def as_float(x):
    return float(x) if isinstance(x, int) else x.astype(F32)


def place(message, is_left, rows, lists):
    nfeat = rows.shape[1]
    gap = rows.shape[0] - SPILL
    rows[0:gap, :] = jnp.zeros((gap, nfeat), BF)
    rows[SPILL : SPILL + gap, :] = jnp.zeros((gap, nfeat), BF)
    rows[pl.ds(pl.multiple_of(jnp.where(is_left, gap, 0), 64), SPILL), :] = message[0:SPILL, :]
    block = message[SPILL : SPILL + ID_ROWS, 0:128].astype(F32)
    atom, offset, cell = [row_of(block[3 * k : 3 * k + 3]) for k in range(3)]
    lists[0:1, :] = atom
    lists[1:2, :] = column_of(atom, offset)
    return cell


def near_groups(is_left):
    ngroup = ATOM_Q // GROUP
    return range(NEAR) if is_left else range(ngroup - NEAR, ngroup)


def add_far(band, blocks, lists, left):
    atom = lists[0:1, :]
    mine = (atom >= 0.0) & (atom < float(ATOM_Q))
    reach = float(NEAR * GROUP)
    beyond = (left & (atom >= reach)) | (jnp.logical_not(left) & (atom < ATOM_Q - reach))
    any_far = jnp.max(jnp.where(mine & beyond, 1.0, 0.0)) > 0.5
    for is_left in (True, False):

        @pl.when(any_far & (left == is_left))
        def _(is_left=is_left):
            for g in range(ATOM_Q // GROUP):
                if g not in near_groups(is_left):
                    first = g * GROUP
                    dense = dense_of(blocks[...], lists[0:1, :], lists[1:2, :], first)
                    put_dense(band, dense, first, band)


def own_kernel(
    feat, src, dst, cell, near, cell_bias, w_in, w_out, _, band, w_in_t, bias_t, w_out_t, blk, blk2, bias8, rows, more, lists
):
    nfeat, width = w_in.shape
    nblk = w_out.shape[1]
    eye = (iota((width, width), 0) == iota((width, width), 1)).astype(BF)
    w_in_t[...] = nt_dot(eye, w_in[...]).astype(BF)
    bias8[...] = jnp.zeros(bias8.shape, F32)
    bias8[0:3, :] = cell_bias[...].astype(F32)
    bias_t[...] = nt_dot(eye, bias8[...].astype(BF)).astype(BF)
    row, col = iota((nblk, nblk), 0), iota((nblk, nblk), 1)
    swap = (col == (row % ORB) * ORB + row // ORB).astype(BF)
    w_out_t[...] = nt_dot(swap, w_out[...]).astype(BF)
    own = feat.shape[0]
    ids = edge_ids(src[...], dst[...], cell[...])
    atom = row_of(ids[0])
    rows[0:1, :] = atom
    rows[1:2, :] = column_of(atom, row_of(ids[1]))
    is_left = device_side() == 1
    cells = place(near, is_left, more, lists)
    blk[...] = pair_blocks(feat[...], row_of(ids[2]), w_in_t, bias_t, w_out_t)
    blk2[...] = pair_blocks(more[...], cells, w_in_t, bias_t, w_out_t)
    spans = []
    for first in range(0, ATOM_Q, GROUP):
        start = jnp.sum((ids[0] < float(first)).astype(F32)).astype(jnp.int32)
        spans.append(pl.ds(pl.multiple_of(jnp.minimum(start // 128 * 128, own - GROUP_SPAN), 128), GROUP_SPAN))
    for left in (True, False):

        @pl.when(is_left == left)
        def _(left=left):
            for g, span in enumerate(spans):
                first = g * GROUP
                dense = dense_of(blk[:, span], rows[0:1, span], rows[1:2, span], first)
                if g in near_groups(left):
                    dense = dense + dense_of(blk2[...], lists[0:1, :], lists[1:2, :], first)
                put_dense(band, dense, first)

    add_far(band, blk2, lists, is_left)


def spill_kernel(own_band, blue, w_in_t, bias_t, w_out_t, band, blk, more, lists):
    is_left = device_side() == 0
    cells = place(blue, is_left, more, lists)
    blk[...] = pair_blocks(more[...], cells, w_in_t, bias_t, w_out_t)
    for left in (True, False):

        @pl.when(is_left == left)
        def _(left=left):
            for g in range(ATOM_Q // GROUP):
                first = g * GROUP
                if g in near_groups(left):
                    dense = dense_of(blk[...], lists[0:1, :], lists[1:2, :], first)
                    put_dense(band, dense, first, own_band)
                else:
                    pair, at = first // PAIR_ATOMS, first % PAIR_ATOMS * ORB
                    band[pair, at : at + GROUP * ORB, :] = own_band[pair, at : at + GROUP * ORB, :]

    add_far(band, blk, lists, is_left)


def own_part(band, field):
    pieces = [field[pl.ds(q, ATOM_Q, stride=ORB), :].astype(BF) for q in range(ORB)]
    rhs = jnp.concatenate(pieces, axis=0)
    return [jnp.dot(band[k, :, :HALF], rhs, preferred_element_type=F32) for k in range(band.shape[0])]


def halo_part(band, blue, red, wide):
    even = device_side() == 0
    wide[0:HALO, :] = jnp.where(even, blue[...], red[...]).astype(F32)
    wide[HALO : 2 * HALO, :] = jnp.where(even, red[...], blue[...]).astype(F32)
    atoms = BAND * TILE_ATOMS
    pieces = [[], []]
    for q in range(ORB):
        left = wide[pl.ds(q, atoms, stride=ORB), :]
        right = wide[pl.ds(HALO + q, atoms, stride=ORB), :]
        pieces[0].append(jnp.concatenate([left, right[:TILE_ATOMS]], axis=0).astype(BF))
        pieces[1].append(jnp.concatenate([left[atoms - TILE_ATOMS :], right], axis=0).astype(BF))
    return [
        jnp.dot(band[k, :, HALF:], jnp.concatenate(pieces[k], axis=0), preferred_element_type=F32)
        for k in range(band.shape[0])
    ]


def put_sends(value_ref, to_blue, to_red):
    side = device_side()
    inner = value_ref.shape[0] - HALO
    off = pl.multiple_of(side * inner, 128)
    to_blue[...] = value_ref[pl.ds(off, HALO), :].astype(BF)
    to_red[...] = value_ref[pl.ds(pl.multiple_of(inner - off, 128), HALO), :].astype(BF)


def spans_of(band):
    height = band.shape[1]
    return [slice(k * height, (k + 1) * height) for k in range(band.shape[0])]


def start_kernel(band, now, part):
    inner = own_part(band, now)
    for k, span in enumerate(spans_of(band)):
        part[span, :] = inner[k]


def inner_kernel(band, before, now, part):
    inner = own_part(band, now)
    for k, span in enumerate(spans_of(band)):
        part[span, :] = 2.0 * inner[k] - before[span, :]


def outer_kernel(scale, band, part, blue, red, after, to_blue, to_red, wide):
    outer = halo_part(band, blue, red, wide)
    for k, span in enumerate(spans_of(band)):
        after[span, :] = scale * outer[k] + part[span, :]
    put_sends(after, to_blue, to_red)


def mix_kernel(coef, band, t0, t1, t2, t3, base, final):
    inner = own_part(band, t3)
    for k, span in enumerate(spans_of(band)):
        total = coef[0] * t0[span, :] + coef[1] * t1[span, :] + (coef[2] - coef[4]) * t2[span, :]
        total = total + coef[3] * t3[span, :] + 2.0 * coef[4] * inner[k]
        base[:, span] = total.T
    final[...] = jnp.full(final.shape, 2.0 * coef[4], F32)


def last_kernel(final, band, base, blue, red, p0, p1, p2, p3, wide, out):
    member = lax.axis_index("edges")
    outer = halo_part(band, blue, red, wide)
    for k, span in enumerate(spans_of(band)):
        out[:, span] = base[:, span] + (final[0:1, :] * outer[k]).T
    for k, piece in enumerate((p0, p1, p2, p3)):
        high = piece.shape[0]
        piece[...] = out[pl.ds(pl.multiple_of((member ^ k) * high, high), high), :].astype(BF)


def join_kernel(p0, p1, p2, p3, out):
    member = lax.axis_index("edges")
    for k, piece in enumerate((p0, p1, p2, p3)):
        width = piece.shape[1]
        at = pl.multiple_of((member ^ k) * width, width)
        out[:, pl.ds(at, width)] = piece[...].astype(F32)


VMEM = pl.BlockSpec(memory_space=pltpu.VMEM)
SMEM = pl.BlockSpec(memory_space=pltpu.SMEM)
IN_HBM = pl.BlockSpec(memory_space=pltpu.HBM)
FULL, PART = 60 * 1024 * 1024, 32 * 1024 * 1024


def shape(dims, dtype):
    return jax.ShapeDtypeStruct(dims, dtype)


def call(kernel, name, outs, scratch, *args, smem=(), in_hbm=(), out_hbm=(), alias=None, limit=PART, micros=1):
    spaces = [SMEM if k in smem else IN_HBM if k in in_hbm else VMEM for k in range(len(args))]
    return pl.pallas_call(
        kernel,
        name=name,
        out_shape=outs,
        in_specs=spaces,
        out_specs=tuple(IN_HBM if k in out_hbm else VMEM for k in range(len(outs))),
        scratch_shapes=scratch,
        input_output_aliases=alias or {},
        cost_estimate=pl.CostEstimate(flops=micros * 10**9, bytes_accessed=0, transcendentals=0),
        compiler_params=pltpu.CompilerParams(vmem_limit_bytes=limit),
    )(*args)


def per_device(features, edge_src, edge_dst, edge_cell, cell_bias, w_in, w_out, vectors, cheb_coef):
    axes = ("rows", "edges")
    nedge = lax.axis_size("edges")
    ndev = lax.axis_size("rows") * nedge
    red_pairs = [(i, i ^ 1) for i in range(ndev)]
    blue_pairs = [(i, (i + 1) % ndev if i % 2 else (i - 1) % ndev) for i in range(ndev)]
    nown, nfeat = features.shape
    high, ncol = vectors.shape
    nrow = ncol // nedge

    def swap(first, last):
        return (
            lax.ppermute(first, axes, blue_pairs),
            lax.ppermute(last, axes, red_pairs),
        )

    def exchange(pieces):
        return [pieces[0]] + [
            lax.ppermute(pieces[k], "edges", [(i, i ^ k) for i in range(nedge)]) for k in (1, 2, 3)
        ]

    msg = shape((SPILL + ID_ROWS, nfeat), BF)
    piece = shape((high, nrow), BF)
    lines = (nown // 128, 128)
    edges = [x.reshape(lines) for x in (edge_src, edge_dst, edge_cell)]
    near_msg = shape((SPILL + ID_ROWS + high * nrow // nfeat, nfeat), BF)
    own_piece, straight, across, blue_msg, near = call(
        prep_kernel,
        "prep",
        (piece,) * 3 + (msg, near_msg),
        [pltpu.VMEM((nedge, high, nrow), F32)]
        + [pltpu.VMEM(lines, jnp.int32)] * 3
        + [pltpu.SemaphoreType.DMA((9,))],
        vectors,
        features,
        *edges,
        in_hbm=range(5),
        limit=FULL,
    )
    across = lax.ppermute(across, "edges", [(i, i ^ 3) for i in range(nedge)])
    straight = lax.ppermute(straight, "edges", [(i, i ^ 2) for i in range(nedge)])
    near = lax.ppermute(near, axes, red_pairs)
    blue_msg = lax.ppermute(blue_msg, axes, blue_pairs)
    (across,) = call(pass_kernel, "pass", (piece,), [], across, micros=0)
    pieces = [own_piece, near, straight, across]
    full, part = shape((nrow, VEC), F32), shape((HALO, VEC), BF)
    t0, to_blue, to_red, token = call(
        field_kernel, "field", (full, part, part, shape((8, VEC), F32)), [pltpu.VMEM((VEC, nrow), F32)], *pieces
    )
    blue, red = swap(to_blue, to_red)

    wide_spill = SPILL + 64
    band_shape = shape((ATOM_Q // PAIR_ATOMS, PAIR_ATOMS * ORB, WIN_ATOMS * ORB), BF)
    width = w_in.shape[1]
    band, *weights = call(
        own_kernel,
        "own",
        (band_shape, shape((width, nfeat), BF), shape((width, 8), BF), shape((ORB * ORB, HID), BF)),
        [
            pltpu.VMEM((ORB * ORB, nown), BF),
            pltpu.VMEM((ORB * ORB, wide_spill), BF),
            pltpu.VMEM((8, width), F32),
            pltpu.VMEM((8, nown), F32),
            pltpu.VMEM((wide_spill, nfeat), BF),
            pltpu.VMEM((8, wide_spill), F32),
        ],
        features,
        *edges,
        near,
        cell_bias,
        w_in,
        w_out,
        token,
        micros=4,
    )
    (band,) = call(
        spill_kernel,
        "spill",
        (band_shape,),
        [
            pltpu.VMEM((ORB * ORB, wide_spill), BF),
            pltpu.VMEM((wide_spill, nfeat), BF),
            pltpu.VMEM((8, wide_spill), F32),
        ],
        band,
        blue_msg,
        *weights,
        alias={0: 0},
        micros=0,
    )

    wide = pltpu.VMEM((2 * HALO, VEC), F32)
    fields = [t0]
    for step in range(1, STEPS):
        if step > 1:
            blue, red = swap(to_blue, to_red)
        inner, name = (start_kernel, "start") if step == 1 else (inner_kernel, "inner")
        (inner,) = call(inner, name, (full,), [], band, *fields[-2:])
        following, to_blue, to_red = call(
            functools.partial(outer_kernel, 1.0 if step == 1 else 2.0),
            "outer",
            (full, part, part),
            [wide],
            band,
            inner,
            blue,
            red,
        )
        fields.append(following)
    blue, red = swap(to_blue, to_red)
    base, final = call(
        mix_kernel,
        "mix",
        (shape((VEC, nrow), F32), shape((8, VEC), F32)),
        [],
        cheb_coef,
        band,
        *fields,
        smem=(0,),
    )
    pieces = call(
        last_kernel,
        "last",
        (piece,) * 4,
        [wide, pltpu.VMEM((VEC, nrow), F32)],
        final,
        band,
        base,
        blue,
        red,
    )
    (result,) = call(join_kernel, "join", (shape((high, ncol), F32),), [], *exchange(pieces))
    return result


def solution(mesh):
    placed = (
        P(("rows", "edges"), None),
        P(("rows", "edges")),
        P(("rows", "edges")),
        P(("rows", "edges")),
        P(),
        P(),
        P(),
        P("edges", "rows"),
        P(),
    )
    return jax.shard_map(
        per_device, mesh=mesh, in_specs=placed, out_specs=P("edges", "rows"), check_vma=False
    )
```

```python
import functools

import jax
import jax.numpy as jnp
from jax import lax
from jax.experimental import pallas as pl
from jax.experimental.pallas import tpu as pltpu
from jax.sharding import PartitionSpec as P

ORB = 16
TILE_ATOMS = 8
BAND = 3
HID = 256
VEC = 128
STEPS = 4
ATOM_Q = 32
SPILL = 320
ID_ROWS = 16
PAIR_ATOMS = 2 * TILE_ATOMS
WIN_ATOMS = (2 * BAND + 2) * TILE_ATOMS
HALO = BAND * TILE_ATOMS * ORB
GROUP = 4
GROUP_SPAN = 384
HALF = ATOM_Q * ORB
NEAR = 3
BF = jnp.bfloat16
F32 = jnp.float32
NT = (((1,), (1,)), ((), ()))


def nt_dot(a, b):
    return lax.dot_general(a, b, NT, preferred_element_type=F32)


def iota(shape, dim):
    return lax.broadcasted_iota(jnp.int32, shape, dim)


def device_side():
    return (lax.axis_index("rows") * lax.axis_size("edges") + lax.axis_index("edges")) % 2


def edge_ids(src, dst, cell):
    ndev = lax.axis_size("rows") * lax.axis_size("edges")
    quarter = lax.axis_index("rows") * lax.axis_size("edges") + lax.axis_index("edges")
    natom = ATOM_Q * ndev
    ntiles = natom // TILE_ATOMS
    rel = src - quarter * ATOM_Q
    rel = jnp.where(rel > natom // 2, rel - natom, jnp.where(rel < -(natom // 2), rel + natom, rel))
    shift = (dst >> 3) - (src >> 3) + BAND
    shift = jnp.where(shift < 0, shift + ntiles, jnp.where(shift >= ntiles, shift - ntiles, shift))
    return [x.astype(F32) for x in (rel, shift * TILE_ATOMS + (dst & 7), cell)]


def prep_kernel(
    vec_hbm, feat, src_hbm, dst_hbm, cell_hbm, p0, p2, p3, blue, red, vectors, src, dst, cell, sems
):
    member, side = lax.axis_index("edges"), device_side()
    pieces = (p0, None, p2, p3)
    loads = []
    high_rows, width = p0.shape
    for k in range(4):
        at = pl.multiple_of((member ^ k) * width, width)
        loads.append(pltpu.make_async_copy(vec_hbm.at[:, pl.ds(at, width)], vectors.at[k], sems.at[k]))
    high = feat.shape[0] - SPILL
    off = pl.multiple_of(side * high, 64)
    copies = [
        pltpu.make_async_copy(feat.at[pl.ds(off, SPILL)], blue.at[pl.ds(0, SPILL)], sems.at[4]),
        pltpu.make_async_copy(
            feat.at[pl.ds(pl.multiple_of(high - off, 64), SPILL)], red.at[pl.ds(0, SPILL)], sems.at[5]
        ),
    ]
    lists = [
        pltpu.make_async_copy(x, y, sems.at[6 + n])
        for n, (x, y) in enumerate(((src_hbm, src), (dst_hbm, dst), (cell_hbm, cell)))
    ]
    for copy in lists + loads + copies:
        copy.start()
    for copy in lists:
        copy.wait()
    three = edge_ids(src[...], dst[...], cell[...])
    lane, line = iota((3, 128), 1), iota((3, 128), 0)
    nrow = src.shape[0]
    starts = [x[0:3] for x in three]
    ends = [x[nrow - 3 : nrow] for x in three]
    starts[0] = jnp.where((line == 2) & (lane >= 64), -64.0, starts[0] + ATOM_Q)
    ends[0] = jnp.where((line == 0) & (lane < 64), -64.0, ends[0] - ATOM_Q)
    pad = jnp.zeros((ID_ROWS - 9, 128), F32)
    low_ids = jnp.concatenate(starts + [pad], axis=0)
    high_ids = jnp.concatenate(ends + [pad], axis=0)
    none = jnp.zeros((ID_ROWS, 128), BF)
    for msg, ids_of in (
        (blue, jnp.where(side == 0, low_ids, high_ids)),
        (red, jnp.where(side == 0, high_ids, low_ids)),
    ):
        msg[SPILL : SPILL + ID_ROWS, 0:128] = ids_of.astype(BF)
        msg[SPILL : SPILL + ID_ROWS, 128:256] = none
    for k, piece in enumerate(pieces):
        loads[k].wait()
        if k == 1:
            for n in range(width // red.shape[1]):
                at = SPILL + ID_ROWS + n * high_rows
                red[at : at + high_rows, :] = vectors[k, :, n * red.shape[1] : (n + 1) * red.shape[1]].astype(BF)
        else:
            piece[...] = vectors[k].astype(BF)
    for copy in copies:
        copy.wait()


def pass_kernel(x, y):
    y[...] = x[...]


def field_kernel(p0, near, p2, p3, t0, to_blue, to_red, token, field):
    member = lax.axis_index("edges")
    high = p0.shape[0]
    for k, piece in ((0, p0), (2, p2), (3, p3)):
        field[pl.ds(pl.multiple_of((member ^ k) * high, high), high), :] = piece[...].astype(F32)
    rows = pl.ds(pl.multiple_of((member ^ 1) * high, high), high)
    width = near.shape[1]
    for n in range(field.shape[1] // width):
        at = SPILL + ID_ROWS + n * high
        field[rows, n * width : (n + 1) * width] = near[at : at + high, :].astype(F32)
    t0[...] = field[...].T
    token[...] = jnp.zeros(token.shape, F32)
    put_sends(t0, to_blue, to_red)


def pair_blocks(x, cell, w_in_t, bias_t, w_out_t):
    bias = [bias_t[:, k : k + 1].astype(F32) for k in range(3)]
    pre = nt_dot(w_in_t[...], x)
    pre = pre + jnp.where(cell == 1.0, bias[1], jnp.where(cell == 2.0, bias[2], bias[0]))
    gate, up = pre[:HID], pre[HID:]
    hidden = (gate * (0.5 + 0.5 * jnp.tanh(0.5 * gate)) * up).astype(BF)
    return jnp.dot(w_out_t[...], hidden, preferred_element_type=F32).astype(BF)


def row_of(x):
    return jnp.concatenate([x[k : k + 1] for k in range(x.shape[0])], axis=1)


def dense_of(blocks, atom, target, first):
    span = atom.shape[1]
    column = (iota((WIN_ATOMS, span), 0).astype(F32) == target).astype(BF)
    onehot = [
        jnp.broadcast_to((atom == as_float(first + s)).astype(F32), (WIN_ATOMS, span)).astype(BF) * column
        for s in range(GROUP)
    ]
    return nt_dot(blocks, jnp.concatenate(onehot, axis=0))


def put_dense(band, dense, first, base=None):
    lane = iota((ORB, 128), 1)
    low, even = lane < 64, lane % 64 < ATOM_Q
    for sp in range(GROUP // 2):
        s = first + 2 * sp
        pair, at_row = s // PAIR_ATOMS, s % PAIR_ATOMS * ORB
        if not isinstance(s, int):
            at_row = pl.multiple_of(at_row, 2 * ORB)
        for m in range(ORB // 4):
            x = [
                dense[(4 * m + i) * ORB : (4 * m + i + 1) * ORB, sp * 128 : sp * 128 + 128].astype(BF)
                for i in range(4)
            ]
            for half in range(2):
                if half == 0:
                    u = [jnp.where(low, x[i], pltpu.roll(x[i + 2], 64, 1)) for i in range(2)]
                else:
                    u = [jnp.where(low, pltpu.roll(x[i], 64, 1), x[i + 2]) for i in range(2)]
                both = (
                    jnp.where(even, u[0], pltpu.roll(u[1], ATOM_Q, 1)),
                    jnp.where(even, pltpu.roll(u[0], 128 - ATOM_Q, 1), u[1]),
                )
                rows = pl.ds(at_row + half * ORB, ORB)
                for n, value in enumerate(both):
                    lo = n * HALF + m * 128
                    if base is not None:
                        value = value + base[pair, rows, lo : lo + 128]
                    band[pair, rows, lo : lo + 128] = value


def column_of(atom, offset):
    target = TILE_ATOMS * (jnp.floor(atom * (1.0 / TILE_ATOMS)) - BAND) + offset
    base = BAND * TILE_ATOMS - PAIR_ATOMS * jnp.floor(atom * (1.0 / PAIR_ATOMS))
    outside = jnp.where(target < 0.0, target + (base + ATOM_Q), target + base)
    return jnp.where((target >= 0.0) & (target < float(ATOM_Q)), target, outside)


def as_float(x):
    return float(x) if isinstance(x, int) else x.astype(F32)


def place(message, is_left, rows, lists):
    nfeat = rows.shape[1]
    gap = rows.shape[0] - SPILL
    rows[0:gap, :] = jnp.zeros((gap, nfeat), BF)
    rows[SPILL : SPILL + gap, :] = jnp.zeros((gap, nfeat), BF)
    rows[pl.ds(pl.multiple_of(jnp.where(is_left, gap, 0), 64), SPILL), :] = message[0:SPILL, :]
    block = message[SPILL : SPILL + ID_ROWS, 0:128].astype(F32)
    atom, offset, cell = [row_of(block[3 * k : 3 * k + 3]) for k in range(3)]
    lists[0:1, :] = atom
    lists[1:2, :] = column_of(atom, offset)
    middle = (atom >= float(NEAR * GROUP)) & (atom < float(ATOM_Q - NEAR * GROUP))
    return cell, jnp.max(jnp.where(middle, 1.0, 0.0)) > 0.5


def at_ends(g):
    return g < NEAR or g >= ATOM_Q // GROUP - NEAR


def add_middle(band, blocks, lists, any_middle):
    @pl.when(any_middle)
    def _():
        for g in range(ATOM_Q // GROUP):
            if not at_ends(g):
                dense = dense_of(blocks[...], lists[0:1, :], lists[1:2, :], g * GROUP)
                put_dense(band, dense, g * GROUP, band)


def own_kernel(
    feat, src, dst, cell, near, cell_bias, w_in, w_out, _, band, w_in_t, bias_t, w_out_t, blk, blk2, bias8, rows, more, lists
):
    nblk = w_out.shape[1]
    w_in_t[...] = w_in[...].astype(F32).T.astype(BF)
    bias8[...] = jnp.zeros(bias8.shape, F32)
    bias8[0:3, :] = cell_bias[...].astype(F32)
    bias_t[...] = bias8[...].T.astype(BF)
    row, col = iota((nblk, nblk), 0), iota((nblk, nblk), 1)
    swap = (col == (row % ORB) * ORB + row // ORB).astype(BF)
    w_out_t[...] = nt_dot(swap, w_out[...]).astype(BF)
    own = feat.shape[0]
    ids = edge_ids(src[...], dst[...], cell[...])
    atom = row_of(ids[0])
    rows[0:1, :] = atom
    rows[1:2, :] = column_of(atom, row_of(ids[1]))
    is_left = device_side() == 1
    cells, any_middle = place(near, is_left, more, lists)
    blk[...] = pair_blocks(feat[...], row_of(ids[2]), w_in_t, bias_t, w_out_t)
    blk2[...] = pair_blocks(more[...], cells, w_in_t, bias_t, w_out_t)
    spans = []
    for first in range(0, ATOM_Q, GROUP):
        start = jnp.sum((ids[0] < float(first)).astype(F32)).astype(jnp.int32)
        spans.append(pl.ds(pl.multiple_of(jnp.minimum(start // 128 * 128, own - GROUP_SPAN), 128), GROUP_SPAN))
    for g, span in enumerate(spans):
        first = g * GROUP
        dense = dense_of(blk[:, span], rows[0:1, span], rows[1:2, span], first)
        if at_ends(g):
            dense = dense + dense_of(blk2[...], lists[0:1, :], lists[1:2, :], first)
        put_dense(band, dense, first)
    add_middle(band, blk2, lists, any_middle)


def spill_kernel(own_band, blue, w_in_t, bias_t, w_out_t, band, blk, more, lists):
    is_left = device_side() == 0
    cells, any_middle = place(blue, is_left, more, lists)
    blk[...] = pair_blocks(more[...], cells, w_in_t, bias_t, w_out_t)
    for g in range(ATOM_Q // GROUP):
        first = g * GROUP
        if at_ends(g):
            dense = dense_of(blk[...], lists[0:1, :], lists[1:2, :], first)
            put_dense(band, dense, first, own_band)
        else:
            pair, at = first // PAIR_ATOMS, first % PAIR_ATOMS * ORB
            band[pair, at : at + GROUP * ORB, :] = own_band[pair, at : at + GROUP * ORB, :]
    add_middle(band, blk, lists, any_middle)


def own_part(band, field):
    pieces = [field[pl.ds(q, ATOM_Q, stride=ORB), :].astype(BF) for q in range(ORB)]
    rhs = jnp.concatenate(pieces, axis=0)
    return [jnp.dot(band[k, :, :HALF], rhs, preferred_element_type=F32) for k in range(band.shape[0])]


def halo_part(band, blue, red, wide):
    even = device_side() == 0
    wide[0:HALO, :] = jnp.where(even, blue[...], red[...]).astype(F32)
    wide[HALO : 2 * HALO, :] = jnp.where(even, red[...], blue[...]).astype(F32)
    atoms = BAND * TILE_ATOMS
    pieces = [[], []]
    for q in range(ORB):
        left = wide[pl.ds(q, atoms, stride=ORB), :]
        right = wide[pl.ds(HALO + q, atoms, stride=ORB), :]
        pieces[0].append(jnp.concatenate([left, right[:TILE_ATOMS]], axis=0).astype(BF))
        pieces[1].append(jnp.concatenate([left[atoms - TILE_ATOMS :], right], axis=0).astype(BF))
    return [
        jnp.dot(band[k, :, HALF:], jnp.concatenate(pieces[k], axis=0), preferred_element_type=F32)
        for k in range(band.shape[0])
    ]


def put_sends(value_ref, to_blue, to_red):
    side = device_side()
    inner = value_ref.shape[0] - HALO
    off = pl.multiple_of(side * inner, 128)
    to_blue[...] = value_ref[pl.ds(off, HALO), :].astype(BF)
    to_red[...] = value_ref[pl.ds(pl.multiple_of(inner - off, 128), HALO), :].astype(BF)


def spans_of(band):
    height = band.shape[1]
    return [slice(k * height, (k + 1) * height) for k in range(band.shape[0])]


def start_kernel(band, now, part):
    inner = own_part(band, now)
    for k, span in enumerate(spans_of(band)):
        part[span, :] = inner[k]


def inner_kernel(band, before, now, part):
    inner = own_part(band, now)
    for k, span in enumerate(spans_of(band)):
        part[span, :] = 2.0 * inner[k] - before[span, :]


def outer_kernel(scale, band, part, blue, red, after, to_blue, to_red, wide):
    outer = halo_part(band, blue, red, wide)
    for k, span in enumerate(spans_of(band)):
        after[span, :] = scale * outer[k] + part[span, :]
    put_sends(after, to_blue, to_red)


def mix_kernel(coef, band, t0, t1, t2, t3, base, final):
    inner = own_part(band, t3)
    for k, span in enumerate(spans_of(band)):
        total = coef[0] * t0[span, :] + coef[1] * t1[span, :] + (coef[2] - coef[4]) * t2[span, :]
        total = total + coef[3] * t3[span, :] + 2.0 * coef[4] * inner[k]
        base[:, span] = total.T
    final[...] = jnp.full(final.shape, 2.0 * coef[4], F32)


def last_kernel(final, band, base, blue, red, p0, p1, p2, p3, wide, out):
    member = lax.axis_index("edges")
    outer = halo_part(band, blue, red, wide)
    for k, span in enumerate(spans_of(band)):
        out[:, span] = base[:, span] + (final[0:1, :] * outer[k]).T
    for k, piece in enumerate((p0, p1, p2, p3)):
        high = piece.shape[0]
        piece[...] = out[pl.ds(pl.multiple_of((member ^ k) * high, high), high), :].astype(BF)


def join_kernel(p0, p1, p2, p3, out):
    member = lax.axis_index("edges")
    for k, piece in enumerate((p0, p1, p2, p3)):
        width = piece.shape[1]
        at = pl.multiple_of((member ^ k) * width, width)
        out[:, pl.ds(at, width)] = piece[...].astype(F32)


VMEM = pl.BlockSpec(memory_space=pltpu.VMEM)
SMEM = pl.BlockSpec(memory_space=pltpu.SMEM)
IN_HBM = pl.BlockSpec(memory_space=pltpu.HBM)
FULL, PART = 60 * 1024 * 1024, 32 * 1024 * 1024


def shape(dims, dtype):
    return jax.ShapeDtypeStruct(dims, dtype)


def call(kernel, name, outs, scratch, *args, smem=(), in_hbm=(), out_hbm=(), alias=None, limit=PART, micros=1):
    spaces = [SMEM if k in smem else IN_HBM if k in in_hbm else VMEM for k in range(len(args))]
    return pl.pallas_call(
        kernel,
        name=name,
        out_shape=outs,
        in_specs=spaces,
        out_specs=tuple(IN_HBM if k in out_hbm else VMEM for k in range(len(outs))),
        scratch_shapes=scratch,
        input_output_aliases=alias or {},
        cost_estimate=pl.CostEstimate(flops=micros * 10**9, bytes_accessed=0, transcendentals=0),
        compiler_params=pltpu.CompilerParams(vmem_limit_bytes=limit),
    )(*args)


def per_device(features, edge_src, edge_dst, edge_cell, cell_bias, w_in, w_out, vectors, cheb_coef):
    axes = ("rows", "edges")
    nedge = lax.axis_size("edges")
    ndev = lax.axis_size("rows") * nedge
    red_pairs = [(i, i ^ 1) for i in range(ndev)]
    blue_pairs = [(i, (i + 1) % ndev if i % 2 else (i - 1) % ndev) for i in range(ndev)]
    nown, nfeat = features.shape
    high, ncol = vectors.shape
    nrow = ncol // nedge

    def swap(first, last):
        return (
            lax.ppermute(first, axes, blue_pairs),
            lax.ppermute(last, axes, red_pairs),
        )

    def exchange(pieces):
        return [pieces[0]] + [
            lax.ppermute(pieces[k], "edges", [(i, i ^ k) for i in range(nedge)]) for k in (1, 2, 3)
        ]

    msg = shape((SPILL + ID_ROWS, nfeat), BF)
    piece = shape((high, nrow), BF)
    lines = (nown // 128, 128)
    edges = [x.reshape(lines) for x in (edge_src, edge_dst, edge_cell)]
    near_msg = shape((SPILL + ID_ROWS + high * nrow // nfeat, nfeat), BF)
    own_piece, straight, across, blue_msg, near = call(
        prep_kernel,
        "prep",
        (piece,) * 3 + (msg, near_msg),
        [pltpu.VMEM((nedge, high, nrow), F32)]
        + [pltpu.VMEM(lines, jnp.int32)] * 3
        + [pltpu.SemaphoreType.DMA((9,))],
        vectors,
        features,
        *edges,
        in_hbm=range(5),
        limit=FULL,
    )
    across = lax.ppermute(across, "edges", [(i, i ^ 3) for i in range(nedge)])
    straight = lax.ppermute(straight, "edges", [(i, i ^ 2) for i in range(nedge)])
    near = lax.ppermute(near, axes, red_pairs)
    blue_msg = lax.ppermute(blue_msg, axes, blue_pairs)
    (across,) = call(pass_kernel, "pass", (piece,), [], across, micros=0)
    pieces = [own_piece, near, straight, across]
    full, part = shape((nrow, VEC), F32), shape((HALO, VEC), BF)
    t0, to_blue, to_red, token = call(
        field_kernel, "field", (full, part, part, shape((8, VEC), F32)), [pltpu.VMEM((VEC, nrow), F32)], *pieces
    )
    blue, red = swap(to_blue, to_red)

    wide_spill = SPILL + 64
    band_shape = shape((ATOM_Q // PAIR_ATOMS, PAIR_ATOMS * ORB, WIN_ATOMS * ORB), BF)
    width = w_in.shape[1]
    band, *weights = call(
        own_kernel,
        "own",
        (band_shape, shape((width, nfeat), BF), shape((width, 8), BF), shape((ORB * ORB, HID), BF)),
        [
            pltpu.VMEM((ORB * ORB, nown), BF),
            pltpu.VMEM((ORB * ORB, wide_spill), BF),
            pltpu.VMEM((8, width), F32),
            pltpu.VMEM((8, nown), F32),
            pltpu.VMEM((wide_spill, nfeat), BF),
            pltpu.VMEM((8, wide_spill), F32),
        ],
        features,
        *edges,
        near,
        cell_bias,
        w_in,
        w_out,
        token,
        micros=4,
    )
    (band,) = call(
        spill_kernel,
        "spill",
        (band_shape,),
        [
            pltpu.VMEM((ORB * ORB, wide_spill), BF),
            pltpu.VMEM((wide_spill, nfeat), BF),
            pltpu.VMEM((8, wide_spill), F32),
        ],
        band,
        blue_msg,
        *weights,
        alias={0: 0},
        micros=0,
    )

    wide = pltpu.VMEM((2 * HALO, VEC), F32)
    fields = [t0]
    for step in range(1, STEPS):
        if step > 1:
            blue, red = swap(to_blue, to_red)
        inner, name = (start_kernel, "start") if step == 1 else (inner_kernel, "inner")
        (inner,) = call(inner, name, (full,), [], band, *fields[-2:])
        following, to_blue, to_red = call(
            functools.partial(outer_kernel, 1.0 if step == 1 else 2.0),
            "outer",
            (full, part, part),
            [wide],
            band,
            inner,
            blue,
            red,
        )
        fields.append(following)
    blue, red = swap(to_blue, to_red)
    base, final = call(
        mix_kernel,
        "mix",
        (shape((VEC, nrow), F32), shape((8, VEC), F32)),
        [],
        cheb_coef,
        band,
        *fields,
        smem=(0,),
    )
    pieces = call(
        last_kernel,
        "last",
        (piece,) * 4,
        [wide, pltpu.VMEM((VEC, nrow), F32)],
        final,
        band,
        base,
        blue,
        red,
    )
    (result,) = call(join_kernel, "join", (shape((high, ncol), F32),), [], *exchange(pieces))
    return result


def solution(mesh):
    placed = (
        P(("rows", "edges"), None),
        P(("rows", "edges")),
        P(("rows", "edges")),
        P(("rows", "edges")),
        P(),
        P(),
        P(),
        P("edges", "rows"),
        P(),
    )
    return jax.shard_map(
        per_device, mesh=mesh, in_specs=placed, out_specs=P("edges", "rows"), check_vma=False
    )
```

```python
import functools

import jax
import jax.numpy as jnp
from jax import lax
from jax.experimental import pallas as pl
from jax.experimental.pallas import tpu as pltpu
from jax.sharding import PartitionSpec as P

ORB = 16
TILE_ATOMS = 8
BAND = 3
HID = 256
VEC = 128
STEPS = 4
ATOM_Q = 32
SPILL = 320
ID_ROWS = 16
PAIR_ATOMS = 2 * TILE_ATOMS
WIN_ATOMS = (2 * BAND + 2) * TILE_ATOMS
HALO = BAND * TILE_ATOMS * ORB
GROUP = 4
GROUP_SPAN = 384
HALF = ATOM_Q * ORB
NEAR = 3
BF = jnp.bfloat16
F32 = jnp.float32
NT = (((1,), (1,)), ((), ()))


def nt_dot(a, b):
    return lax.dot_general(a, b, NT, preferred_element_type=F32)


def iota(shape, dim):
    return lax.broadcasted_iota(jnp.int32, shape, dim)


def device_side():
    return (lax.axis_index("rows") * lax.axis_size("edges") + lax.axis_index("edges")) % 2


def edge_ids(src, dst, cell):
    ndev = lax.axis_size("rows") * lax.axis_size("edges")
    quarter = lax.axis_index("rows") * lax.axis_size("edges") + lax.axis_index("edges")
    natom = ATOM_Q * ndev
    ntiles = natom // TILE_ATOMS
    rel = src - quarter * ATOM_Q
    rel = jnp.where(rel > natom // 2, rel - natom, jnp.where(rel < -(natom // 2), rel + natom, rel))
    shift = (dst >> 3) - (src >> 3) + BAND
    shift = jnp.where(shift < 0, shift + ntiles, jnp.where(shift >= ntiles, shift - ntiles, shift))
    return [x.astype(F32) for x in (rel, shift * TILE_ATOMS + (dst & 7), cell)]


def prep_kernel(
    vec_hbm,
    feat,
    src_hbm,
    dst_hbm,
    cell_hbm,
    p0,
    p2,
    p3,
    blue,
    red,
    vectors,
    halves,
    sends,
    msgs,
    src,
    dst,
    cell,
    sems,
    out_sems,
):
    member, side = lax.axis_index("edges"), device_side()
    high_rows, width = p0.shape
    nfeat = feat.shape[1]
    lists = [
        pltpu.make_async_copy(x, y, sems.at[6 + n])
        for n, (x, y) in enumerate(((src_hbm, src), (dst_hbm, dst), (cell_hbm, cell)))
    ]
    loads = []
    for k in range(4):
        at = pl.multiple_of((member ^ k) * width, width)
        loads.append(pltpu.make_async_copy(vec_hbm.at[:, pl.ds(at, width)], vectors.at[k], sems.at[k]))
    high = feat.shape[0] - SPILL
    off = pl.multiple_of(side * high, 64)
    copies = [
        pltpu.make_async_copy(feat.at[pl.ds(off, SPILL)], halves.at[0], sems.at[4]),
        pltpu.make_async_copy(feat.at[pl.ds(pl.multiple_of(high - off, 64), SPILL)], halves.at[1], sems.at[5]),
    ]
    outs = []

    def send(x, y):
        copy = pltpu.make_async_copy(x, y, out_sems.at[len(outs)])
        copy.start()
        outs.append(copy)

    for copy in lists + loads + copies:
        copy.start()
    for copy in lists:
        copy.wait()
    three = edge_ids(src[...], dst[...], cell[...])
    lane, line = iota((3, 128), 1), iota((3, 128), 0)
    nrow = src.shape[0]
    starts = [x[0:3] for x in three]
    ends = [x[nrow - 3 : nrow] for x in three]
    starts[0] = jnp.where((line == 2) & (lane >= 64), -64.0, starts[0] + ATOM_Q)
    ends[0] = jnp.where((line == 0) & (lane < 64), -64.0, ends[0] - ATOM_Q)
    pad = jnp.zeros((ID_ROWS - 9, 128), F32)
    low_ids = jnp.concatenate(starts + [pad], axis=0)
    high_ids = jnp.concatenate(ends + [pad], axis=0)
    none = jnp.zeros((ID_ROWS, 128), BF)
    for n, ids_of in enumerate((jnp.where(side == 0, low_ids, high_ids), jnp.where(side == 0, high_ids, low_ids))):
        msgs[n, 0:ID_ROWS, 0:128] = ids_of.astype(BF)
        msgs[n, 0:ID_ROWS, 128:256] = none
    send(msgs.at[0, pl.ds(0, ID_ROWS)], blue.at[pl.ds(SPILL, ID_ROWS)])
    for k in (3, 2, 1, 0):
        loads[k].wait()
        if k == 1:
            for n in range(width // nfeat):
                at = ID_ROWS + n * high_rows
                msgs[1, at : at + high_rows, :] = vectors[k, :, n * nfeat : (n + 1) * nfeat].astype(BF)
            rest = red.shape[0] - SPILL
            send(msgs.at[1, pl.ds(0, rest)], red.at[pl.ds(SPILL, rest)])
        else:
            sends[k] = vectors[k].astype(BF)
            send(sends.at[k], {0: p0, 2: p2, 3: p3}[k])
    for n, msg in ((1, red), (0, blue)):
        copies[n].wait()
        send(halves.at[n], msg.at[pl.ds(0, SPILL)])
    for copy in outs:
        copy.wait()


def pass_kernel(x, y):
    y[...] = x[...]


def field_kernel(p0, near, p2, p3, t0, to_blue, to_red, token, field):
    member = lax.axis_index("edges")
    high = p0.shape[0]
    for k, piece in ((0, p0), (2, p2), (3, p3)):
        field[pl.ds(pl.multiple_of((member ^ k) * high, high), high), :] = piece[...].astype(F32)
    rows = pl.ds(pl.multiple_of((member ^ 1) * high, high), high)
    width = near.shape[1]
    for n in range(field.shape[1] // width):
        at = SPILL + ID_ROWS + n * high
        field[rows, n * width : (n + 1) * width] = near[at : at + high, :].astype(F32)
    t0[...] = field[...].T
    token[...] = jnp.zeros(token.shape, F32)
    put_sends(t0, to_blue, to_red)


def pair_blocks(x, cell, w_in_t, bias_t, w_out_t):
    bias = [bias_t[:, k : k + 1].astype(F32) for k in range(3)]
    pre = nt_dot(w_in_t[...], x)
    pre = pre + jnp.where(cell == 1.0, bias[1], jnp.where(cell == 2.0, bias[2], bias[0]))
    gate, up = pre[:HID], pre[HID:]
    hidden = (gate * (0.5 + 0.5 * jnp.tanh(0.5 * gate)) * up).astype(BF)
    return jnp.dot(w_out_t[...], hidden, preferred_element_type=F32).astype(BF)


def row_of(x):
    return jnp.concatenate([x[k : k + 1] for k in range(x.shape[0])], axis=1)


def dense_of(blocks, atom, target, first):
    span = atom.shape[1]
    column = (iota((WIN_ATOMS, span), 0).astype(F32) == target).astype(BF)
    onehot = [
        jnp.broadcast_to((atom == as_float(first + s)).astype(F32), (WIN_ATOMS, span)).astype(BF) * column
        for s in range(GROUP)
    ]
    return nt_dot(blocks, jnp.concatenate(onehot, axis=0))


def put_dense(band, dense, first, base=None):
    lane = iota((ORB, 128), 1)
    low, even = lane < 64, lane % 64 < ATOM_Q
    for sp in range(GROUP // 2):
        s = first + 2 * sp
        pair, at_row = s // PAIR_ATOMS, s % PAIR_ATOMS * ORB
        if not isinstance(s, int):
            at_row = pl.multiple_of(at_row, 2 * ORB)
        for m in range(ORB // 4):
            x = [
                dense[(4 * m + i) * ORB : (4 * m + i + 1) * ORB, sp * 128 : sp * 128 + 128].astype(BF)
                for i in range(4)
            ]
            for half in range(2):
                if half == 0:
                    u = [jnp.where(low, x[i], pltpu.roll(x[i + 2], 64, 1)) for i in range(2)]
                else:
                    u = [jnp.where(low, pltpu.roll(x[i], 64, 1), x[i + 2]) for i in range(2)]
                both = (
                    jnp.where(even, u[0], pltpu.roll(u[1], ATOM_Q, 1)),
                    jnp.where(even, pltpu.roll(u[0], 128 - ATOM_Q, 1), u[1]),
                )
                rows = pl.ds(at_row + half * ORB, ORB)
                for n, value in enumerate(both):
                    lo = n * HALF + m * 128
                    if base is not None:
                        value = value + base[pair, rows, lo : lo + 128]
                    band[pair, rows, lo : lo + 128] = value


def column_of(atom, offset):
    target = TILE_ATOMS * (jnp.floor(atom * (1.0 / TILE_ATOMS)) - BAND) + offset
    base = BAND * TILE_ATOMS - PAIR_ATOMS * jnp.floor(atom * (1.0 / PAIR_ATOMS))
    outside = jnp.where(target < 0.0, target + (base + ATOM_Q), target + base)
    return jnp.where((target >= 0.0) & (target < float(ATOM_Q)), target, outside)


def as_float(x):
    return float(x) if isinstance(x, int) else x.astype(F32)


def place(message, is_left, rows, lists):
    nfeat = rows.shape[1]
    gap = rows.shape[0] - SPILL
    rows[0:gap, :] = jnp.zeros((gap, nfeat), BF)
    rows[SPILL : SPILL + gap, :] = jnp.zeros((gap, nfeat), BF)
    rows[pl.ds(pl.multiple_of(jnp.where(is_left, gap, 0), 64), SPILL), :] = message[0:SPILL, :]
    block = message[SPILL : SPILL + ID_ROWS, 0:128].astype(F32)
    atom, offset, cell = [row_of(block[3 * k : 3 * k + 3]) for k in range(3)]
    lists[0:1, :] = atom
    lists[1:2, :] = column_of(atom, offset)
    middle = (atom >= float(NEAR * GROUP)) & (atom < float(ATOM_Q - NEAR * GROUP))
    return cell, jnp.max(jnp.where(middle, 1.0, 0.0)) > 0.5


def at_ends(g):
    return g < NEAR or g >= ATOM_Q // GROUP - NEAR


def add_middle(band, blocks, lists, any_middle):
    @pl.when(any_middle)
    def _():
        for g in range(ATOM_Q // GROUP):
            if not at_ends(g):
                dense = dense_of(blocks[...], lists[0:1, :], lists[1:2, :], g * GROUP)
                put_dense(band, dense, g * GROUP, band)


def own_kernel(
    feat, src, dst, cell, near, cell_bias, w_in, w_out, _, band, w_in_t, bias_t, w_out_t, blk, blk2, bias8, rows, more, lists
):
    nblk = w_out.shape[1]
    w_in_t[...] = w_in[...].astype(F32).T.astype(BF)
    bias8[...] = jnp.zeros(bias8.shape, F32)
    bias8[0:3, :] = cell_bias[...].astype(F32)
    bias_t[...] = bias8[...].T.astype(BF)
    row, col = iota((nblk, nblk), 0), iota((nblk, nblk), 1)
    swap = (col == (row % ORB) * ORB + row // ORB).astype(BF)
    w_out_t[...] = nt_dot(swap, w_out[...]).astype(BF)
    own = feat.shape[0]
    ids = edge_ids(src[...], dst[...], cell[...])
    atom = row_of(ids[0])
    rows[0:1, :] = atom
    rows[1:2, :] = column_of(atom, row_of(ids[1]))
    is_left = device_side() == 1
    cells, any_middle = place(near, is_left, more, lists)
    blk[...] = pair_blocks(feat[...], row_of(ids[2]), w_in_t, bias_t, w_out_t)
    blk2[...] = pair_blocks(more[...], cells, w_in_t, bias_t, w_out_t)
    spans = []
    for first in range(0, ATOM_Q, GROUP):
        start = jnp.sum((ids[0] < float(first)).astype(F32)).astype(jnp.int32)
        spans.append(pl.ds(pl.multiple_of(jnp.minimum(start // 128 * 128, own - GROUP_SPAN), 128), GROUP_SPAN))
    for g, span in enumerate(spans):
        first = g * GROUP
        dense = dense_of(blk[:, span], rows[0:1, span], rows[1:2, span], first)
        if at_ends(g):
            dense = dense + dense_of(blk2[...], lists[0:1, :], lists[1:2, :], first)
        put_dense(band, dense, first)
    add_middle(band, blk2, lists, any_middle)


def spill_kernel(own_band, blue, w_in_t, bias_t, w_out_t, band, blk, more, lists):
    is_left = device_side() == 0
    cells, any_middle = place(blue, is_left, more, lists)
    blk[...] = pair_blocks(more[...], cells, w_in_t, bias_t, w_out_t)
    for g in range(ATOM_Q // GROUP):
        first = g * GROUP
        if at_ends(g):
            dense = dense_of(blk[...], lists[0:1, :], lists[1:2, :], first)
            put_dense(band, dense, first, own_band)
        else:
            pair, at = first // PAIR_ATOMS, first % PAIR_ATOMS * ORB
            band[pair, at : at + GROUP * ORB, :] = own_band[pair, at : at + GROUP * ORB, :]
    add_middle(band, blk, lists, any_middle)


def own_part(band, field):
    pieces = [field[pl.ds(q, ATOM_Q, stride=ORB), :].astype(BF) for q in range(ORB)]
    rhs = jnp.concatenate(pieces, axis=0)
    return [jnp.dot(band[k, :, :HALF], rhs, preferred_element_type=F32) for k in range(band.shape[0])]


def halo_part(band, blue, red, wide):
    even = device_side() == 0
    wide[0:HALO, :] = jnp.where(even, blue[...], red[...]).astype(F32)
    wide[HALO : 2 * HALO, :] = jnp.where(even, red[...], blue[...]).astype(F32)
    atoms = BAND * TILE_ATOMS
    pieces = [[], []]
    for q in range(ORB):
        left = wide[pl.ds(q, atoms, stride=ORB), :]
        right = wide[pl.ds(HALO + q, atoms, stride=ORB), :]
        pieces[0].append(jnp.concatenate([left, right[:TILE_ATOMS]], axis=0).astype(BF))
        pieces[1].append(jnp.concatenate([left[atoms - TILE_ATOMS :], right], axis=0).astype(BF))
    return [
        jnp.dot(band[k, :, HALF:], jnp.concatenate(pieces[k], axis=0), preferred_element_type=F32)
        for k in range(band.shape[0])
    ]


def put_sends(value_ref, to_blue, to_red):
    side = device_side()
    inner = value_ref.shape[0] - HALO
    off = pl.multiple_of(side * inner, 128)
    to_blue[...] = value_ref[pl.ds(off, HALO), :].astype(BF)
    to_red[...] = value_ref[pl.ds(pl.multiple_of(inner - off, 128), HALO), :].astype(BF)


def spans_of(band):
    height = band.shape[1]
    return [slice(k * height, (k + 1) * height) for k in range(band.shape[0])]


def start_kernel(band, now, part):
    inner = own_part(band, now)
    for k, span in enumerate(spans_of(band)):
        part[span, :] = inner[k]


def inner_kernel(band, before, now, part):
    inner = own_part(band, now)
    for k, span in enumerate(spans_of(band)):
        part[span, :] = 2.0 * inner[k] - before[span, :]


def outer_kernel(scale, band, part, blue, red, after, to_blue, to_red, wide):
    outer = halo_part(band, blue, red, wide)
    for k, span in enumerate(spans_of(band)):
        after[span, :] = scale * outer[k] + part[span, :]
    put_sends(after, to_blue, to_red)


def mix_kernel(coef, band, t0, t1, t2, t3, base, final):
    inner = own_part(band, t3)
    for k, span in enumerate(spans_of(band)):
        total = coef[0] * t0[span, :] + coef[1] * t1[span, :] + (coef[2] - coef[4]) * t2[span, :]
        total = total + coef[3] * t3[span, :] + 2.0 * coef[4] * inner[k]
        base[:, span] = total.T
    final[...] = jnp.full(final.shape, 2.0 * coef[4], F32)


def last_kernel(final, band, base, blue, red, p0, p1, p2, p3, wide, out):
    member = lax.axis_index("edges")
    outer = halo_part(band, blue, red, wide)
    for k, span in enumerate(spans_of(band)):
        out[:, span] = base[:, span] + (final[0:1, :] * outer[k]).T
    for k, piece in enumerate((p0, p1, p2, p3)):
        high = piece.shape[0]
        piece[...] = out[pl.ds(pl.multiple_of((member ^ k) * high, high), high), :].astype(BF)


def join_kernel(p0, p1, p2, p3, out):
    member = lax.axis_index("edges")
    for k, piece in enumerate((p0, p1, p2, p3)):
        width = piece.shape[1]
        at = pl.multiple_of((member ^ k) * width, width)
        out[:, pl.ds(at, width)] = piece[...].astype(F32)


VMEM = pl.BlockSpec(memory_space=pltpu.VMEM)
SMEM = pl.BlockSpec(memory_space=pltpu.SMEM)
IN_HBM = pl.BlockSpec(memory_space=pltpu.HBM)
FULL, PART = 60 * 1024 * 1024, 32 * 1024 * 1024


def shape(dims, dtype):
    return jax.ShapeDtypeStruct(dims, dtype)


def call(kernel, name, outs, scratch, *args, smem=(), in_hbm=(), out_hbm=(), alias=None, limit=PART, micros=1):
    spaces = [SMEM if k in smem else IN_HBM if k in in_hbm else VMEM for k in range(len(args))]
    return pl.pallas_call(
        kernel,
        name=name,
        out_shape=outs,
        in_specs=spaces,
        out_specs=tuple(IN_HBM if k in out_hbm else VMEM for k in range(len(outs))),
        scratch_shapes=scratch,
        input_output_aliases=alias or {},
        cost_estimate=pl.CostEstimate(flops=micros * 10**9, bytes_accessed=0, transcendentals=0),
        compiler_params=pltpu.CompilerParams(vmem_limit_bytes=limit),
    )(*args)


def per_device(features, edge_src, edge_dst, edge_cell, cell_bias, w_in, w_out, vectors, cheb_coef):
    axes = ("rows", "edges")
    nedge = lax.axis_size("edges")
    ndev = lax.axis_size("rows") * nedge
    red_pairs = [(i, i ^ 1) for i in range(ndev)]
    blue_pairs = [(i, (i + 1) % ndev if i % 2 else (i - 1) % ndev) for i in range(ndev)]
    nown, nfeat = features.shape
    high, ncol = vectors.shape
    nrow = ncol // nedge

    def swap(first, last):
        return (
            lax.ppermute(first, axes, blue_pairs),
            lax.ppermute(last, axes, red_pairs),
        )

    def exchange(pieces):
        return [pieces[0]] + [
            lax.ppermute(pieces[k], "edges", [(i, i ^ k) for i in range(nedge)]) for k in (1, 2, 3)
        ]

    msg = shape((SPILL + ID_ROWS, nfeat), BF)
    piece = shape((high, nrow), BF)
    lines = (nown // 128, 128)
    edges = [x.reshape(lines) for x in (edge_src, edge_dst, edge_cell)]
    near_msg = shape((SPILL + ID_ROWS + high * nrow // nfeat, nfeat), BF)
    own_piece, straight, across, blue_msg, near = call(
        prep_kernel,
        "prep",
        (piece,) * 3 + (msg, near_msg),
        [
            pltpu.VMEM((nedge, high, nrow), F32),
            pltpu.VMEM((2, SPILL, nfeat), BF),
            pltpu.VMEM((nedge, high, nrow), BF),
            pltpu.VMEM((2, near_msg.shape[0] - SPILL, nfeat), BF),
        ]
        + [pltpu.VMEM(lines, jnp.int32)] * 3
        + [pltpu.SemaphoreType.DMA((9,)), pltpu.SemaphoreType.DMA((7,))],
        vectors,
        features,
        *edges,
        in_hbm=range(5),
        out_hbm=range(5),
        limit=FULL,
    )
    across = lax.ppermute(across, "edges", [(i, i ^ 3) for i in range(nedge)])
    straight = lax.ppermute(straight, "edges", [(i, i ^ 2) for i in range(nedge)])
    near = lax.ppermute(near, axes, red_pairs)
    blue_msg = lax.ppermute(blue_msg, axes, blue_pairs)
    (across,) = call(pass_kernel, "pass", (piece,), [], across, micros=0)
    pieces = [own_piece, near, straight, across]
    full, part = shape((nrow, VEC), F32), shape((HALO, VEC), BF)
    t0, to_blue, to_red, token = call(
        field_kernel, "field", (full, part, part, shape((8, VEC), F32)), [pltpu.VMEM((VEC, nrow), F32)], *pieces
    )
    blue, red = swap(to_blue, to_red)

    wide_spill = SPILL + 64
    band_shape = shape((ATOM_Q // PAIR_ATOMS, PAIR_ATOMS * ORB, WIN_ATOMS * ORB), BF)
    width = w_in.shape[1]
    band, *weights = call(
        own_kernel,
        "own",
        (band_shape, shape((width, nfeat), BF), shape((width, 8), BF), shape((ORB * ORB, HID), BF)),
        [
            pltpu.VMEM((ORB * ORB, nown), BF),
            pltpu.VMEM((ORB * ORB, wide_spill), BF),
            pltpu.VMEM((8, width), F32),
            pltpu.VMEM((8, nown), F32),
            pltpu.VMEM((wide_spill, nfeat), BF),
            pltpu.VMEM((8, wide_spill), F32),
        ],
        features,
        *edges,
        near,
        cell_bias,
        w_in,
        w_out,
        token,
        micros=4,
    )
    (band,) = call(
        spill_kernel,
        "spill",
        (band_shape,),
        [
            pltpu.VMEM((ORB * ORB, wide_spill), BF),
            pltpu.VMEM((wide_spill, nfeat), BF),
            pltpu.VMEM((8, wide_spill), F32),
        ],
        band,
        blue_msg,
        *weights,
        alias={0: 0},
        micros=0,
    )

    wide = pltpu.VMEM((2 * HALO, VEC), F32)
    fields = [t0]
    for step in range(1, STEPS):
        if step > 1:
            blue, red = swap(to_blue, to_red)
        inner, name = (start_kernel, "start") if step == 1 else (inner_kernel, "inner")
        (inner,) = call(inner, name, (full,), [], band, *fields[-2:])
        following, to_blue, to_red = call(
            functools.partial(outer_kernel, 1.0 if step == 1 else 2.0),
            "outer",
            (full, part, part),
            [wide],
            band,
            inner,
            blue,
            red,
        )
        fields.append(following)
    blue, red = swap(to_blue, to_red)
    base, final = call(
        mix_kernel,
        "mix",
        (shape((VEC, nrow), F32), shape((8, VEC), F32)),
        [],
        cheb_coef,
        band,
        *fields,
        smem=(0,),
    )
    pieces = call(
        last_kernel,
        "last",
        (piece,) * 4,
        [wide, pltpu.VMEM((VEC, nrow), F32)],
        final,
        band,
        base,
        blue,
        red,
    )
    (result,) = call(join_kernel, "join", (shape((high, ncol), F32),), [], *exchange(pieces))
    return result


def solution(mesh):
    placed = (
        P(("rows", "edges"), None),
        P(("rows", "edges")),
        P(("rows", "edges")),
        P(("rows", "edges")),
        P(),
        P(),
        P(),
        P("edges", "rows"),
        P(),
    )
    return jax.shard_map(
        per_device, mesh=mesh, in_specs=placed, out_specs=P("edges", "rows"), check_vma=False
    )
```

```python
import functools

import jax
import jax.numpy as jnp
from jax import lax
from jax.experimental import pallas as pl
from jax.experimental.pallas import tpu as pltpu
from jax.sharding import PartitionSpec as P

ORB = 16
TILE_ATOMS = 8
BAND = 3
HID = 256
VEC = 128
STEPS = 4
ATOM_Q = 32
SPILL = 320
ID_ROWS = 16
PAIR_ATOMS = 2 * TILE_ATOMS
WIN_ATOMS = (2 * BAND + 2) * TILE_ATOMS
HALO = BAND * TILE_ATOMS * ORB
GROUP = 4
GROUP_SPAN = 384
HALF = ATOM_Q * ORB
NEAR = 3
BF = jnp.bfloat16
F32 = jnp.float32
NT = (((1,), (1,)), ((), ()))


def nt_dot(a, b):
    return lax.dot_general(a, b, NT, preferred_element_type=F32)


def iota(shape, dim):
    return lax.broadcasted_iota(jnp.int32, shape, dim)


def device_side():
    return (lax.axis_index("rows") * lax.axis_size("edges") + lax.axis_index("edges")) % 2


def edge_ids(src, dst, cell):
    ndev = lax.axis_size("rows") * lax.axis_size("edges")
    quarter = lax.axis_index("rows") * lax.axis_size("edges") + lax.axis_index("edges")
    natom = ATOM_Q * ndev
    ntiles = natom // TILE_ATOMS
    rel = src - quarter * ATOM_Q
    rel = jnp.where(rel > natom // 2, rel - natom, jnp.where(rel < -(natom // 2), rel + natom, rel))
    shift = (dst >> 3) - (src >> 3) + BAND
    shift = jnp.where(shift < 0, shift + ntiles, jnp.where(shift >= ntiles, shift - ntiles, shift))
    return [x.astype(F32) for x in (rel, shift * TILE_ATOMS + (dst & 7), cell)]


def split_kernel(vectors, p0, p1, p2, p3):
    member = lax.axis_index("edges")
    for k, piece in enumerate((p0, p1, p2, p3)):
        width = piece.shape[1]
        at = pl.multiple_of((member ^ k) * width, width)
        piece[...] = vectors[:, pl.ds(at, width)].astype(BF)


def message_kernel(feat, src, dst, cell, p1, blue, red):
    side = device_side()
    high_rows, width = p1.shape
    nfeat = feat.shape[1]
    high = feat.shape[0] - SPILL
    off = pl.multiple_of(side * high, 64)
    blue[0:SPILL, :] = feat[pl.ds(off, SPILL), :]
    red[0:SPILL, :] = feat[pl.ds(pl.multiple_of(high - off, 64), SPILL), :]
    three = edge_ids(src[...], dst[...], cell[...])
    lane, line = iota((3, 128), 1), iota((3, 128), 0)
    nrow = src.shape[0]
    starts = [x[0:3] for x in three]
    ends = [x[nrow - 3 : nrow] for x in three]
    starts[0] = jnp.where((line == 2) & (lane >= 64), -64.0, starts[0] + ATOM_Q)
    ends[0] = jnp.where((line == 0) & (lane < 64), -64.0, ends[0] - ATOM_Q)
    pad = jnp.zeros((ID_ROWS - 9, 128), F32)
    low_ids = jnp.concatenate(starts + [pad], axis=0)
    high_ids = jnp.concatenate(ends + [pad], axis=0)
    none = jnp.zeros((ID_ROWS, 128), BF)
    for msg, ids_of in (
        (blue, jnp.where(side == 0, low_ids, high_ids)),
        (red, jnp.where(side == 0, high_ids, low_ids)),
    ):
        msg[SPILL : SPILL + ID_ROWS, 0:128] = ids_of.astype(BF)
        msg[SPILL : SPILL + ID_ROWS, 128:256] = none
    for n in range(width // nfeat):
        at = SPILL + ID_ROWS + n * high_rows
        red[at : at + high_rows, :] = p1[:, n * nfeat : (n + 1) * nfeat]


def pass_kernel(x, y):
    y[...] = x[...]


def field_kernel(p0, near, p2, p3, t0, to_blue, to_red, token, field):
    member = lax.axis_index("edges")
    high = p0.shape[0]
    for k, piece in ((0, p0), (2, p2), (3, p3)):
        field[pl.ds(pl.multiple_of((member ^ k) * high, high), high), :] = piece[...].astype(F32)
    rows = pl.ds(pl.multiple_of((member ^ 1) * high, high), high)
    width = near.shape[1]
    for n in range(field.shape[1] // width):
        at = SPILL + ID_ROWS + n * high
        field[rows, n * width : (n + 1) * width] = near[at : at + high, :].astype(F32)
    t0[...] = field[...].T
    token[...] = jnp.zeros(token.shape, F32)
    put_sends(t0, to_blue, to_red)


def pair_blocks(x, cell, w_in_t, bias_t, w_out_t):
    bias = [bias_t[:, k : k + 1].astype(F32) for k in range(3)]
    pre = nt_dot(w_in_t[...], x)
    pre = pre + jnp.where(cell == 1.0, bias[1], jnp.where(cell == 2.0, bias[2], bias[0]))
    gate, up = pre[:HID], pre[HID:]
    hidden = (gate * (0.5 + 0.5 * jnp.tanh(0.5 * gate)) * up).astype(BF)
    return jnp.dot(w_out_t[...], hidden, preferred_element_type=F32).astype(BF)


def row_of(x):
    return jnp.concatenate([x[k : k + 1] for k in range(x.shape[0])], axis=1)


def dense_of(blocks, atom, target, first):
    span = atom.shape[1]
    column = (iota((WIN_ATOMS, span), 0).astype(F32) == target).astype(BF)
    onehot = [
        jnp.broadcast_to((atom == as_float(first + s)).astype(F32), (WIN_ATOMS, span)).astype(BF) * column
        for s in range(GROUP)
    ]
    return nt_dot(blocks, jnp.concatenate(onehot, axis=0))


def put_dense(band, dense, first, base=None):
    lane = iota((ORB, 128), 1)
    low, even = lane < 64, lane % 64 < ATOM_Q
    for sp in range(GROUP // 2):
        s = first + 2 * sp
        pair, at_row = s // PAIR_ATOMS, s % PAIR_ATOMS * ORB
        if not isinstance(s, int):
            at_row = pl.multiple_of(at_row, 2 * ORB)
        for m in range(ORB // 4):
            x = [
                dense[(4 * m + i) * ORB : (4 * m + i + 1) * ORB, sp * 128 : sp * 128 + 128].astype(BF)
                for i in range(4)
            ]
            for half in range(2):
                if half == 0:
                    u = [jnp.where(low, x[i], pltpu.roll(x[i + 2], 64, 1)) for i in range(2)]
                else:
                    u = [jnp.where(low, pltpu.roll(x[i], 64, 1), x[i + 2]) for i in range(2)]
                both = (
                    jnp.where(even, u[0], pltpu.roll(u[1], ATOM_Q, 1)),
                    jnp.where(even, pltpu.roll(u[0], 128 - ATOM_Q, 1), u[1]),
                )
                rows = pl.ds(at_row + half * ORB, ORB)
                for n, value in enumerate(both):
                    lo = n * HALF + m * 128
                    if base is not None:
                        value = value + base[pair, rows, lo : lo + 128]
                    band[pair, rows, lo : lo + 128] = value


def column_of(atom, offset):
    target = TILE_ATOMS * (jnp.floor(atom * (1.0 / TILE_ATOMS)) - BAND) + offset
    base = BAND * TILE_ATOMS - PAIR_ATOMS * jnp.floor(atom * (1.0 / PAIR_ATOMS))
    outside = jnp.where(target < 0.0, target + (base + ATOM_Q), target + base)
    return jnp.where((target >= 0.0) & (target < float(ATOM_Q)), target, outside)


def as_float(x):
    return float(x) if isinstance(x, int) else x.astype(F32)


def place(message, is_left, rows, lists):
    nfeat = rows.shape[1]
    gap = rows.shape[0] - SPILL
    rows[0:gap, :] = jnp.zeros((gap, nfeat), BF)
    rows[SPILL : SPILL + gap, :] = jnp.zeros((gap, nfeat), BF)
    rows[pl.ds(pl.multiple_of(jnp.where(is_left, gap, 0), 64), SPILL), :] = message[0:SPILL, :]
    block = message[SPILL : SPILL + ID_ROWS, 0:128].astype(F32)
    atom, offset, cell = [row_of(block[3 * k : 3 * k + 3]) for k in range(3)]
    lists[0:1, :] = atom
    lists[1:2, :] = column_of(atom, offset)
    middle = (atom >= float(NEAR * GROUP)) & (atom < float(ATOM_Q - NEAR * GROUP))
    return cell, jnp.max(jnp.where(middle, 1.0, 0.0)) > 0.5


def at_ends(g):
    return g < NEAR or g >= ATOM_Q // GROUP - NEAR


def add_middle(band, blocks, lists, any_middle):
    @pl.when(any_middle)
    def _():
        for g in range(ATOM_Q // GROUP):
            if not at_ends(g):
                dense = dense_of(blocks[...], lists[0:1, :], lists[1:2, :], g * GROUP)
                put_dense(band, dense, g * GROUP, band)


def own_kernel(
    feat, src, dst, cell, near, cell_bias, w_in, w_out, _, band, w_in_t, bias_t, w_out_t, blk, blk2, bias8, rows, more, lists
):
    nblk = w_out.shape[1]
    w_in_t[...] = w_in[...].astype(F32).T.astype(BF)
    bias8[...] = jnp.zeros(bias8.shape, F32)
    bias8[0:3, :] = cell_bias[...].astype(F32)
    bias_t[...] = bias8[...].T.astype(BF)
    row, col = iota((nblk, nblk), 0), iota((nblk, nblk), 1)
    swap = (col == (row % ORB) * ORB + row // ORB).astype(BF)
    w_out_t[...] = nt_dot(swap, w_out[...]).astype(BF)
    own = feat.shape[0]
    ids = edge_ids(src[...], dst[...], cell[...])
    atom = row_of(ids[0])
    rows[0:1, :] = atom
    rows[1:2, :] = column_of(atom, row_of(ids[1]))
    is_left = device_side() == 1
    cells, any_middle = place(near, is_left, more, lists)
    blk[...] = pair_blocks(feat[...], row_of(ids[2]), w_in_t, bias_t, w_out_t)
    blk2[...] = pair_blocks(more[...], cells, w_in_t, bias_t, w_out_t)
    spans = []
    for first in range(0, ATOM_Q, GROUP):
        start = jnp.sum((ids[0] < float(first)).astype(F32)).astype(jnp.int32)
        spans.append(pl.ds(pl.multiple_of(jnp.minimum(start // 128 * 128, own - GROUP_SPAN), 128), GROUP_SPAN))
    for g, span in enumerate(spans):
        first = g * GROUP
        dense = dense_of(blk[:, span], rows[0:1, span], rows[1:2, span], first)
        if at_ends(g):
            dense = dense + dense_of(blk2[...], lists[0:1, :], lists[1:2, :], first)
        put_dense(band, dense, first)
    add_middle(band, blk2, lists, any_middle)


def spill_kernel(own_band, blue, w_in_t, bias_t, w_out_t, band, blk, more, lists):
    is_left = device_side() == 0
    cells, any_middle = place(blue, is_left, more, lists)
    blk[...] = pair_blocks(more[...], cells, w_in_t, bias_t, w_out_t)
    for g in range(ATOM_Q // GROUP):
        first = g * GROUP
        if at_ends(g):
            dense = dense_of(blk[...], lists[0:1, :], lists[1:2, :], first)
            put_dense(band, dense, first, own_band)
        else:
            pair, at = first // PAIR_ATOMS, first % PAIR_ATOMS * ORB
            band[pair, at : at + GROUP * ORB, :] = own_band[pair, at : at + GROUP * ORB, :]
    add_middle(band, blk, lists, any_middle)


def own_part(band, field):
    pieces = [field[pl.ds(q, ATOM_Q, stride=ORB), :].astype(BF) for q in range(ORB)]
    rhs = jnp.concatenate(pieces, axis=0)
    return [jnp.dot(band[k, :, :HALF], rhs, preferred_element_type=F32) for k in range(band.shape[0])]


def halo_part(band, blue, red, wide):
    even = device_side() == 0
    wide[0:HALO, :] = jnp.where(even, blue[...], red[...]).astype(F32)
    wide[HALO : 2 * HALO, :] = jnp.where(even, red[...], blue[...]).astype(F32)
    atoms = BAND * TILE_ATOMS
    pieces = [[], []]
    for q in range(ORB):
        left = wide[pl.ds(q, atoms, stride=ORB), :]
        right = wide[pl.ds(HALO + q, atoms, stride=ORB), :]
        pieces[0].append(jnp.concatenate([left, right[:TILE_ATOMS]], axis=0).astype(BF))
        pieces[1].append(jnp.concatenate([left[atoms - TILE_ATOMS :], right], axis=0).astype(BF))
    return [
        jnp.dot(band[k, :, HALF:], jnp.concatenate(pieces[k], axis=0), preferred_element_type=F32)
        for k in range(band.shape[0])
    ]


def put_sends(value_ref, to_blue, to_red):
    side = device_side()
    inner = value_ref.shape[0] - HALO
    off = pl.multiple_of(side * inner, 128)
    to_blue[...] = value_ref[pl.ds(off, HALO), :].astype(BF)
    to_red[...] = value_ref[pl.ds(pl.multiple_of(inner - off, 128), HALO), :].astype(BF)


def spans_of(band):
    height = band.shape[1]
    return [slice(k * height, (k + 1) * height) for k in range(band.shape[0])]


def start_kernel(band, now, part):
    inner = own_part(band, now)
    for k, span in enumerate(spans_of(band)):
        part[span, :] = inner[k]


def inner_kernel(band, before, now, part):
    inner = own_part(band, now)
    for k, span in enumerate(spans_of(band)):
        part[span, :] = 2.0 * inner[k] - before[span, :]


def outer_kernel(scale, band, part, blue, red, after, to_blue, to_red, wide):
    outer = halo_part(band, blue, red, wide)
    for k, span in enumerate(spans_of(band)):
        after[span, :] = scale * outer[k] + part[span, :]
    put_sends(after, to_blue, to_red)


def mix_kernel(coef, band, t0, t1, t2, t3, base, final):
    inner = own_part(band, t3)
    for k, span in enumerate(spans_of(band)):
        total = coef[0] * t0[span, :] + coef[1] * t1[span, :] + (coef[2] - coef[4]) * t2[span, :]
        total = total + coef[3] * t3[span, :] + 2.0 * coef[4] * inner[k]
        base[:, span] = total.T
    final[...] = jnp.full(final.shape, 2.0 * coef[4], F32)


def last_kernel(final, band, base, blue, red, p0, p1, p2, p3, wide, out):
    member = lax.axis_index("edges")
    outer = halo_part(band, blue, red, wide)
    for k, span in enumerate(spans_of(band)):
        out[:, span] = base[:, span] + (final[0:1, :] * outer[k]).T
    for k, piece in enumerate((p0, p1, p2, p3)):
        high = piece.shape[0]
        piece[...] = out[pl.ds(pl.multiple_of((member ^ k) * high, high), high), :].astype(BF)


def join_kernel(p0, p1, p2, p3, out):
    member = lax.axis_index("edges")
    for k, piece in enumerate((p0, p1, p2, p3)):
        width = piece.shape[1]
        at = pl.multiple_of((member ^ k) * width, width)
        out[:, pl.ds(at, width)] = piece[...].astype(F32)


VMEM = pl.BlockSpec(memory_space=pltpu.VMEM)
SMEM = pl.BlockSpec(memory_space=pltpu.SMEM)
IN_HBM = pl.BlockSpec(memory_space=pltpu.HBM)
FULL, PART = 60 * 1024 * 1024, 32 * 1024 * 1024


def shape(dims, dtype):
    return jax.ShapeDtypeStruct(dims, dtype)


def call(kernel, name, outs, scratch, *args, smem=(), in_hbm=(), out_hbm=(), alias=None, limit=PART, micros=1):
    spaces = [SMEM if k in smem else IN_HBM if k in in_hbm else VMEM for k in range(len(args))]
    return pl.pallas_call(
        kernel,
        name=name,
        out_shape=outs,
        in_specs=spaces,
        out_specs=tuple(IN_HBM if k in out_hbm else VMEM for k in range(len(outs))),
        scratch_shapes=scratch,
        input_output_aliases=alias or {},
        cost_estimate=pl.CostEstimate(flops=micros * 10**9, bytes_accessed=0, transcendentals=0),
        compiler_params=pltpu.CompilerParams(vmem_limit_bytes=limit),
    )(*args)


def per_device(features, edge_src, edge_dst, edge_cell, cell_bias, w_in, w_out, vectors, cheb_coef):
    axes = ("rows", "edges")
    nedge = lax.axis_size("edges")
    ndev = lax.axis_size("rows") * nedge
    red_pairs = [(i, i ^ 1) for i in range(ndev)]
    blue_pairs = [(i, (i + 1) % ndev if i % 2 else (i - 1) % ndev) for i in range(ndev)]
    nown, nfeat = features.shape
    high, ncol = vectors.shape
    nrow = ncol // nedge

    def swap(first, last):
        return (
            lax.ppermute(first, axes, blue_pairs),
            lax.ppermute(last, axes, red_pairs),
        )

    def exchange(pieces):
        return [pieces[0]] + [
            lax.ppermute(pieces[k], "edges", [(i, i ^ k) for i in range(nedge)]) for k in (1, 2, 3)
        ]

    msg = shape((SPILL + ID_ROWS, nfeat), BF)
    piece = shape((high, nrow), BF)
    lines = (nown // 128, 128)
    edges = [x.reshape(lines) for x in (edge_src, edge_dst, edge_cell)]
    near_msg = shape((SPILL + ID_ROWS + high * nrow // nfeat, nfeat), BF)
    own_piece, beside, straight, across = call(
        split_kernel, "split", (piece,) * 4, [], vectors, micros=1
    )
    blue_msg, near = call(
        message_kernel, "message", (msg, near_msg), [], features, *edges, beside, micros=0
    )
    across = lax.ppermute(across, "edges", [(i, i ^ 3) for i in range(nedge)])
    straight = lax.ppermute(straight, "edges", [(i, i ^ 2) for i in range(nedge)])
    near = lax.ppermute(near, axes, red_pairs)
    blue_msg = lax.ppermute(blue_msg, axes, blue_pairs)
    (across,) = call(pass_kernel, "pass", (piece,), [], across, micros=0)
    pieces = [own_piece, near, straight, across]
    full, part = shape((nrow, VEC), F32), shape((HALO, VEC), BF)
    t0, to_blue, to_red, token = call(
        field_kernel, "field", (full, part, part, shape((8, VEC), F32)), [pltpu.VMEM((VEC, nrow), F32)], *pieces
    )
    blue, red = swap(to_blue, to_red)

    wide_spill = SPILL + 64
    band_shape = shape((ATOM_Q // PAIR_ATOMS, PAIR_ATOMS * ORB, WIN_ATOMS * ORB), BF)
    width = w_in.shape[1]
    band, *weights = call(
        own_kernel,
        "own",
        (band_shape, shape((width, nfeat), BF), shape((width, 8), BF), shape((ORB * ORB, HID), BF)),
        [
            pltpu.VMEM((ORB * ORB, nown), BF),
            pltpu.VMEM((ORB * ORB, wide_spill), BF),
            pltpu.VMEM((8, width), F32),
            pltpu.VMEM((8, nown), F32),
            pltpu.VMEM((wide_spill, nfeat), BF),
            pltpu.VMEM((8, wide_spill), F32),
        ],
        features,
        *edges,
        near,
        cell_bias,
        w_in,
        w_out,
        token,
        micros=4,
    )
    (band,) = call(
        spill_kernel,
        "spill",
        (band_shape,),
        [
            pltpu.VMEM((ORB * ORB, wide_spill), BF),
            pltpu.VMEM((wide_spill, nfeat), BF),
            pltpu.VMEM((8, wide_spill), F32),
        ],
        band,
        blue_msg,
        *weights,
        alias={0: 0},
        micros=0,
    )

    wide = pltpu.VMEM((2 * HALO, VEC), F32)
    fields = [t0]
    for step in range(1, STEPS):
        if step > 1:
            blue, red = swap(to_blue, to_red)
        inner, name = (start_kernel, "start") if step == 1 else (inner_kernel, "inner")
        (inner,) = call(inner, name, (full,), [], band, *fields[-2:])
        following, to_blue, to_red = call(
            functools.partial(outer_kernel, 1.0 if step == 1 else 2.0),
            "outer",
            (full, part, part),
            [wide],
            band,
            inner,
            blue,
            red,
        )
        fields.append(following)
    blue, red = swap(to_blue, to_red)
    base, final = call(
        mix_kernel,
        "mix",
        (shape((VEC, nrow), F32), shape((8, VEC), F32)),
        [],
        cheb_coef,
        band,
        *fields,
        smem=(0,),
    )
    pieces = call(
        last_kernel,
        "last",
        (piece,) * 4,
        [wide, pltpu.VMEM((VEC, nrow), F32)],
        final,
        band,
        base,
        blue,
        red,
    )
    (result,) = call(join_kernel, "join", (shape((high, ncol), F32),), [], *exchange(pieces))
    return result


def solution(mesh):
    placed = (
        P(("rows", "edges"), None),
        P(("rows", "edges")),
        P(("rows", "edges")),
        P(("rows", "edges")),
        P(),
        P(),
        P(),
        P("edges", "rows"),
        P(),
    )
    return jax.shard_map(
        per_device, mesh=mesh, in_specs=placed, out_specs=P("edges", "rows"), check_vma=False
    )
```

```python
import functools

import jax
import jax.numpy as jnp
from jax import lax
from jax.experimental import pallas as pl
from jax.experimental.pallas import tpu as pltpu
from jax.sharding import PartitionSpec as P

ORB = 16
TILE_ATOMS = 8
BAND = 3
HID = 256
VEC = 128
STEPS = 4
ATOM_Q = 32
SPILL = 320
ID_ROWS = 16
PAIR_ATOMS = 2 * TILE_ATOMS
WIN_ATOMS = (2 * BAND + 2) * TILE_ATOMS
HALO = BAND * TILE_ATOMS * ORB
GROUP = 4
GROUP_SPAN = 384
HALF = ATOM_Q * ORB
NEAR = 3
BF = jnp.bfloat16
F32 = jnp.float32
NT = (((1,), (1,)), ((), ()))


def nt_dot(a, b):
    return lax.dot_general(a, b, NT, preferred_element_type=F32)


def iota(shape, dim):
    return lax.broadcasted_iota(jnp.int32, shape, dim)


def device_side():
    return (lax.axis_index("rows") * lax.axis_size("edges") + lax.axis_index("edges")) % 2


def edge_ids(src, dst, cell):
    ndev = lax.axis_size("rows") * lax.axis_size("edges")
    quarter = lax.axis_index("rows") * lax.axis_size("edges") + lax.axis_index("edges")
    natom = ATOM_Q * ndev
    ntiles = natom // TILE_ATOMS
    rel = src - quarter * ATOM_Q
    rel = jnp.where(rel > natom // 2, rel - natom, jnp.where(rel < -(natom // 2), rel + natom, rel))
    shift = (dst >> 3) - (src >> 3) + BAND
    shift = jnp.where(shift < 0, shift + ntiles, jnp.where(shift >= ntiles, shift - ntiles, shift))
    return [x.astype(F32) for x in (rel, shift * TILE_ATOMS + (dst & 7), cell)]


def tick_kernel(token):
    token[...] = jnp.zeros(token.shape, F32)


def split_kernel(vectors, _, src, dst, cell, p0, p1, p2, p3):
    member = lax.axis_index("edges")
    for k, piece in enumerate((p0, p1, p2, p3)):
        width = piece.shape[1]
        at = pl.multiple_of((member ^ k) * width, width)
        piece[...] = vectors[:, pl.ds(at, width)].astype(BF)


def message_kernel(feat, src, dst, cell, p1, blue, red):
    side = device_side()
    high_rows, width = p1.shape
    nfeat = feat.shape[1]
    high = feat.shape[0] - SPILL
    off = pl.multiple_of(side * high, 64)
    blue[0:SPILL, :] = feat[pl.ds(off, SPILL), :]
    red[0:SPILL, :] = feat[pl.ds(pl.multiple_of(high - off, 64), SPILL), :]
    three = edge_ids(src[...], dst[...], cell[...])
    lane, line = iota((3, 128), 1), iota((3, 128), 0)
    nrow = src.shape[0]
    starts = [x[0:3] for x in three]
    ends = [x[nrow - 3 : nrow] for x in three]
    starts[0] = jnp.where((line == 2) & (lane >= 64), -64.0, starts[0] + ATOM_Q)
    ends[0] = jnp.where((line == 0) & (lane < 64), -64.0, ends[0] - ATOM_Q)
    pad = jnp.zeros((ID_ROWS - 9, 128), F32)
    low_ids = jnp.concatenate(starts + [pad], axis=0)
    high_ids = jnp.concatenate(ends + [pad], axis=0)
    none = jnp.zeros((ID_ROWS, 128), BF)
    for msg, ids_of in (
        (blue, jnp.where(side == 0, low_ids, high_ids)),
        (red, jnp.where(side == 0, high_ids, low_ids)),
    ):
        msg[SPILL : SPILL + ID_ROWS, 0:128] = ids_of.astype(BF)
        msg[SPILL : SPILL + ID_ROWS, 128:256] = none
    for n in range(width // nfeat):
        at = SPILL + ID_ROWS + n * high_rows
        red[at : at + high_rows, :] = p1[:, n * nfeat : (n + 1) * nfeat]


def pass_kernel(x, y):
    y[...] = x[...]


def field_kernel(p0, near, p2, p3, t0, to_blue, to_red, token, field):
    member = lax.axis_index("edges")
    high = p0.shape[0]
    for k, piece in ((0, p0), (2, p2), (3, p3)):
        field[pl.ds(pl.multiple_of((member ^ k) * high, high), high), :] = piece[...].astype(F32)
    rows = pl.ds(pl.multiple_of((member ^ 1) * high, high), high)
    width = near.shape[1]
    for n in range(field.shape[1] // width):
        at = SPILL + ID_ROWS + n * high
        field[rows, n * width : (n + 1) * width] = near[at : at + high, :].astype(F32)
    t0[...] = field[...].T
    token[...] = jnp.zeros(token.shape, F32)
    put_sends(t0, to_blue, to_red)


def pair_blocks(x, cell, w_in_t, bias_t, w_out_t):
    bias = [bias_t[:, k : k + 1].astype(F32) for k in range(3)]
    pre = nt_dot(w_in_t[...], x)
    pre = pre + jnp.where(cell == 1.0, bias[1], jnp.where(cell == 2.0, bias[2], bias[0]))
    gate, up = pre[:HID], pre[HID:]
    hidden = (gate * (0.5 + 0.5 * jnp.tanh(0.5 * gate)) * up).astype(BF)
    return jnp.dot(w_out_t[...], hidden, preferred_element_type=F32).astype(BF)


def row_of(x):
    return jnp.concatenate([x[k : k + 1] for k in range(x.shape[0])], axis=1)


def dense_of(blocks, atom, target, first):
    span = atom.shape[1]
    column = (iota((WIN_ATOMS, span), 0).astype(F32) == target).astype(BF)
    onehot = [
        jnp.broadcast_to((atom == as_float(first + s)).astype(F32), (WIN_ATOMS, span)).astype(BF) * column
        for s in range(GROUP)
    ]
    return nt_dot(blocks, jnp.concatenate(onehot, axis=0))


def put_dense(band, dense, first, base=None):
    lane = iota((ORB, 128), 1)
    low, even = lane < 64, lane % 64 < ATOM_Q
    for sp in range(GROUP // 2):
        s = first + 2 * sp
        pair, at_row = s // PAIR_ATOMS, s % PAIR_ATOMS * ORB
        if not isinstance(s, int):
            at_row = pl.multiple_of(at_row, 2 * ORB)
        for m in range(ORB // 4):
            x = [
                dense[(4 * m + i) * ORB : (4 * m + i + 1) * ORB, sp * 128 : sp * 128 + 128].astype(BF)
                for i in range(4)
            ]
            for half in range(2):
                if half == 0:
                    u = [jnp.where(low, x[i], pltpu.roll(x[i + 2], 64, 1)) for i in range(2)]
                else:
                    u = [jnp.where(low, pltpu.roll(x[i], 64, 1), x[i + 2]) for i in range(2)]
                both = (
                    jnp.where(even, u[0], pltpu.roll(u[1], ATOM_Q, 1)),
                    jnp.where(even, pltpu.roll(u[0], 128 - ATOM_Q, 1), u[1]),
                )
                rows = pl.ds(at_row + half * ORB, ORB)
                for n, value in enumerate(both):
                    lo = n * HALF + m * 128
                    if base is not None:
                        value = value + base[pair, rows, lo : lo + 128]
                    band[pair, rows, lo : lo + 128] = value


def column_of(atom, offset):
    target = TILE_ATOMS * (jnp.floor(atom * (1.0 / TILE_ATOMS)) - BAND) + offset
    base = BAND * TILE_ATOMS - PAIR_ATOMS * jnp.floor(atom * (1.0 / PAIR_ATOMS))
    outside = jnp.where(target < 0.0, target + (base + ATOM_Q), target + base)
    return jnp.where((target >= 0.0) & (target < float(ATOM_Q)), target, outside)


def as_float(x):
    return float(x) if isinstance(x, int) else x.astype(F32)


def place(message, is_left, rows, lists):
    nfeat = rows.shape[1]
    gap = rows.shape[0] - SPILL
    rows[0:gap, :] = jnp.zeros((gap, nfeat), BF)
    rows[SPILL : SPILL + gap, :] = jnp.zeros((gap, nfeat), BF)
    rows[pl.ds(pl.multiple_of(jnp.where(is_left, gap, 0), 64), SPILL), :] = message[0:SPILL, :]
    block = message[SPILL : SPILL + ID_ROWS, 0:128].astype(F32)
    atom, offset, cell = [row_of(block[3 * k : 3 * k + 3]) for k in range(3)]
    lists[0:1, :] = atom
    lists[1:2, :] = column_of(atom, offset)
    middle = (atom >= float(NEAR * GROUP)) & (atom < float(ATOM_Q - NEAR * GROUP))
    return cell, jnp.max(jnp.where(middle, 1.0, 0.0)) > 0.5


def at_ends(g):
    return g < NEAR or g >= ATOM_Q // GROUP - NEAR


def add_middle(band, blocks, lists, any_middle):
    @pl.when(any_middle)
    def _():
        for g in range(ATOM_Q // GROUP):
            if not at_ends(g):
                dense = dense_of(blocks[...], lists[0:1, :], lists[1:2, :], g * GROUP)
                put_dense(band, dense, g * GROUP, band)


def own_kernel(
    feat, src, dst, cell, near, cell_bias, w_in, w_out, _, band, w_in_t, bias_t, w_out_t, blk, blk2, bias8, rows, more, lists
):
    nblk = w_out.shape[1]
    w_in_t[...] = w_in[...].astype(F32).T.astype(BF)
    bias8[...] = jnp.zeros(bias8.shape, F32)
    bias8[0:3, :] = cell_bias[...].astype(F32)
    bias_t[...] = bias8[...].T.astype(BF)
    row, col = iota((nblk, nblk), 0), iota((nblk, nblk), 1)
    swap = (col == (row % ORB) * ORB + row // ORB).astype(BF)
    w_out_t[...] = nt_dot(swap, w_out[...]).astype(BF)
    own = feat.shape[0]
    ids = edge_ids(src[...], dst[...], cell[...])
    atom = row_of(ids[0])
    rows[0:1, :] = atom
    rows[1:2, :] = column_of(atom, row_of(ids[1]))
    is_left = device_side() == 1
    cells, any_middle = place(near, is_left, more, lists)
    blk[...] = pair_blocks(feat[...], row_of(ids[2]), w_in_t, bias_t, w_out_t)
    blk2[...] = pair_blocks(more[...], cells, w_in_t, bias_t, w_out_t)
    spans = []
    for first in range(0, ATOM_Q, GROUP):
        start = jnp.sum((ids[0] < float(first)).astype(F32)).astype(jnp.int32)
        spans.append(pl.ds(pl.multiple_of(jnp.minimum(start // 128 * 128, own - GROUP_SPAN), 128), GROUP_SPAN))
    for g, span in enumerate(spans):
        first = g * GROUP
        dense = dense_of(blk[:, span], rows[0:1, span], rows[1:2, span], first)
        if at_ends(g):
            dense = dense + dense_of(blk2[...], lists[0:1, :], lists[1:2, :], first)
        put_dense(band, dense, first)
    add_middle(band, blk2, lists, any_middle)


def spill_kernel(own_band, blue, w_in_t, bias_t, w_out_t, band, blk, more, lists):
    is_left = device_side() == 0
    cells, any_middle = place(blue, is_left, more, lists)
    blk[...] = pair_blocks(more[...], cells, w_in_t, bias_t, w_out_t)
    for g in range(ATOM_Q // GROUP):
        first = g * GROUP
        if at_ends(g):
            dense = dense_of(blk[...], lists[0:1, :], lists[1:2, :], first)
            put_dense(band, dense, first, own_band)
        else:
            pair, at = first // PAIR_ATOMS, first % PAIR_ATOMS * ORB
            band[pair, at : at + GROUP * ORB, :] = own_band[pair, at : at + GROUP * ORB, :]
    add_middle(band, blk, lists, any_middle)


def own_part(band, field):
    pieces = [field[pl.ds(q, ATOM_Q, stride=ORB), :].astype(BF) for q in range(ORB)]
    rhs = jnp.concatenate(pieces, axis=0)
    return [jnp.dot(band[k, :, :HALF], rhs, preferred_element_type=F32) for k in range(band.shape[0])]


def halo_part(band, blue, red, wide):
    even = device_side() == 0
    wide[0:HALO, :] = jnp.where(even, blue[...], red[...]).astype(F32)
    wide[HALO : 2 * HALO, :] = jnp.where(even, red[...], blue[...]).astype(F32)
    atoms = BAND * TILE_ATOMS
    pieces = [[], []]
    for q in range(ORB):
        left = wide[pl.ds(q, atoms, stride=ORB), :]
        right = wide[pl.ds(HALO + q, atoms, stride=ORB), :]
        pieces[0].append(jnp.concatenate([left, right[:TILE_ATOMS]], axis=0).astype(BF))
        pieces[1].append(jnp.concatenate([left[atoms - TILE_ATOMS :], right], axis=0).astype(BF))
    return [
        jnp.dot(band[k, :, HALF:], jnp.concatenate(pieces[k], axis=0), preferred_element_type=F32)
        for k in range(band.shape[0])
    ]


def put_sends(value_ref, to_blue, to_red):
    side = device_side()
    inner = value_ref.shape[0] - HALO
    off = pl.multiple_of(side * inner, 128)
    to_blue[...] = value_ref[pl.ds(off, HALO), :].astype(BF)
    to_red[...] = value_ref[pl.ds(pl.multiple_of(inner - off, 128), HALO), :].astype(BF)


def spans_of(band):
    height = band.shape[1]
    return [slice(k * height, (k + 1) * height) for k in range(band.shape[0])]


def start_kernel(band, now, part):
    inner = own_part(band, now)
    for k, span in enumerate(spans_of(band)):
        part[span, :] = inner[k]


def inner_kernel(band, before, now, part):
    inner = own_part(band, now)
    for k, span in enumerate(spans_of(band)):
        part[span, :] = 2.0 * inner[k] - before[span, :]


def outer_kernel(scale, band, part, blue, red, after, to_blue, to_red, wide):
    outer = halo_part(band, blue, red, wide)
    for k, span in enumerate(spans_of(band)):
        after[span, :] = scale * outer[k] + part[span, :]
    put_sends(after, to_blue, to_red)


def mix_kernel(coef, band, t0, t1, t2, t3, base, final):
    inner = own_part(band, t3)
    for k, span in enumerate(spans_of(band)):
        total = coef[0] * t0[span, :] + coef[1] * t1[span, :] + (coef[2] - coef[4]) * t2[span, :]
        total = total + coef[3] * t3[span, :] + 2.0 * coef[4] * inner[k]
        base[:, span] = total.T
    final[...] = jnp.full(final.shape, 2.0 * coef[4], F32)


def last_kernel(final, band, base, blue, red, p0, p1, p2, p3, wide, out):
    member = lax.axis_index("edges")
    outer = halo_part(band, blue, red, wide)
    for k, span in enumerate(spans_of(band)):
        out[:, span] = base[:, span] + (final[0:1, :] * outer[k]).T
    for k, piece in enumerate((p0, p1, p2, p3)):
        high = piece.shape[0]
        piece[...] = out[pl.ds(pl.multiple_of((member ^ k) * high, high), high), :].astype(BF)


def join_kernel(p0, p1, p2, p3, out):
    member = lax.axis_index("edges")
    for k, piece in enumerate((p0, p1, p2, p3)):
        width = piece.shape[1]
        at = pl.multiple_of((member ^ k) * width, width)
        out[:, pl.ds(at, width)] = piece[...].astype(F32)


VMEM = pl.BlockSpec(memory_space=pltpu.VMEM)
SMEM = pl.BlockSpec(memory_space=pltpu.SMEM)
IN_HBM = pl.BlockSpec(memory_space=pltpu.HBM)
FULL, PART = 60 * 1024 * 1024, 32 * 1024 * 1024


def shape(dims, dtype):
    return jax.ShapeDtypeStruct(dims, dtype)


def call(kernel, name, outs, scratch, *args, smem=(), in_hbm=(), out_hbm=(), alias=None, limit=PART, micros=1):
    spaces = [SMEM if k in smem else IN_HBM if k in in_hbm else VMEM for k in range(len(args))]
    return pl.pallas_call(
        kernel,
        name=name,
        out_shape=outs,
        in_specs=spaces,
        out_specs=tuple(IN_HBM if k in out_hbm else VMEM for k in range(len(outs))),
        scratch_shapes=scratch,
        input_output_aliases=alias or {},
        cost_estimate=pl.CostEstimate(flops=micros * 10**9, bytes_accessed=0, transcendentals=0),
        compiler_params=pltpu.CompilerParams(vmem_limit_bytes=limit),
    )(*args)


def per_device(features, edge_src, edge_dst, edge_cell, cell_bias, w_in, w_out, vectors, cheb_coef):
    axes = ("rows", "edges")
    nedge = lax.axis_size("edges")
    ndev = lax.axis_size("rows") * nedge
    red_pairs = [(i, i ^ 1) for i in range(ndev)]
    blue_pairs = [(i, (i + 1) % ndev if i % 2 else (i - 1) % ndev) for i in range(ndev)]
    nown, nfeat = features.shape
    high, ncol = vectors.shape
    nrow = ncol // nedge

    def swap(first, last):
        return (
            lax.ppermute(first, axes, blue_pairs),
            lax.ppermute(last, axes, red_pairs),
        )

    def exchange(pieces):
        return [pieces[0]] + [
            lax.ppermute(pieces[k], "edges", [(i, i ^ k) for i in range(nedge)]) for k in (1, 2, 3)
        ]

    msg = shape((SPILL + ID_ROWS, nfeat), BF)
    piece = shape((high, nrow), BF)
    lines = (nown // 128, 128)
    edges = [x.reshape(lines) for x in (edge_src, edge_dst, edge_cell)]
    near_msg = shape((SPILL + ID_ROWS + high * nrow // nfeat, nfeat), BF)
    (tick,) = call(tick_kernel, "tick", (shape((8, VEC), F32),), [], micros=5)
    own_piece, beside, straight, across = call(
        split_kernel, "split", (piece,) * 4, [], vectors, tick, *edges, micros=0
    )
    blue_msg, near = call(
        message_kernel, "message", (msg, near_msg), [], features, *edges, beside, micros=0
    )
    across = lax.ppermute(across, "edges", [(i, i ^ 3) for i in range(nedge)])
    straight = lax.ppermute(straight, "edges", [(i, i ^ 2) for i in range(nedge)])
    near = lax.ppermute(near, axes, red_pairs)
    blue_msg = lax.ppermute(blue_msg, axes, blue_pairs)
    (across,) = call(pass_kernel, "pass", (piece,), [], across, micros=0)
    pieces = [own_piece, near, straight, across]
    full, part = shape((nrow, VEC), F32), shape((HALO, VEC), BF)
    t0, to_blue, to_red, token = call(
        field_kernel, "field", (full, part, part, shape((8, VEC), F32)), [pltpu.VMEM((VEC, nrow), F32)], *pieces
    )
    blue, red = swap(to_blue, to_red)

    wide_spill = SPILL + 64
    band_shape = shape((ATOM_Q // PAIR_ATOMS, PAIR_ATOMS * ORB, WIN_ATOMS * ORB), BF)
    width = w_in.shape[1]
    band, *weights = call(
        own_kernel,
        "own",
        (band_shape, shape((width, nfeat), BF), shape((width, 8), BF), shape((ORB * ORB, HID), BF)),
        [
            pltpu.VMEM((ORB * ORB, nown), BF),
            pltpu.VMEM((ORB * ORB, wide_spill), BF),
            pltpu.VMEM((8, width), F32),
            pltpu.VMEM((8, nown), F32),
            pltpu.VMEM((wide_spill, nfeat), BF),
            pltpu.VMEM((8, wide_spill), F32),
        ],
        features,
        *edges,
        near,
        cell_bias,
        w_in,
        w_out,
        token,
        micros=4,
    )
    (band,) = call(
        spill_kernel,
        "spill",
        (band_shape,),
        [
            pltpu.VMEM((ORB * ORB, wide_spill), BF),
            pltpu.VMEM((wide_spill, nfeat), BF),
            pltpu.VMEM((8, wide_spill), F32),
        ],
        band,
        blue_msg,
        *weights,
        alias={0: 0},
        micros=0,
    )

    wide = pltpu.VMEM((2 * HALO, VEC), F32)
    fields = [t0]
    for step in range(1, STEPS):
        if step > 1:
            blue, red = swap(to_blue, to_red)
        inner, name = (start_kernel, "start") if step == 1 else (inner_kernel, "inner")
        (inner,) = call(inner, name, (full,), [], band, *fields[-2:])
        following, to_blue, to_red = call(
            functools.partial(outer_kernel, 1.0 if step == 1 else 2.0),
            "outer",
            (full, part, part),
            [wide],
            band,
            inner,
            blue,
            red,
        )
        fields.append(following)
    blue, red = swap(to_blue, to_red)
    base, final = call(
        mix_kernel,
        "mix",
        (shape((VEC, nrow), F32), shape((8, VEC), F32)),
        [],
        cheb_coef,
        band,
        *fields,
        smem=(0,),
    )
    pieces = call(
        last_kernel,
        "last",
        (piece,) * 4,
        [wide, pltpu.VMEM((VEC, nrow), F32)],
        final,
        band,
        base,
        blue,
        red,
    )
    (result,) = call(join_kernel, "join", (shape((high, ncol), F32),), [], *exchange(pieces))
    return result


def solution(mesh):
    placed = (
        P(("rows", "edges"), None),
        P(("rows", "edges")),
        P(("rows", "edges")),
        P(("rows", "edges")),
        P(),
        P(),
        P(),
        P("edges", "rows"),
        P(),
    )
    return jax.shard_map(
        per_device, mesh=mesh, in_specs=placed, out_specs=P("edges", "rows"), check_vma=False
    )
```

```python
import functools

import jax
import jax.numpy as jnp
from jax import lax
from jax.experimental import pallas as pl
from jax.experimental.pallas import tpu as pltpu
from jax.sharding import PartitionSpec as P

ORB = 16
TILE_ATOMS = 8
BAND = 3
HID = 256
VEC = 128
STEPS = 4
ATOM_Q = 32
SPILL = 320
ID_ROWS = 16
PAIR_ATOMS = 2 * TILE_ATOMS
WIN_ATOMS = (2 * BAND + 2) * TILE_ATOMS
HALO = BAND * TILE_ATOMS * ORB
GROUP = 4
GROUP_SPAN = 384
HALF = ATOM_Q * ORB
NEAR = 3
BF = jnp.bfloat16
F32 = jnp.float32
NT = (((1,), (1,)), ((), ()))


def nt_dot(a, b):
    return lax.dot_general(a, b, NT, preferred_element_type=F32)


def iota(shape, dim):
    return lax.broadcasted_iota(jnp.int32, shape, dim)


def device_side():
    return (lax.axis_index("rows") * lax.axis_size("edges") + lax.axis_index("edges")) % 2


def edge_ids(src, dst, cell):
    ndev = lax.axis_size("rows") * lax.axis_size("edges")
    quarter = lax.axis_index("rows") * lax.axis_size("edges") + lax.axis_index("edges")
    natom = ATOM_Q * ndev
    ntiles = natom // TILE_ATOMS
    rel = src - quarter * ATOM_Q
    rel = jnp.where(rel > natom // 2, rel - natom, jnp.where(rel < -(natom // 2), rel + natom, rel))
    shift = (dst >> 3) - (src >> 3) + BAND
    shift = jnp.where(shift < 0, shift + ntiles, jnp.where(shift >= ntiles, shift - ntiles, shift))
    return [x.astype(F32) for x in (rel, shift * TILE_ATOMS + (dst & 7), cell)]


def tick_kernel(token):
    token[...] = jnp.zeros(token.shape, F32)


def split_kernel(vectors, _, src, dst, cell, p0, p1, p2, p3):
    member = lax.axis_index("edges")
    for k, piece in enumerate((p0, p1, p2, p3)):
        width = piece.shape[1]
        at = pl.multiple_of((member ^ k) * width, width)
        piece[...] = vectors[:, pl.ds(at, width)].astype(BF)


def message_kernel(feat, src, dst, cell, p1, blue, red):
    side = device_side()
    high_rows, width = p1.shape
    nfeat = feat.shape[1]
    high = feat.shape[0] - SPILL
    off = pl.multiple_of(side * high, 64)
    blue[0:SPILL, :] = feat[pl.ds(off, SPILL), :]
    red[0:SPILL, :] = feat[pl.ds(pl.multiple_of(high - off, 64), SPILL), :]
    three = edge_ids(src[...], dst[...], cell[...])
    lane, line = iota((3, 128), 1), iota((3, 128), 0)
    nrow = src.shape[0]
    starts = [x[0:3] for x in three]
    ends = [x[nrow - 3 : nrow] for x in three]
    starts[0] = jnp.where((line == 2) & (lane >= 64), -64.0, starts[0] + ATOM_Q)
    ends[0] = jnp.where((line == 0) & (lane < 64), -64.0, ends[0] - ATOM_Q)
    pad = jnp.zeros((ID_ROWS - 9, 128), F32)
    low_ids = jnp.concatenate(starts + [pad], axis=0)
    high_ids = jnp.concatenate(ends + [pad], axis=0)
    none = jnp.zeros((ID_ROWS, 128), BF)
    for msg, ids_of in (
        (blue, jnp.where(side == 0, low_ids, high_ids)),
        (red, jnp.where(side == 0, high_ids, low_ids)),
    ):
        msg[SPILL : SPILL + ID_ROWS, 0:128] = ids_of.astype(BF)
        msg[SPILL : SPILL + ID_ROWS, 128:256] = none
    for n in range(width // nfeat):
        at = SPILL + ID_ROWS + n * high_rows
        red[at : at + high_rows, :] = p1[:, n * nfeat : (n + 1) * nfeat]


def pass_kernel(x, y):
    y[...] = x[...]


def field_kernel(p0, near, p2, p3, t0, to_blue, to_red, token, field):
    member = lax.axis_index("edges")
    high = p0.shape[0]
    for k, piece in ((0, p0), (2, p2), (3, p3)):
        field[pl.ds(pl.multiple_of((member ^ k) * high, high), high), :] = piece[...].astype(F32)
    rows = pl.ds(pl.multiple_of((member ^ 1) * high, high), high)
    width = near.shape[1]
    for n in range(field.shape[1] // width):
        at = SPILL + ID_ROWS + n * high
        field[rows, n * width : (n + 1) * width] = near[at : at + high, :].astype(F32)
    t0[...] = field[...].T
    token[...] = jnp.zeros(token.shape, F32)
    put_sends(t0, to_blue, to_red)


def pair_blocks(x, cell, w_in_t, bias_t, w_out_t):
    bias = [bias_t[:, k : k + 1].astype(F32) for k in range(3)]
    pre = nt_dot(w_in_t[...], x)
    pre = pre + jnp.where(cell == 1.0, bias[1], jnp.where(cell == 2.0, bias[2], bias[0]))
    gate, up = pre[:HID], pre[HID:]
    hidden = (gate * (0.5 + 0.5 * jnp.tanh(0.5 * gate)) * up).astype(BF)
    return jnp.dot(w_out_t[...], hidden, preferred_element_type=F32).astype(BF)


def row_of(x):
    return jnp.concatenate([x[k : k + 1] for k in range(x.shape[0])], axis=1)


def dense_of(blocks, atom, target, first):
    span = atom.shape[1]
    column = (iota((WIN_ATOMS, span), 0).astype(F32) == target).astype(BF)
    onehot = [
        jnp.broadcast_to((atom == as_float(first + s)).astype(F32), (WIN_ATOMS, span)).astype(BF) * column
        for s in range(GROUP)
    ]
    return nt_dot(blocks, jnp.concatenate(onehot, axis=0))


def put_dense(band, dense, first, base=None):
    lane = iota((ORB, 128), 1)
    low, even = lane < 64, lane % 64 < ATOM_Q
    for sp in range(GROUP // 2):
        s = first + 2 * sp
        pair, at_row = s // PAIR_ATOMS, s % PAIR_ATOMS * ORB
        if not isinstance(s, int):
            at_row = pl.multiple_of(at_row, 2 * ORB)
        for m in range(ORB // 4):
            x = [
                dense[(4 * m + i) * ORB : (4 * m + i + 1) * ORB, sp * 128 : sp * 128 + 128].astype(BF)
                for i in range(4)
            ]
            for half in range(2):
                if half == 0:
                    u = [jnp.where(low, x[i], pltpu.roll(x[i + 2], 64, 1)) for i in range(2)]
                else:
                    u = [jnp.where(low, pltpu.roll(x[i], 64, 1), x[i + 2]) for i in range(2)]
                both = (
                    jnp.where(even, u[0], pltpu.roll(u[1], ATOM_Q, 1)),
                    jnp.where(even, pltpu.roll(u[0], 128 - ATOM_Q, 1), u[1]),
                )
                rows = pl.ds(at_row + half * ORB, ORB)
                for n, value in enumerate(both):
                    lo = n * HALF + m * 128
                    if base is not None:
                        value = value + base[pair, rows, lo : lo + 128]
                    band[pair, rows, lo : lo + 128] = value


def column_of(atom, offset):
    target = TILE_ATOMS * (jnp.floor(atom * (1.0 / TILE_ATOMS)) - BAND) + offset
    base = BAND * TILE_ATOMS - PAIR_ATOMS * jnp.floor(atom * (1.0 / PAIR_ATOMS))
    outside = jnp.where(target < 0.0, target + (base + ATOM_Q), target + base)
    return jnp.where((target >= 0.0) & (target < float(ATOM_Q)), target, outside)


def as_float(x):
    return float(x) if isinstance(x, int) else x.astype(F32)


def place(message, is_left, rows, lists):
    nfeat = rows.shape[1]
    gap = rows.shape[0] - SPILL
    rows[0:gap, :] = jnp.zeros((gap, nfeat), BF)
    rows[SPILL : SPILL + gap, :] = jnp.zeros((gap, nfeat), BF)
    rows[pl.ds(pl.multiple_of(jnp.where(is_left, gap, 0), 64), SPILL), :] = message[0:SPILL, :]
    block = message[SPILL : SPILL + ID_ROWS, 0:128].astype(F32)
    atom, offset, cell = [row_of(block[3 * k : 3 * k + 3]) for k in range(3)]
    lists[0:1, :] = atom
    lists[1:2, :] = column_of(atom, offset)
    middle = (atom >= float(NEAR * GROUP)) & (atom < float(ATOM_Q - NEAR * GROUP))
    return cell, jnp.max(jnp.where(middle, 1.0, 0.0)) > 0.5


def at_ends(g):
    return g < NEAR or g >= ATOM_Q // GROUP - NEAR


def add_middle(band, blocks, lists, any_middle):
    @pl.when(any_middle)
    def _():
        for g in range(ATOM_Q // GROUP):
            if not at_ends(g):
                dense = dense_of(blocks[...], lists[0:1, :], lists[1:2, :], g * GROUP)
                put_dense(band, dense, g * GROUP, band)


def own_kernel(
    feat, src, dst, cell, near, cell_bias, w_in, w_out, _, band, w_in_t, bias_t, w_out_t, blk, blk2, bias8, rows, more, lists
):
    nblk = w_out.shape[1]
    w_in_t[...] = w_in[...].astype(F32).T.astype(BF)
    bias8[...] = jnp.zeros(bias8.shape, F32)
    bias8[0:3, :] = cell_bias[...].astype(F32)
    bias_t[...] = bias8[...].T.astype(BF)
    row, col = iota((nblk, nblk), 0), iota((nblk, nblk), 1)
    swap = (col == (row % ORB) * ORB + row // ORB).astype(BF)
    w_out_t[...] = nt_dot(swap, w_out[...]).astype(BF)
    own = feat.shape[0]
    ids = edge_ids(src[...], dst[...], cell[...])
    atom = row_of(ids[0])
    rows[0:1, :] = atom
    rows[1:2, :] = column_of(atom, row_of(ids[1]))
    is_left = device_side() == 1
    cells, any_middle = place(near, is_left, more, lists)
    blk[...] = pair_blocks(feat[...], row_of(ids[2]), w_in_t, bias_t, w_out_t)
    blk2[...] = pair_blocks(more[...], cells, w_in_t, bias_t, w_out_t)
    spans = []
    for first in range(0, ATOM_Q, GROUP):
        start = jnp.sum((ids[0] < float(first)).astype(F32)).astype(jnp.int32)
        spans.append(pl.ds(pl.multiple_of(jnp.minimum(start // 128 * 128, own - GROUP_SPAN), 128), GROUP_SPAN))
    for g, span in enumerate(spans):
        first = g * GROUP
        dense = dense_of(blk[:, span], rows[0:1, span], rows[1:2, span], first)
        if at_ends(g):
            dense = dense + dense_of(blk2[...], lists[0:1, :], lists[1:2, :], first)
        put_dense(band, dense, first)
    add_middle(band, blk2, lists, any_middle)


def spill_kernel(own_band, blue, w_in_t, bias_t, w_out_t, band, blk, more, lists):
    is_left = device_side() == 0
    cells, any_middle = place(blue, is_left, more, lists)
    blk[...] = pair_blocks(more[...], cells, w_in_t, bias_t, w_out_t)
    for g in range(ATOM_Q // GROUP):
        first = g * GROUP
        if at_ends(g):
            dense = dense_of(blk[...], lists[0:1, :], lists[1:2, :], first)
            put_dense(band, dense, first, own_band)
        else:
            pair, at = first // PAIR_ATOMS, first % PAIR_ATOMS * ORB
            band[pair, at : at + GROUP * ORB, :] = own_band[pair, at : at + GROUP * ORB, :]
    add_middle(band, blk, lists, any_middle)


def own_part(band, field):
    pieces = [field[pl.ds(q, ATOM_Q, stride=ORB), :].astype(BF) for q in range(ORB)]
    rhs = jnp.concatenate(pieces, axis=0)
    return [jnp.dot(band[k, :, :HALF], rhs, preferred_element_type=F32) for k in range(band.shape[0])]


def halo_part(band, blue, red, wide):
    off = pl.multiple_of(device_side() * HALO, HALO)
    wide[pl.ds(off, HALO), :] = blue[...].astype(F32)
    wide[pl.ds(pl.multiple_of(HALO - off, HALO), HALO), :] = red[...].astype(F32)
    atoms = BAND * TILE_ATOMS
    pieces = [[], []]
    for q in range(ORB):
        left = wide[pl.ds(q, atoms, stride=ORB), :]
        right = wide[pl.ds(HALO + q, atoms, stride=ORB), :]
        pieces[0].append(jnp.concatenate([left, right[:TILE_ATOMS]], axis=0).astype(BF))
        pieces[1].append(jnp.concatenate([left[atoms - TILE_ATOMS :], right], axis=0).astype(BF))
    return [
        jnp.dot(band[k, :, HALF:], jnp.concatenate(pieces[k], axis=0), preferred_element_type=F32)
        for k in range(band.shape[0])
    ]


def put_sends(value_ref, to_blue, to_red):
    side = device_side()
    inner = value_ref.shape[0] - HALO
    off = pl.multiple_of(side * inner, 128)
    to_blue[...] = value_ref[pl.ds(off, HALO), :].astype(BF)
    to_red[...] = value_ref[pl.ds(pl.multiple_of(inner - off, 128), HALO), :].astype(BF)


def spans_of(band):
    height = band.shape[1]
    return [slice(k * height, (k + 1) * height) for k in range(band.shape[0])]


def start_kernel(band, now, part):
    inner = own_part(band, now)
    for k, span in enumerate(spans_of(band)):
        part[span, :] = inner[k]


def inner_kernel(band, before, now, part):
    inner = own_part(band, now)
    for k, span in enumerate(spans_of(band)):
        part[span, :] = 2.0 * inner[k] - before[span, :]


def outer_kernel(scale, band, part, blue, red, after, to_blue, to_red, wide):
    outer = halo_part(band, blue, red, wide)
    for k, span in enumerate(spans_of(band)):
        after[span, :] = scale * outer[k] + part[span, :]
    put_sends(after, to_blue, to_red)


def mix_kernel(coef, band, t0, t1, t2, t3, base, final):
    inner = own_part(band, t3)
    for k, span in enumerate(spans_of(band)):
        total = coef[0] * t0[span, :] + coef[1] * t1[span, :] + (coef[2] - coef[4]) * t2[span, :]
        total = total + coef[3] * t3[span, :] + 2.0 * coef[4] * inner[k]
        base[:, span] = total.T
    final[...] = jnp.full(final.shape, 2.0 * coef[4], F32)


def last_kernel(final, band, base, blue, red, p0, p1, p2, p3, wide, out):
    member = lax.axis_index("edges")
    outer = halo_part(band, blue, red, wide)
    for k, span in enumerate(spans_of(band)):
        out[:, span] = base[:, span] + (final[0:1, :] * outer[k]).T
    for k, piece in enumerate((p0, p1, p2, p3)):
        high = piece.shape[0]
        piece[...] = out[pl.ds(pl.multiple_of((member ^ k) * high, high), high), :].astype(BF)


def join_kernel(p0, p1, p2, p3, out):
    member = lax.axis_index("edges")
    for k, piece in enumerate((p0, p1, p2, p3)):
        width = piece.shape[1]
        at = pl.multiple_of((member ^ k) * width, width)
        out[:, pl.ds(at, width)] = piece[...].astype(F32)


VMEM = pl.BlockSpec(memory_space=pltpu.VMEM)
SMEM = pl.BlockSpec(memory_space=pltpu.SMEM)
IN_HBM = pl.BlockSpec(memory_space=pltpu.HBM)
FULL, PART = 60 * 1024 * 1024, 32 * 1024 * 1024


def shape(dims, dtype):
    return jax.ShapeDtypeStruct(dims, dtype)


def call(kernel, name, outs, scratch, *args, smem=(), in_hbm=(), out_hbm=(), alias=None, limit=PART, micros=1):
    spaces = [SMEM if k in smem else IN_HBM if k in in_hbm else VMEM for k in range(len(args))]
    return pl.pallas_call(
        kernel,
        name=name,
        out_shape=outs,
        in_specs=spaces,
        out_specs=tuple(IN_HBM if k in out_hbm else VMEM for k in range(len(outs))),
        scratch_shapes=scratch,
        input_output_aliases=alias or {},
        cost_estimate=pl.CostEstimate(flops=micros * 10**9, bytes_accessed=0, transcendentals=0),
        compiler_params=pltpu.CompilerParams(vmem_limit_bytes=limit),
    )(*args)


def per_device(features, edge_src, edge_dst, edge_cell, cell_bias, w_in, w_out, vectors, cheb_coef):
    axes = ("rows", "edges")
    nedge = lax.axis_size("edges")
    ndev = lax.axis_size("rows") * nedge
    red_pairs = [(i, i ^ 1) for i in range(ndev)]
    blue_pairs = [(i, (i + 1) % ndev if i % 2 else (i - 1) % ndev) for i in range(ndev)]
    nown, nfeat = features.shape
    high, ncol = vectors.shape
    nrow = ncol // nedge

    def swap(first, last):
        return (
            lax.ppermute(first, axes, blue_pairs),
            lax.ppermute(last, axes, red_pairs),
        )

    def exchange(pieces):
        return [pieces[0]] + [
            lax.ppermute(pieces[k], "edges", [(i, i ^ k) for i in range(nedge)]) for k in (3, 2, 1)
        ][::-1]

    msg = shape((SPILL + ID_ROWS, nfeat), BF)
    piece = shape((high, nrow), BF)
    lines = (nown // 128, 128)
    edges = [x.reshape(lines) for x in (edge_src, edge_dst, edge_cell)]
    near_msg = shape((SPILL + ID_ROWS + high * nrow // nfeat, nfeat), BF)
    (tick,) = call(tick_kernel, "tick", (shape((8, VEC), F32),), [], micros=5)
    own_piece, beside, straight, across = call(
        split_kernel, "split", (piece,) * 4, [], vectors, tick, *edges, micros=0
    )
    blue_msg, near = call(
        message_kernel, "message", (msg, near_msg), [], features, *edges, beside, micros=0
    )
    across = lax.ppermute(across, "edges", [(i, i ^ 3) for i in range(nedge)])
    straight = lax.ppermute(straight, "edges", [(i, i ^ 2) for i in range(nedge)])
    near = lax.ppermute(near, axes, red_pairs)
    blue_msg = lax.ppermute(blue_msg, axes, blue_pairs)
    (across,) = call(pass_kernel, "pass", (piece,), [], across, micros=0)
    pieces = [own_piece, near, straight, across]
    full, part = shape((nrow, VEC), F32), shape((HALO, VEC), BF)
    t0, to_blue, to_red, token = call(
        field_kernel, "field", (full, part, part, shape((8, VEC), F32)), [pltpu.VMEM((VEC, nrow), F32)], *pieces
    )
    blue, red = swap(to_blue, to_red)

    wide_spill = SPILL + 64
    band_shape = shape((ATOM_Q // PAIR_ATOMS, PAIR_ATOMS * ORB, WIN_ATOMS * ORB), BF)
    width = w_in.shape[1]
    band, *weights = call(
        own_kernel,
        "own",
        (band_shape, shape((width, nfeat), BF), shape((width, 8), BF), shape((ORB * ORB, HID), BF)),
        [
            pltpu.VMEM((ORB * ORB, nown), BF),
            pltpu.VMEM((ORB * ORB, wide_spill), BF),
            pltpu.VMEM((8, width), F32),
            pltpu.VMEM((8, nown), F32),
            pltpu.VMEM((wide_spill, nfeat), BF),
            pltpu.VMEM((8, wide_spill), F32),
        ],
        features,
        *edges,
        near,
        cell_bias,
        w_in,
        w_out,
        token,
        micros=4,
    )
    (band,) = call(
        spill_kernel,
        "spill",
        (band_shape,),
        [
            pltpu.VMEM((ORB * ORB, wide_spill), BF),
            pltpu.VMEM((wide_spill, nfeat), BF),
            pltpu.VMEM((8, wide_spill), F32),
        ],
        band,
        blue_msg,
        *weights,
        alias={0: 0},
        micros=0,
    )

    wide = pltpu.VMEM((2 * HALO, VEC), F32)
    fields = [t0]
    for step in range(1, STEPS):
        if step > 1:
            blue, red = swap(to_blue, to_red)
        inner, name = (start_kernel, "start") if step == 1 else (inner_kernel, "inner")
        (inner,) = call(inner, name, (full,), [], band, *fields[-2:])
        following, to_blue, to_red = call(
            functools.partial(outer_kernel, 1.0 if step == 1 else 2.0),
            "outer",
            (full, part, part),
            [wide],
            band,
            inner,
            blue,
            red,
        )
        fields.append(following)
    blue, red = swap(to_blue, to_red)
    base, final = call(
        mix_kernel,
        "mix",
        (shape((VEC, nrow), F32), shape((8, VEC), F32)),
        [],
        cheb_coef,
        band,
        *fields,
        smem=(0,),
    )
    pieces = call(
        last_kernel,
        "last",
        (piece,) * 4,
        [wide, pltpu.VMEM((VEC, nrow), F32)],
        final,
        band,
        base,
        blue,
        red,
    )
    pieces = exchange(pieces)
    pieces[3:] = call(pass_kernel, "pass", (piece,), [], pieces[3], micros=1)
    (result,) = call(join_kernel, "join", (shape((high, ncol), F32),), [], *pieces)
    return result


def solution(mesh):
    placed = (
        P(("rows", "edges"), None),
        P(("rows", "edges")),
        P(("rows", "edges")),
        P(("rows", "edges")),
        P(),
        P(),
        P(),
        P("edges", "rows"),
        P(),
    )
    return jax.shard_map(
        per_device, mesh=mesh, in_specs=placed, out_specs=P("edges", "rows"), check_vma=False
    )
```

```python
import functools

import jax
import jax.numpy as jnp
from jax import lax
from jax.experimental import pallas as pl
from jax.experimental.pallas import tpu as pltpu
from jax.sharding import PartitionSpec as P

ORB = 16
TILE_ATOMS = 8
BAND = 3
HID = 256
VEC = 128
STEPS = 4
ATOM_Q = 32
SPILL = 320
ID_ROWS = 16
PAIR_ATOMS = 2 * TILE_ATOMS
WIN_ATOMS = (2 * BAND + 2) * TILE_ATOMS
HALO = BAND * TILE_ATOMS * ORB
GROUP = 4
GROUP_SPAN = 384
HALF = ATOM_Q * ORB
NEAR = 3
BF = jnp.bfloat16
F32 = jnp.float32
NT = (((1,), (1,)), ((), ()))


def nt_dot(a, b):
    return lax.dot_general(a, b, NT, preferred_element_type=F32)


def iota(shape, dim):
    return lax.broadcasted_iota(jnp.int32, shape, dim)


def device_side():
    return (lax.axis_index("rows") * lax.axis_size("edges") + lax.axis_index("edges")) % 2


def edge_ids(src, dst, cell):
    ndev = lax.axis_size("rows") * lax.axis_size("edges")
    quarter = lax.axis_index("rows") * lax.axis_size("edges") + lax.axis_index("edges")
    natom = ATOM_Q * ndev
    ntiles = natom // TILE_ATOMS
    rel = src - quarter * ATOM_Q
    rel = jnp.where(rel > natom // 2, rel - natom, jnp.where(rel < -(natom // 2), rel + natom, rel))
    shift = (dst >> 3) - (src >> 3) + BAND
    shift = jnp.where(shift < 0, shift + ntiles, jnp.where(shift >= ntiles, shift - ntiles, shift))
    return [x.astype(F32) for x in (rel, shift * TILE_ATOMS + (dst & 7), cell)]


def tick_kernel(token):
    token[...] = jnp.zeros(token.shape, F32)


def split_kernel(vectors, _, src, dst, cell, p0, p1, p2, p3):
    member = lax.axis_index("edges")
    for k, piece in enumerate((p0, p1, p2, p3)):
        width = piece.shape[1]
        at = pl.multiple_of((member ^ k) * width, width)
        piece[...] = vectors[:, pl.ds(at, width)].astype(BF)


def message_kernel(feat, src, dst, cell, p1, blue, red):
    side = device_side()
    high_rows, width = p1.shape
    nfeat = feat.shape[1]
    high = feat.shape[0] - SPILL
    off = pl.multiple_of(side * high, 64)
    blue[0:SPILL, :] = feat[pl.ds(off, SPILL), :]
    red[0:SPILL, :] = feat[pl.ds(pl.multiple_of(high - off, 64), SPILL), :]
    three = edge_ids(src[...], dst[...], cell[...])
    lane, line = iota((3, 128), 1), iota((3, 128), 0)
    nrow = src.shape[0]
    starts = [x[0:3] for x in three]
    ends = [x[nrow - 3 : nrow] for x in three]
    starts[0] = jnp.where((line == 2) & (lane >= 64), -64.0, starts[0] + ATOM_Q)
    ends[0] = jnp.where((line == 0) & (lane < 64), -64.0, ends[0] - ATOM_Q)
    pad = jnp.zeros((ID_ROWS - 9, 128), F32)
    low_ids = jnp.concatenate(starts + [pad], axis=0)
    high_ids = jnp.concatenate(ends + [pad], axis=0)
    none = jnp.zeros((ID_ROWS, 128), BF)
    for msg, ids_of in (
        (blue, jnp.where(side == 0, low_ids, high_ids)),
        (red, jnp.where(side == 0, high_ids, low_ids)),
    ):
        msg[SPILL : SPILL + ID_ROWS, 0:128] = ids_of.astype(BF)
        msg[SPILL : SPILL + ID_ROWS, 128:256] = none
    for n in range(width // nfeat):
        at = SPILL + ID_ROWS + n * high_rows
        red[at : at + high_rows, :] = p1[:, n * nfeat : (n + 1) * nfeat]


def pass_kernel(x, y):
    y[...] = x[...]


def field_kernel(p0, near, p2, p3, t0, to_blue, to_red, token, field):
    member = lax.axis_index("edges")
    high = p0.shape[0]
    for k, piece in ((0, p0), (2, p2), (3, p3)):
        field[pl.ds(pl.multiple_of((member ^ k) * high, high), high), :] = piece[...].astype(F32)
    rows = pl.ds(pl.multiple_of((member ^ 1) * high, high), high)
    width = near.shape[1]
    for n in range(field.shape[1] // width):
        at = SPILL + ID_ROWS + n * high
        field[rows, n * width : (n + 1) * width] = near[at : at + high, :].astype(F32)
    t0[...] = field[...].T
    token[...] = jnp.zeros(token.shape, F32)
    put_sends(t0, to_blue, to_red)


def pair_blocks(x, cell, w_in_t, bias_t, w_out_t):
    bias = [bias_t[:, k : k + 1].astype(F32) for k in range(3)]
    pre = nt_dot(w_in_t[...], x)
    pre = pre + jnp.where(cell == 1.0, bias[1], jnp.where(cell == 2.0, bias[2], bias[0]))
    gate, up = pre[:HID], pre[HID:]
    hidden = (gate * (0.5 + 0.5 * jnp.tanh(0.5 * gate)) * up).astype(BF)
    return jnp.dot(w_out_t[...], hidden, preferred_element_type=F32).astype(BF)


def row_of(x):
    return jnp.concatenate([x[k : k + 1] for k in range(x.shape[0])], axis=1)


def dense_of(blocks, atom, target, first):
    span = atom.shape[1]
    column = (iota((WIN_ATOMS, span), 0).astype(F32) == target).astype(BF)
    onehot = [
        jnp.broadcast_to((atom == as_float(first + s)).astype(F32), (WIN_ATOMS, span)).astype(BF) * column
        for s in range(GROUP)
    ]
    return nt_dot(blocks, jnp.concatenate(onehot, axis=0))


def put_dense(band, dense, first, base=None):
    lane = iota((ORB, 128), 1)
    low, even = lane < 64, lane % 64 < ATOM_Q
    for sp in range(GROUP // 2):
        s = first + 2 * sp
        pair, at_row = s // PAIR_ATOMS, s % PAIR_ATOMS * ORB
        if not isinstance(s, int):
            at_row = pl.multiple_of(at_row, 2 * ORB)
        for m in range(ORB // 4):
            x = [
                dense[(4 * m + i) * ORB : (4 * m + i + 1) * ORB, sp * 128 : sp * 128 + 128].astype(BF)
                for i in range(4)
            ]
            for half in range(2):
                if half == 0:
                    u = [jnp.where(low, x[i], pltpu.roll(x[i + 2], 64, 1)) for i in range(2)]
                else:
                    u = [jnp.where(low, pltpu.roll(x[i], 64, 1), x[i + 2]) for i in range(2)]
                both = (
                    jnp.where(even, u[0], pltpu.roll(u[1], ATOM_Q, 1)),
                    jnp.where(even, pltpu.roll(u[0], 128 - ATOM_Q, 1), u[1]),
                )
                rows = pl.ds(at_row + half * ORB, ORB)
                for n, value in enumerate(both):
                    lo = n * HALF + m * 128
                    if base is not None:
                        value = value + base[pair, rows, lo : lo + 128]
                    band[pair, rows, lo : lo + 128] = value


def column_of(atom, offset):
    target = TILE_ATOMS * (jnp.floor(atom * (1.0 / TILE_ATOMS)) - BAND) + offset
    base = BAND * TILE_ATOMS - PAIR_ATOMS * jnp.floor(atom * (1.0 / PAIR_ATOMS))
    outside = jnp.where(target < 0.0, target + (base + ATOM_Q), target + base)
    return jnp.where((target >= 0.0) & (target < float(ATOM_Q)), target, outside)


def as_float(x):
    return float(x) if isinstance(x, int) else x.astype(F32)


def place(message, is_left, rows, lists):
    nfeat = rows.shape[1]
    gap = rows.shape[0] - SPILL
    rows[0:gap, :] = jnp.zeros((gap, nfeat), BF)
    rows[SPILL : SPILL + gap, :] = jnp.zeros((gap, nfeat), BF)
    rows[pl.ds(pl.multiple_of(jnp.where(is_left, gap, 0), 64), SPILL), :] = message[0:SPILL, :]
    block = message[SPILL : SPILL + ID_ROWS, 0:128].astype(F32)
    atom, offset, cell = [row_of(block[3 * k : 3 * k + 3]) for k in range(3)]
    lists[0:1, :] = atom
    lists[1:2, :] = column_of(atom, offset)
    middle = (atom >= float(NEAR * GROUP)) & (atom < float(ATOM_Q - NEAR * GROUP))
    return cell, jnp.max(jnp.where(middle, 1.0, 0.0)) > 0.5


def at_ends(g):
    return g < NEAR or g >= ATOM_Q // GROUP - NEAR


def add_middle(band, blocks, lists, any_middle):
    @pl.when(any_middle)
    def _():
        for g in range(ATOM_Q // GROUP):
            if not at_ends(g):
                dense = dense_of(blocks[...], lists[0:1, :], lists[1:2, :], g * GROUP)
                put_dense(band, dense, g * GROUP, band)


def own_kernel(
    feat, src, dst, cell, near, cell_bias, w_in, w_out, _, band, w_in_t, bias_t, w_out_t, blk, blk2, bias8, rows, more, lists
):
    nblk = w_out.shape[1]
    w_in_t[...] = w_in[...].astype(F32).T.astype(BF)
    bias8[...] = jnp.zeros(bias8.shape, F32)
    bias8[0:3, :] = cell_bias[...].astype(F32)
    bias_t[...] = bias8[...].T.astype(BF)
    row, col = iota((nblk, nblk), 0), iota((nblk, nblk), 1)
    swap = (col == (row % ORB) * ORB + row // ORB).astype(BF)
    w_out_t[...] = nt_dot(swap, w_out[...]).astype(BF)
    own = feat.shape[0]
    ids = edge_ids(src[...], dst[...], cell[...])
    atom = row_of(ids[0])
    rows[0:1, :] = atom
    rows[1:2, :] = column_of(atom, row_of(ids[1]))
    is_left = device_side() == 1
    cells, any_middle = place(near, is_left, more, lists)
    blk[...] = pair_blocks(feat[...], row_of(ids[2]), w_in_t, bias_t, w_out_t)
    blk2[...] = pair_blocks(more[...], cells, w_in_t, bias_t, w_out_t)
    spans = []
    for first in range(0, ATOM_Q, GROUP):
        start = jnp.sum((ids[0] < float(first)).astype(F32)).astype(jnp.int32)
        spans.append(pl.ds(pl.multiple_of(jnp.minimum(start // 128 * 128, own - GROUP_SPAN), 128), GROUP_SPAN))
    for g, span in enumerate(spans):
        first = g * GROUP
        dense = dense_of(blk[:, span], rows[0:1, span], rows[1:2, span], first)
        if at_ends(g):
            dense = dense + dense_of(blk2[...], lists[0:1, :], lists[1:2, :], first)
        put_dense(band, dense, first)
    add_middle(band, blk2, lists, any_middle)


def spill_kernel(own_band, blue, w_in_t, bias_t, w_out_t, band, blk, more, lists):
    is_left = device_side() == 0
    cells, any_middle = place(blue, is_left, more, lists)
    blk[...] = pair_blocks(more[...], cells, w_in_t, bias_t, w_out_t)
    for g in range(ATOM_Q // GROUP):
        first = g * GROUP
        if at_ends(g):
            dense = dense_of(blk[...], lists[0:1, :], lists[1:2, :], first)
            put_dense(band, dense, first, own_band)
        else:
            pair, at = first // PAIR_ATOMS, first % PAIR_ATOMS * ORB
            band[pair, at : at + GROUP * ORB, :] = own_band[pair, at : at + GROUP * ORB, :]
    add_middle(band, blk, lists, any_middle)


def own_part(band, field):
    pieces = [field[pl.ds(q, ATOM_Q, stride=ORB), :].astype(BF) for q in range(ORB)]
    rhs = jnp.concatenate(pieces, axis=0)
    return [jnp.dot(band[k, :, :HALF], rhs, preferred_element_type=F32) for k in range(band.shape[0])]


def halo_part(band, blue, red, wide):
    off = pl.multiple_of(device_side() * HALO, HALO)
    wide[pl.ds(off, HALO), :] = blue[...].astype(F32)
    wide[pl.ds(pl.multiple_of(HALO - off, HALO), HALO), :] = red[...].astype(F32)
    atoms = BAND * TILE_ATOMS
    pieces = [[], []]
    for q in range(ORB):
        left = wide[pl.ds(q, atoms, stride=ORB), :]
        right = wide[pl.ds(HALO + q, atoms, stride=ORB), :]
        pieces[0].append(jnp.concatenate([left, right[:TILE_ATOMS]], axis=0).astype(BF))
        pieces[1].append(jnp.concatenate([left[atoms - TILE_ATOMS :], right], axis=0).astype(BF))
    return [
        jnp.dot(band[k, :, HALF:], jnp.concatenate(pieces[k], axis=0), preferred_element_type=F32)
        for k in range(band.shape[0])
    ]


def put_sends(value_ref, to_blue, to_red):
    side = device_side()
    inner = value_ref.shape[0] - HALO
    off = pl.multiple_of(side * inner, 128)
    to_blue[...] = value_ref[pl.ds(off, HALO), :].astype(BF)
    to_red[...] = value_ref[pl.ds(pl.multiple_of(inner - off, 128), HALO), :].astype(BF)


def spans_of(band):
    height = band.shape[1]
    return [slice(k * height, (k + 1) * height) for k in range(band.shape[0])]


def start_kernel(band, now, part):
    inner = own_part(band, now)
    for k, span in enumerate(spans_of(band)):
        part[span, :] = inner[k]


def inner_kernel(band, before, now, part):
    inner = own_part(band, now)
    for k, span in enumerate(spans_of(band)):
        part[span, :] = 2.0 * inner[k] - before[span, :]


def outer_kernel(scale, band, part, blue, red, after, to_blue, to_red, wide):
    outer = halo_part(band, blue, red, wide)
    for k, span in enumerate(spans_of(band)):
        after[span, :] = scale * outer[k] + part[span, :]
    put_sends(after, to_blue, to_red)


def mix_kernel(coef, band, t0, t1, t2, t3, base, final):
    inner = own_part(band, t3)
    for k, span in enumerate(spans_of(band)):
        total = coef[0] * t0[span, :] + coef[1] * t1[span, :] + (coef[2] - coef[4]) * t2[span, :]
        total = total + coef[3] * t3[span, :] + 2.0 * coef[4] * inner[k]
        base[:, span] = total.T
    final[...] = jnp.full(final.shape, 2.0 * coef[4], F32)


def last_kernel(final, band, base, blue, red, p0, p1, p2, p3, wide, out):
    member = lax.axis_index("edges")
    outer = halo_part(band, blue, red, wide)
    for k, span in enumerate(spans_of(band)):
        out[:, span] = base[:, span] + (final[0:1, :] * outer[k]).T
    for k, piece in enumerate((p0, p1, p2, p3)):
        high = piece.shape[0]
        piece[...] = out[pl.ds(pl.multiple_of((member ^ k) * high, high), high), :].astype(BF)


def join_kernel(p0, p1, p2, p3, out):
    member = lax.axis_index("edges")
    for k, piece in enumerate((p0, p1, p2, p3)):
        width = piece.shape[1]
        at = pl.multiple_of((member ^ k) * width, width)
        out[:, pl.ds(at, width)] = piece[...].astype(F32)


VMEM = pl.BlockSpec(memory_space=pltpu.VMEM)
SMEM = pl.BlockSpec(memory_space=pltpu.SMEM)
IN_HBM = pl.BlockSpec(memory_space=pltpu.HBM)
FULL, PART = 60 * 1024 * 1024, 32 * 1024 * 1024


def shape(dims, dtype):
    return jax.ShapeDtypeStruct(dims, dtype)


def call(kernel, name, outs, scratch, *args, smem=(), in_hbm=(), out_hbm=(), alias=None, limit=PART, micros=1):
    spaces = [SMEM if k in smem else IN_HBM if k in in_hbm else VMEM for k in range(len(args))]
    return pl.pallas_call(
        kernel,
        name=name,
        out_shape=outs,
        in_specs=spaces,
        out_specs=tuple(IN_HBM if k in out_hbm else VMEM for k in range(len(outs))),
        scratch_shapes=scratch,
        input_output_aliases=alias or {},
        cost_estimate=pl.CostEstimate(flops=micros * 10**9, bytes_accessed=0, transcendentals=0),
        compiler_params=pltpu.CompilerParams(vmem_limit_bytes=limit),
    )(*args)


def per_device(features, edge_src, edge_dst, edge_cell, cell_bias, w_in, w_out, vectors, cheb_coef):
    axes = ("rows", "edges")
    nedge = lax.axis_size("edges")
    ndev = lax.axis_size("rows") * nedge
    red_pairs = [(i, i ^ 1) for i in range(ndev)]
    blue_pairs = [(i, (i + 1) % ndev if i % 2 else (i - 1) % ndev) for i in range(ndev)]
    nown, nfeat = features.shape
    high, ncol = vectors.shape
    nrow = ncol // nedge

    def swap(first, last):
        return (
            lax.ppermute(first, axes, blue_pairs),
            lax.ppermute(last, axes, red_pairs),
        )

    def exchange(pieces):
        return [pieces[0]] + [
            lax.ppermute(pieces[k], "edges", [(i, i ^ k) for i in range(nedge)]) for k in (3, 2, 1)
        ][::-1]

    msg = shape((SPILL + ID_ROWS, nfeat), BF)
    piece = shape((high, nrow), BF)
    lines = (nown // 128, 128)
    edges = [x.reshape(lines) for x in (edge_src, edge_dst, edge_cell)]
    near_msg = shape((SPILL + ID_ROWS + high * nrow // nfeat, nfeat), BF)
    (tick,) = call(tick_kernel, "tick", (shape((8, VEC), F32),), [], micros=5)
    own_piece, beside, straight, across = call(
        split_kernel, "split", (piece,) * 4, [], vectors, tick, *edges, micros=0
    )
    blue_msg, near = call(
        message_kernel, "message", (msg, near_msg), [], features, *edges, beside, micros=0
    )
    across = lax.ppermute(across, "edges", [(i, i ^ 3) for i in range(nedge)])
    straight = lax.ppermute(straight, "edges", [(i, i ^ 2) for i in range(nedge)])
    near = lax.ppermute(near, axes, red_pairs)
    blue_msg = lax.ppermute(blue_msg, axes, blue_pairs)
    (straight,) = call(pass_kernel, "pass", (piece,), [], straight, micros=0)
    pieces = [own_piece, near, straight, across]
    full, part = shape((nrow, VEC), F32), shape((HALO, VEC), BF)
    t0, to_blue, to_red, token = call(
        field_kernel, "field", (full, part, part, shape((8, VEC), F32)), [pltpu.VMEM((VEC, nrow), F32)], *pieces
    )
    blue, red = swap(to_blue, to_red)

    wide_spill = SPILL + 64
    band_shape = shape((ATOM_Q // PAIR_ATOMS, PAIR_ATOMS * ORB, WIN_ATOMS * ORB), BF)
    width = w_in.shape[1]
    band, *weights = call(
        own_kernel,
        "own",
        (band_shape, shape((width, nfeat), BF), shape((width, 8), BF), shape((ORB * ORB, HID), BF)),
        [
            pltpu.VMEM((ORB * ORB, nown), BF),
            pltpu.VMEM((ORB * ORB, wide_spill), BF),
            pltpu.VMEM((8, width), F32),
            pltpu.VMEM((8, nown), F32),
            pltpu.VMEM((wide_spill, nfeat), BF),
            pltpu.VMEM((8, wide_spill), F32),
        ],
        features,
        *edges,
        near,
        cell_bias,
        w_in,
        w_out,
        token,
        micros=4,
    )
    (band,) = call(
        spill_kernel,
        "spill",
        (band_shape,),
        [
            pltpu.VMEM((ORB * ORB, wide_spill), BF),
            pltpu.VMEM((wide_spill, nfeat), BF),
            pltpu.VMEM((8, wide_spill), F32),
        ],
        band,
        blue_msg,
        *weights,
        alias={0: 0},
        micros=0,
    )

    wide = pltpu.VMEM((2 * HALO, VEC), F32)
    fields = [t0]
    for step in range(1, STEPS):
        if step > 1:
            blue, red = swap(to_blue, to_red)
        inner, name = (start_kernel, "start") if step == 1 else (inner_kernel, "inner")
        (inner,) = call(inner, name, (full,), [], band, *fields[-2:])
        following, to_blue, to_red = call(
            functools.partial(outer_kernel, 1.0 if step == 1 else 2.0),
            "outer",
            (full, part, part),
            [wide],
            band,
            inner,
            blue,
            red,
        )
        fields.append(following)
    blue, red = swap(to_blue, to_red)
    base, final = call(
        mix_kernel,
        "mix",
        (shape((VEC, nrow), F32), shape((8, VEC), F32)),
        [],
        cheb_coef,
        band,
        *fields,
        smem=(0,),
    )
    pieces = call(
        last_kernel,
        "last",
        (piece,) * 4,
        [wide, pltpu.VMEM((VEC, nrow), F32)],
        final,
        band,
        base,
        blue,
        red,
    )
    pieces = exchange(pieces)
    pieces[3:] = call(pass_kernel, "pass", (piece,), [], pieces[3], micros=1)
    (result,) = call(join_kernel, "join", (shape((high, ncol), F32),), [], *pieces)
    return result


def solution(mesh):
    placed = (
        P(("rows", "edges"), None),
        P(("rows", "edges")),
        P(("rows", "edges")),
        P(("rows", "edges")),
        P(),
        P(),
        P(),
        P("edges", "rows"),
        P(),
    )
    return jax.shard_map(
        per_device, mesh=mesh, in_specs=placed, out_specs=P("edges", "rows"), check_vma=False
    )
```

```python
import functools

import jax
import jax.numpy as jnp
from jax import lax
from jax.experimental import pallas as pl
from jax.experimental.pallas import tpu as pltpu
from jax.sharding import PartitionSpec as P

ORB = 16
TILE_ATOMS = 8
BAND = 3
HID = 256
VEC = 128
STEPS = 4
ATOM_Q = 32
SPILL = 320
ID_ROWS = 16
PAIR_ATOMS = 2 * TILE_ATOMS
WIN_ATOMS = (2 * BAND + 2) * TILE_ATOMS
HALO = BAND * TILE_ATOMS * ORB
GROUP = 4
GROUP_SPAN = 384
HALF = ATOM_Q * ORB
NEAR = 3
BF = jnp.bfloat16
F32 = jnp.float32
NT = (((1,), (1,)), ((), ()))


def nt_dot(a, b):
    return lax.dot_general(a, b, NT, preferred_element_type=F32)


def iota(shape, dim):
    return lax.broadcasted_iota(jnp.int32, shape, dim)


def device_side():
    return (lax.axis_index("rows") * lax.axis_size("edges") + lax.axis_index("edges")) % 2


def edge_ids(src, dst, cell):
    ndev = lax.axis_size("rows") * lax.axis_size("edges")
    quarter = lax.axis_index("rows") * lax.axis_size("edges") + lax.axis_index("edges")
    natom = ATOM_Q * ndev
    ntiles = natom // TILE_ATOMS
    rel = src - quarter * ATOM_Q
    rel = jnp.where(rel > natom // 2, rel - natom, jnp.where(rel < -(natom // 2), rel + natom, rel))
    shift = (dst >> 3) - (src >> 3) + BAND
    shift = jnp.where(shift < 0, shift + ntiles, jnp.where(shift >= ntiles, shift - ntiles, shift))
    return [x.astype(F32) for x in (rel, shift * TILE_ATOMS + (dst & 7), cell)]


def tick_kernel(token):
    token[...] = jnp.zeros(token.shape, F32)


def split_kernel(vectors, _, src, dst, cell, p0, p1, p2, p3):
    member = lax.axis_index("edges")
    for k, piece in enumerate((p0, p1, p2, p3)):
        width = piece.shape[1]
        at = pl.multiple_of((member ^ k) * width, width)
        piece[...] = vectors[:, pl.ds(at, width)].astype(BF)


def message_kernel(feat, src, dst, cell, p1, blue, red):
    side = device_side()
    high_rows, width = p1.shape
    nfeat = feat.shape[1]
    high = feat.shape[0] - SPILL
    off = pl.multiple_of(side * high, 64)
    blue[0:SPILL, :] = feat[pl.ds(off, SPILL), :]
    red[0:SPILL, :] = feat[pl.ds(pl.multiple_of(high - off, 64), SPILL), :]
    three = edge_ids(src[...], dst[...], cell[...])
    lane, line = iota((3, 128), 1), iota((3, 128), 0)
    nrow = src.shape[0]
    starts = [x[0:3] for x in three]
    ends = [x[nrow - 3 : nrow] for x in three]
    starts[0] = jnp.where((line == 2) & (lane >= 64), -64.0, starts[0] + ATOM_Q)
    ends[0] = jnp.where((line == 0) & (lane < 64), -64.0, ends[0] - ATOM_Q)
    pad = jnp.zeros((ID_ROWS - 9, 128), F32)
    low_ids = jnp.concatenate(starts + [pad], axis=0)
    high_ids = jnp.concatenate(ends + [pad], axis=0)
    none = jnp.zeros((ID_ROWS, 128), BF)
    for msg, ids_of in (
        (blue, jnp.where(side == 0, low_ids, high_ids)),
        (red, jnp.where(side == 0, high_ids, low_ids)),
    ):
        msg[SPILL : SPILL + ID_ROWS, 0:128] = ids_of.astype(BF)
        msg[SPILL : SPILL + ID_ROWS, 128:256] = none
    for n in range(width // nfeat):
        at = SPILL + ID_ROWS + n * high_rows
        red[at : at + high_rows, :] = p1[:, n * nfeat : (n + 1) * nfeat]


def pass_kernel(x, y):
    y[...] = x[...]


def field_kernel(p0, near, p2, p3, t0, to_blue, to_red, token, field):
    member = lax.axis_index("edges")
    high = p0.shape[0]
    for k, piece in ((0, p0), (2, p2), (3, p3)):
        field[pl.ds(pl.multiple_of((member ^ k) * high, high), high), :] = piece[...].astype(F32)
    rows = pl.ds(pl.multiple_of((member ^ 1) * high, high), high)
    width = near.shape[1]
    for n in range(field.shape[1] // width):
        at = SPILL + ID_ROWS + n * high
        field[rows, n * width : (n + 1) * width] = near[at : at + high, :].astype(F32)
    t0[...] = field[...].T
    token[...] = jnp.zeros(token.shape, F32)
    put_sends(t0, to_blue, to_red)


def pair_blocks(x, cell, w_in_t, bias_t, w_out_t):
    bias = [bias_t[:, k : k + 1].astype(F32) for k in range(3)]
    pre = nt_dot(w_in_t[...], x)
    pre = pre + jnp.where(cell == 1.0, bias[1], jnp.where(cell == 2.0, bias[2], bias[0]))
    gate, up = pre[:HID], pre[HID:]
    hidden = (gate * (0.5 + 0.5 * jnp.tanh(0.5 * gate)) * up).astype(BF)
    return jnp.dot(w_out_t[...], hidden, preferred_element_type=F32).astype(BF)


def row_of(x):
    return jnp.concatenate([x[k : k + 1] for k in range(x.shape[0])], axis=1)


def dense_of(blocks, atom, target, first):
    span = atom.shape[1]
    column = (iota((WIN_ATOMS, span), 0).astype(F32) == target).astype(BF)
    onehot = [
        jnp.broadcast_to((atom == as_float(first + s)).astype(F32), (WIN_ATOMS, span)).astype(BF) * column
        for s in range(GROUP)
    ]
    return nt_dot(blocks, jnp.concatenate(onehot, axis=0))


def put_dense(band, dense, first, base=None):
    lane = iota((ORB, 128), 1)
    low, even = lane < 64, lane % 64 < ATOM_Q
    for sp in range(GROUP // 2):
        s = first + 2 * sp
        pair, at_row = s // PAIR_ATOMS, s % PAIR_ATOMS * ORB
        if not isinstance(s, int):
            at_row = pl.multiple_of(at_row, 2 * ORB)
        for m in range(ORB // 4):
            x = [
                dense[(4 * m + i) * ORB : (4 * m + i + 1) * ORB, sp * 128 : sp * 128 + 128].astype(BF)
                for i in range(4)
            ]
            for half in range(2):
                if half == 0:
                    u = [jnp.where(low, x[i], pltpu.roll(x[i + 2], 64, 1)) for i in range(2)]
                else:
                    u = [jnp.where(low, pltpu.roll(x[i], 64, 1), x[i + 2]) for i in range(2)]
                both = (
                    jnp.where(even, u[0], pltpu.roll(u[1], ATOM_Q, 1)),
                    jnp.where(even, pltpu.roll(u[0], 128 - ATOM_Q, 1), u[1]),
                )
                rows = pl.ds(at_row + half * ORB, ORB)
                for n, value in enumerate(both):
                    lo = n * HALF + m * 128
                    if base is not None:
                        value = value + base[pair, rows, lo : lo + 128]
                    band[pair, rows, lo : lo + 128] = value


def column_of(atom, offset):
    target = TILE_ATOMS * (jnp.floor(atom * (1.0 / TILE_ATOMS)) - BAND) + offset
    base = BAND * TILE_ATOMS - PAIR_ATOMS * jnp.floor(atom * (1.0 / PAIR_ATOMS))
    outside = jnp.where(target < 0.0, target + (base + ATOM_Q), target + base)
    return jnp.where((target >= 0.0) & (target < float(ATOM_Q)), target, outside)


def as_float(x):
    return float(x) if isinstance(x, int) else x.astype(F32)


def place(message, is_left, rows, lists):
    nfeat = rows.shape[1]
    gap = rows.shape[0] - SPILL
    rows[0:gap, :] = jnp.zeros((gap, nfeat), BF)
    rows[SPILL : SPILL + gap, :] = jnp.zeros((gap, nfeat), BF)
    rows[pl.ds(pl.multiple_of(jnp.where(is_left, gap, 0), 64), SPILL), :] = message[0:SPILL, :]
    block = message[SPILL : SPILL + ID_ROWS, 0:128].astype(F32)
    atom, offset, cell = [row_of(block[3 * k : 3 * k + 3]) for k in range(3)]
    lists[0:1, :] = atom
    lists[1:2, :] = column_of(atom, offset)
    middle = (atom >= float(NEAR * GROUP)) & (atom < float(ATOM_Q - NEAR * GROUP))
    return cell, jnp.max(jnp.where(middle, 1.0, 0.0)) > 0.5


def at_ends(g):
    return g < NEAR or g >= ATOM_Q // GROUP - NEAR


def add_middle(band, blocks, lists, any_middle):
    @pl.when(any_middle)
    def _():
        for g in range(ATOM_Q // GROUP):
            if not at_ends(g):
                dense = dense_of(blocks[...], lists[0:1, :], lists[1:2, :], g * GROUP)
                put_dense(band, dense, g * GROUP, band)


def own_kernel(
    feat, src, dst, cell, near, cell_bias, w_in, w_out, _, band, w_in_t, bias_t, w_out_t, blk, blk2, bias8, rows, more, lists
):
    nblk = w_out.shape[1]
    w_in_t[...] = w_in[...].astype(F32).T.astype(BF)
    bias8[...] = jnp.zeros(bias8.shape, F32)
    bias8[0:3, :] = cell_bias[...].astype(F32)
    bias_t[...] = bias8[...].T.astype(BF)
    row, col = iota((nblk, nblk), 0), iota((nblk, nblk), 1)
    swap = (col == (row % ORB) * ORB + row // ORB).astype(BF)
    w_out_t[...] = nt_dot(swap, w_out[...]).astype(BF)
    own = feat.shape[0]
    ids = edge_ids(src[...], dst[...], cell[...])
    atom = row_of(ids[0])
    rows[0:1, :] = atom
    rows[1:2, :] = column_of(atom, row_of(ids[1]))
    is_left = device_side() == 1
    cells, any_middle = place(near, is_left, more, lists)
    blk[...] = pair_blocks(feat[...], row_of(ids[2]), w_in_t, bias_t, w_out_t)
    blk2[...] = pair_blocks(more[...], cells, w_in_t, bias_t, w_out_t)
    spans = []
    for first in range(0, ATOM_Q, GROUP):
        start = jnp.sum((ids[0] < float(first)).astype(F32)).astype(jnp.int32)
        spans.append(pl.ds(pl.multiple_of(jnp.minimum(start // 128 * 128, own - GROUP_SPAN), 128), GROUP_SPAN))
    for g, span in enumerate(spans):
        first = g * GROUP
        dense = dense_of(blk[:, span], rows[0:1, span], rows[1:2, span], first)
        if at_ends(g):
            dense = dense + dense_of(blk2[...], lists[0:1, :], lists[1:2, :], first)
        put_dense(band, dense, first)
    add_middle(band, blk2, lists, any_middle)


def spill_kernel(own_band, blue, w_in_t, bias_t, w_out_t, band, blk, more, lists):
    is_left = device_side() == 0
    cells, any_middle = place(blue, is_left, more, lists)
    blk[...] = pair_blocks(more[...], cells, w_in_t, bias_t, w_out_t)
    for g in range(ATOM_Q // GROUP):
        first = g * GROUP
        if at_ends(g):
            dense = dense_of(blk[...], lists[0:1, :], lists[1:2, :], first)
            put_dense(band, dense, first, own_band)
        else:
            pair, at = first // PAIR_ATOMS, first % PAIR_ATOMS * ORB
            band[pair, at : at + GROUP * ORB, :] = own_band[pair, at : at + GROUP * ORB, :]
    add_middle(band, blk, lists, any_middle)


def own_part(band, field):
    pieces = [field[pl.ds(q, ATOM_Q, stride=ORB), :].astype(BF) for q in range(ORB)]
    rhs = jnp.concatenate(pieces, axis=0)
    return [jnp.dot(band[k, :, :HALF], rhs, preferred_element_type=F32) for k in range(band.shape[0])]


def halo_part(band, blue, red, wide):
    off = pl.multiple_of(device_side() * HALO, HALO)
    wide[pl.ds(off, HALO), :] = blue[...].astype(F32)
    wide[pl.ds(pl.multiple_of(HALO - off, HALO), HALO), :] = red[...].astype(F32)
    atoms = BAND * TILE_ATOMS
    pieces = [[], []]
    for q in range(ORB):
        left = wide[pl.ds(q, atoms, stride=ORB), :]
        right = wide[pl.ds(HALO + q, atoms, stride=ORB), :]
        pieces[0].append(jnp.concatenate([left, right[:TILE_ATOMS]], axis=0).astype(BF))
        pieces[1].append(jnp.concatenate([left[atoms - TILE_ATOMS :], right], axis=0).astype(BF))
    return [
        jnp.dot(band[k, :, HALF:], jnp.concatenate(pieces[k], axis=0), preferred_element_type=F32)
        for k in range(band.shape[0])
    ]


def put_sends(value_ref, to_blue, to_red):
    side = device_side()
    inner = value_ref.shape[0] - HALO
    off = pl.multiple_of(side * inner, 128)
    to_blue[...] = value_ref[pl.ds(off, HALO), :].astype(BF)
    to_red[...] = value_ref[pl.ds(pl.multiple_of(inner - off, 128), HALO), :].astype(BF)


def spans_of(band):
    height = band.shape[1]
    return [slice(k * height, (k + 1) * height) for k in range(band.shape[0])]


def start_kernel(band, now, part):
    inner = own_part(band, now)
    for k, span in enumerate(spans_of(band)):
        part[span, :] = inner[k]


def inner_kernel(band, before, now, part):
    inner = own_part(band, now)
    for k, span in enumerate(spans_of(band)):
        part[span, :] = 2.0 * inner[k] - before[span, :]


def outer_kernel(scale, band, part, blue, red, after, to_blue, to_red, wide):
    outer = halo_part(band, blue, red, wide)
    for k, span in enumerate(spans_of(band)):
        after[span, :] = scale * outer[k] + part[span, :]
    put_sends(after, to_blue, to_red)


def mix_kernel(coef, band, t0, t1, t2, t3, base, final):
    inner = own_part(band, t3)
    for k, span in enumerate(spans_of(band)):
        total = coef[0] * t0[span, :] + coef[1] * t1[span, :] + (coef[2] - coef[4]) * t2[span, :]
        total = total + coef[3] * t3[span, :] + 2.0 * coef[4] * inner[k]
        base[:, span] = total.T
    final[...] = jnp.full(final.shape, 2.0 * coef[4], F32)


def last_kernel(final, band, base, blue, red, p0, p1, p2, p3, wide, out):
    member = lax.axis_index("edges")
    outer = halo_part(band, blue, red, wide)
    for k, span in enumerate(spans_of(band)):
        out[:, span] = base[:, span] + (final[0:1, :] * outer[k]).T
    for k, piece in enumerate((p0, p1, p2, p3)):
        high = piece.shape[0]
        piece[...] = out[pl.ds(pl.multiple_of((member ^ k) * high, high), high), :].astype(BF)


def join_kernel(p0, p1, p2, p3, out):
    member = lax.axis_index("edges")
    for k, piece in enumerate((p0, p1, p2, p3)):
        width = piece.shape[1]
        at = pl.multiple_of((member ^ k) * width, width)
        out[:, pl.ds(at, width)] = piece[...].astype(F32)


VMEM = pl.BlockSpec(memory_space=pltpu.VMEM)
SMEM = pl.BlockSpec(memory_space=pltpu.SMEM)
IN_HBM = pl.BlockSpec(memory_space=pltpu.HBM)
FULL, PART = 60 * 1024 * 1024, 32 * 1024 * 1024


def shape(dims, dtype):
    return jax.ShapeDtypeStruct(dims, dtype)


def call(kernel, name, outs, scratch, *args, smem=(), in_hbm=(), out_hbm=(), alias=None, limit=PART, micros=1):
    spaces = [SMEM if k in smem else IN_HBM if k in in_hbm else VMEM for k in range(len(args))]
    return pl.pallas_call(
        kernel,
        name=name,
        out_shape=outs,
        in_specs=spaces,
        out_specs=tuple(IN_HBM if k in out_hbm else VMEM for k in range(len(outs))),
        scratch_shapes=scratch,
        input_output_aliases=alias or {},
        cost_estimate=pl.CostEstimate(flops=micros * 10**9, bytes_accessed=0, transcendentals=0),
        compiler_params=pltpu.CompilerParams(vmem_limit_bytes=limit),
    )(*args)


def per_device(features, edge_src, edge_dst, edge_cell, cell_bias, w_in, w_out, vectors, cheb_coef):
    axes = ("rows", "edges")
    nedge = lax.axis_size("edges")
    ndev = lax.axis_size("rows") * nedge
    red_pairs = [(i, i ^ 1) for i in range(ndev)]
    blue_pairs = [(i, (i + 1) % ndev if i % 2 else (i - 1) % ndev) for i in range(ndev)]
    nown, nfeat = features.shape
    high, ncol = vectors.shape
    nrow = ncol // nedge

    def swap(first, last):
        return (
            lax.ppermute(first, axes, blue_pairs),
            lax.ppermute(last, axes, red_pairs),
        )

    def exchange(pieces):
        return [pieces[0]] + [
            lax.ppermute(pieces[k], "edges", [(i, i ^ k) for i in range(nedge)]) for k in (3, 2, 1)
        ][::-1]

    msg = shape((SPILL + ID_ROWS, nfeat), BF)
    piece = shape((high, nrow), BF)
    lines = (nown // 128, 128)
    edges = [x.reshape(lines) for x in (edge_src, edge_dst, edge_cell)]
    near_msg = shape((SPILL + ID_ROWS + high * nrow // nfeat, nfeat), BF)
    (tick,) = call(tick_kernel, "tick", (shape((8, VEC), F32),), [], micros=5)
    own_piece, beside, straight, across = call(
        split_kernel, "split", (piece,) * 4, [], vectors, tick, *edges, micros=0
    )
    blue_msg, near = call(
        message_kernel, "message", (msg, near_msg), [], features, *edges, beside, micros=0
    )
    across = lax.ppermute(across, "edges", [(i, i ^ 3) for i in range(nedge)])
    straight = lax.ppermute(straight, "edges", [(i, i ^ 2) for i in range(nedge)])
    near = lax.ppermute(near, axes, red_pairs)
    blue_msg = lax.ppermute(blue_msg, axes, blue_pairs)
    (across,) = call(pass_kernel, "pass", (piece,), [], across, micros=0)
    pieces = [own_piece, near, straight, across]
    full, part = shape((nrow, VEC), F32), shape((HALO, VEC), BF)
    t0, to_blue, to_red, token = call(
        field_kernel, "field", (full, part, part, shape((8, VEC), F32)), [pltpu.VMEM((VEC, nrow), F32)], *pieces
    )
    blue, red = swap(to_blue, to_red)

    wide_spill = SPILL + 64
    band_shape = shape((ATOM_Q // PAIR_ATOMS, PAIR_ATOMS * ORB, WIN_ATOMS * ORB), BF)
    width = w_in.shape[1]
    band, *weights = call(
        own_kernel,
        "own",
        (band_shape, shape((width, nfeat), BF), shape((width, 8), BF), shape((ORB * ORB, HID), BF)),
        [
            pltpu.VMEM((ORB * ORB, nown), BF),
            pltpu.VMEM((ORB * ORB, wide_spill), BF),
            pltpu.VMEM((8, width), F32),
            pltpu.VMEM((8, nown), F32),
            pltpu.VMEM((wide_spill, nfeat), BF),
            pltpu.VMEM((8, wide_spill), F32),
        ],
        features,
        *edges,
        near,
        cell_bias,
        w_in,
        w_out,
        token,
        micros=4,
    )
    (band,) = call(
        spill_kernel,
        "spill",
        (band_shape,),
        [
            pltpu.VMEM((ORB * ORB, wide_spill), BF),
            pltpu.VMEM((wide_spill, nfeat), BF),
            pltpu.VMEM((8, wide_spill), F32),
        ],
        band,
        blue_msg,
        *weights,
        alias={0: 0},
        micros=0,
    )

    wide = pltpu.VMEM((2 * HALO, VEC), F32)
    fields = [t0]
    for step in range(1, STEPS):
        if step > 1:
            blue, red = swap(to_blue, to_red)
        inner, name = (start_kernel, "start") if step == 1 else (inner_kernel, "inner")
        (inner,) = call(inner, name, (full,), [], band, *fields[-2:])
        following, to_blue, to_red = call(
            functools.partial(outer_kernel, 1.0 if step == 1 else 2.0),
            "outer",
            (full, part, part),
            [wide],
            band,
            inner,
            blue,
            red,
        )
        fields.append(following)
    blue, red = swap(to_blue, to_red)
    base, final = call(
        mix_kernel,
        "mix",
        (shape((VEC, nrow), F32), shape((8, VEC), F32)),
        [],
        cheb_coef,
        band,
        *fields,
        smem=(0,),
    )
    pieces = call(
        last_kernel,
        "last",
        (piece,) * 4,
        [wide, pltpu.VMEM((VEC, nrow), F32)],
        final,
        band,
        base,
        blue,
        red,
    )
    pieces = exchange(pieces)
    pieces[3:] = call(pass_kernel, "pass", (piece,), [], pieces[3], micros=1)
    pieces[2:3] = call(pass_kernel, "pass", (piece,), [], pieces[2], micros=1)
    (result,) = call(join_kernel, "join", (shape((high, ncol), F32),), [], *pieces)
    return result


def solution(mesh):
    placed = (
        P(("rows", "edges"), None),
        P(("rows", "edges")),
        P(("rows", "edges")),
        P(("rows", "edges")),
        P(),
        P(),
        P(),
        P("edges", "rows"),
        P(),
    )
    return jax.shard_map(
        per_device, mesh=mesh, in_specs=placed, out_specs=P("edges", "rows"), check_vma=False
    )
```
